32 devices in a mesh: section: 4 (over z), latent: 8 (over y, x, core).
Axes of the slice: x: 2, y: 2, z: 4, core: 2. Of those that a mesh axis runs over, the one named last changes fastest.
Arguments:
- residual: bfloat16 [4, 320, 4608], P(None, None, 'latent'), may hold values from -6 to 6
- encoder: bfloat16 [4, 4608, 1024], P('section', None, 'latent'), may hold values from -0.09375 to 0.09375
- enc_bias: float32 [4, 1024], P('section', 'latent'), may hold values from -4 to 4
- gate_code: int32 [4, 1024], P('section', 'latent'), may hold values from 0 to 2
- decoder: bfloat16 [4, 3, 1024, 4608], P('section', None, 'latent'), may hold values from -0.15625 to 0.15625
Outputs:
- reconstruction: bfloat16 [4, 320, 4608], P('section', None, 'latent')
- latent_acts: bfloat16 [4, 320, 1024], P('section', None, 'latent')
The draws below stay inside these ranges and needn't reach their ends.
Inputs may be any that keep to these rules, and one draw needn't show every extreme that they name: `gate_code`: 0: the latent is always active; 1: its threshold is zero; 2: it is never active.
All inputs are finite; a program needn't handle non-finite values.
Results may differ from the reference program's by a relative error of at most 0.019.
Values may be sent and summed in bfloat16 or wider, within the bound.
No kernel may reach another device: no remote copies, remote signals or barrier semaphores. Data moves between devices by JAX's collectives and lax.ppermute only.
A program may use at most 64 MiB of HBM per device.

```python
import jax
import jax.numpy as jnp
from jax import lax

D = 4608
LAYERS = 4
LAT_DEV = 128
REACH = 3
TOK = 320
GROUP = 1
LATG = 1024
LATENTS = 1024
N_SECTION = 4
N_LATENT = 8


def with_ends(drawn, own_key, least, high):
    longest = drawn.shape.index(max(drawn.shape))
    spots = []
    for shift in (0, 1):
        where = [jax.random.randint(jax.random.fold_in(own_key, axis), (), 0, length) for axis, length in enumerate(drawn.shape)]
        where[longest] = (where[longest] + shift) % drawn.shape[longest]
        spots.append(tuple(where))
    return drawn.at[spots[0]].set(least).at[spots[1]].set(high)


def strengthened(array, stream_key, source, target, blocks, factor):
    owner, partner = [(jnp.arange(array.shape[position]) // (array.shape[position] // blocks)).reshape([-1 if axis == position else 1 for axis in range(array.ndim)]) for position in (source, target)]
    chosen = jax.random.permutation(stream_key, blocks)[partner]
    strong = (owner == chosen) | (owner == (partner + blocks // 2) % blocks)
    return jnp.where(strong, factor * array, array)


def level_of(rng, dims, split, low, largest):
    def one(position, blocks):
        heights = jax.random.uniform(jax.random.fold_in(jax.random.fold_in(rng, 6), position), (blocks,), jnp.float32, low / len(split), largest / len(split))
        return jnp.repeat(jnp.exp(heights), dims[position] // blocks).reshape((-1,) + (1,) * (len(dims) - position - 1))

    level = one(*split[0])
    for cut in split[1:]:
        level = level * one(*cut)
    return level


def centred(key, dims, scale, limit, split=(), held_as=jnp.bfloat16):
    values = jax.random.normal(key, dims, jnp.float32) * scale
    if len(split) > 0:
        values = level_of(key, dims, split, -0.22, 0.18) * values
    return jnp.clip(values, min=-limit, max=limit).astype(held_as)


def gaussian_with(rng, dims, scale, reach, shards, heavy, held_as=jnp.bfloat16):
    entries = scale * jax.random.normal(rng, dims, jnp.float32)
    if shards:
        entries = entries * level_of(rng, dims, shards, -0.22, 0.18)
    return jnp.clip(strengthened(entries, jax.random.fold_in(rng, 3), *heavy), -reach, reach).astype(held_as)


def setup_inputs(seed: int = 0) -> dict:
    keys = jax.random.split(jax.random.key(seed), 6)
    residual = centred(keys[0], (LAYERS, TOK, D), 1.0, 6.0, ((2, 8),))
    encoder = centred(keys[1], (N_SECTION, D, LATG), D ** -0.5, 0.09375, ((0, 4), (2, 8)))
    enc_bias = centred(keys[2], (N_SECTION, LATG), 1.0, 4.0, ((0, 4), (1, 8)), jnp.float32)
    gate_code = with_ends(jax.random.randint(keys[3], (N_SECTION, LATG), 0, 3), jax.random.fold_in(keys[3], 1), 0, 2).astype(jnp.int32)
    decoder = gaussian_with(keys[4], (N_SECTION, REACH, LATG, D), (LATENTS * REACH) ** -0.5, 0.15625, ((0, 4), (2, 8)), (2, 3, 8, 2.0))
    return {"residual": residual, "encoder": encoder, "enc_bias": enc_bias, "gate_code": gate_code, "decoder": decoder}


def reference(residual, encoder, enc_bias, gate_code, decoder):
    threshold = 10000.0 * (gate_code.astype(jnp.float32) - 1.0)
    resid_rows = jnp.repeat(residual, GROUP, axis=0)

    def encode(inputs):
        resid_layer, enc_layer, bias_layer, thresh_layer = inputs
        preact = jnp.dot(resid_layer, enc_layer, preferred_element_type=jnp.float32) + bias_layer
        return jnp.where(preact > thresh_layer, preact, jnp.zeros_like(preact)).astype(jnp.bfloat16)

    latent_acts = lax.map(encode, (resid_rows, encoder, enc_bias, threshold))
    slots = LAYERS * GROUP
    shifted = []
    for hop_index in range(REACH):
        lead = hop_index * GROUP
        zero_start = jnp.zeros((lead, TOK, LATG), jnp.bfloat16)
        shifted.append(jnp.concatenate([zero_start, latent_acts[:slots - lead]], axis=0))
    sources = jnp.stack(shifted, axis=1)

    def decode(inputs):
        source_acts, dec_layer = inputs
        spread = source_acts.astype(jnp.float32).reshape(REACH, TOK, N_LATENT, LAT_DEV)
        weights_full = dec_layer.astype(jnp.float32).reshape(REACH, N_LATENT, LAT_DEV, D)
        shares = jnp.einsum("ktjl,kjld->jtd", spread, weights_full, precision=lax.Precision.HIGHEST)
        shares = lax.optimization_barrier(shares.astype(jnp.bfloat16)).astype(jnp.float32)
        return jnp.sum(shares, axis=0)

    parts_all = lax.map(decode, (sources, decoder))
    full = jnp.sum(parts_all.reshape(LAYERS, GROUP, TOK, D), axis=1).astype(jnp.bfloat16)
    reconstruction = full.reshape(LAYERS * GROUP, TOK // GROUP, D)
    return reconstruction, latent_acts
```

```python
import functools
import math

import jax
import jax.numpy as jnp
from jax import lax
from jax.experimental import pallas as pl
from jax.experimental.pallas import tpu as pltpu
from jax.sharding import PartitionSpec as P

LAYERS = 4
VMEM_LIMIT = 40 * 1024 * 1024


def swapped(shard, axis, stride):
    return lax.ppermute(shard, axis, [(i, i ^ 1 << stride) for i in range(lax.axis_size(axis))])


def passed_along(value, axis, steps):
    count = lax.axis_size(axis)
    first, last = (max(0, -steps), min(count, count - steps))
    return lax.ppermute(value, axis, [(source, source + steps) for source in range(first, last)])


def group_reduce(partial_rows, group_size):
    current = partial_rows
    section_index = lax.axis_index("section")
    level_count = group_size.bit_length() - 1
    for level in reversed(range(level_count)):
        half = current.shape[0] // 2
        lower = current[:half]
        upper = current[half:]
        high_side = section_index // 2**level % 2 == 1
        kept = jnp.where(high_side, upper, lower)
        sent = jnp.where(high_side, lower, upper)
        received = swapped(sent.astype(jnp.bfloat16), "section", level).astype(sent.dtype)
        current = kept + received
    return current


def encode_kernel(x_ref, own_ref, sib_ref, bias_ref, thr_ref, acts_ref):
    count, rows, depth = x_ref.shape
    lat = own_ref.shape[1]
    halves = []
    for side, weights in enumerate((own_ref, sib_ref)):
        total = jnp.zeros((rows, lat), jnp.float32)
        for source in range(count):
            total += jnp.dot(
                x_ref[source],
                weights[source * depth:(source + 1) * depth, :],
                preferred_element_type=jnp.float32,
            )
        preact = total + bias_ref[side:side + 1, :]
        halves.append(jnp.where(preact > thr_ref[side:side + 1, :], preact, 0.0).astype(jnp.bfloat16))
    acts_ref[...] = jnp.concatenate(halves, axis=1)


def encode(gathered, own, sib, bias, thr):
    rows, lat = gathered.shape[1], own.shape[1]
    return pl.pallas_call(
        encode_kernel,
        out_shape=jax.ShapeDtypeStruct((rows, 2 * lat), jnp.bfloat16),
        compiler_params=pltpu.CompilerParams(vmem_limit_bytes=VMEM_LIMIT),
    )(gathered, own, sib, bias, thr)


def decode_kernel(reach, *refs):
    acts = refs[:reach]
    own_ref, sib_ref, out_ref = refs[reach:]
    per_block, _, width = out_ref.shape
    lat = own_ref.shape[1]
    total = None
    for hop in range(reach):
        values = acts[hop][...]
        part = jnp.dot(values[:, :lat], own_ref[hop], preferred_element_type=jnp.float32)
        part += jnp.dot(values[:, lat:], sib_ref[hop], preferred_element_type=jnp.float32)
        total = part if total is None else total + part
    for piece in range(per_block):
        out_ref[piece] = total[:, piece * width:(piece + 1) * width].astype(jnp.bfloat16)


def decode(acts, own, sib, count):
    reach, lat, features = own.shape
    rows = acts[0].shape[0]
    width = features // count
    block = math.lcm(width, 128)
    whole = pl.BlockSpec(acts[0].shape, lambda i: (0, 0))
    weights = pl.BlockSpec((reach, lat, block), lambda i: (0, 0, i))
    return pl.pallas_call(
        functools.partial(decode_kernel, reach),
        grid=(features // block,),
        in_specs=[whole] * reach + [weights] * 2,
        out_specs=pl.BlockSpec((block // width, rows, width), lambda i: (i, 0, 0)),
        out_shape=jax.ShapeDtypeStruct((count, rows, width), jnp.bfloat16),
        compiler_params=pltpu.CompilerParams(vmem_limit_bytes=VMEM_LIMIT),
    )(*acts, own, sib)


def shards(residual, encoder, enc_bias, gate_code, decoder):
    group_size = lax.axis_size("section") // LAYERS
    layer_index = lax.axis_index("section") // group_size
    count = lax.axis_size("latent")
    chips = count // 2
    core = lax.axis_index("latent") % 2
    resid_layer = lax.dynamic_index_in_dim(residual, layer_index, 0, keepdims=False)
    tok, width = resid_layer.shape
    half = tok // 2
    enc_own = encoder[0]
    dec_own = decoder[0]
    lat = enc_own.shape[1]
    reach = dec_own.shape[0]

    threshold = 10000.0 * (gate_code[0].astype(jnp.float32) - 1.0)
    gates_own = jnp.stack([enc_bias[0], threshold])
    enc_sib = swapped(enc_own, "latent", 0)
    gates_sib = swapped(gates_own, "latent", 0)
    dec_sib = swapped(dec_own, "latent", 0)
    bias, thr = (jnp.stack([gates_own[i], gates_sib[i]]) for i in (0, 1))

    split = resid_layer.reshape(1, 2, half, width)
    outgoing = jnp.broadcast_to(split, (chips, 2, half, width)).reshape(count, half, width)
    gathered = lax.all_to_all(outgoing, "latent", 0, 0, tiled=True)
    acts = encode(gathered, enc_own, enc_sib, bias, thr)

    sources = [acts]
    for hop in range(1, reach):
        sources.append(passed_along(acts, "section", hop * group_size))
    other = swapped(acts[:, lat:], "latent", 0)
    mine = acts[:, :lat]
    latent_acts = jnp.where(core == 0, jnp.stack([mine, other]), jnp.stack([other, mine])).reshape(tok, lat)

    shares = decode(sources, dec_own, dec_sib, count)
    received = lax.all_to_all(shares, "latent", 0, 0, tiled=True)
    summed = jnp.sum(received.reshape(chips, tok, width).astype(jnp.float32), axis=0)
    rebuilt = group_reduce(summed, group_size).astype(jnp.bfloat16)
    return (rebuilt[None], latent_acts[None])


def solution(mesh):
    return jax.shard_map(
        shards,
        mesh=mesh,
        in_specs=(
            P(None, None, "latent"),
            P("section", None, "latent"),
            P("section", "latent"),
            P("section", "latent"),
            P("section", None, "latent", None),
        ),
        out_specs=(P("section", None, "latent"), P("section", None, "latent")),
        check_vma=False,
    )
```

```python
import functools
import math

import jax
import jax.numpy as jnp
from jax import lax
from jax.experimental import pallas as pl
from jax.experimental.pallas import tpu as pltpu
from jax.sharding import PartitionSpec as P

LAYERS = 4
VMEM_LIMIT = 16 * 1024 * 1024


def swapped(shard, axis, stride):
    return lax.ppermute(shard, axis, [(i, i ^ 1 << stride) for i in range(lax.axis_size(axis))])


def passed_along(value, axis, steps):
    count = lax.axis_size(axis)
    first, last = (max(0, -steps), min(count, count - steps))
    return lax.ppermute(value, axis, [(source, source + steps) for source in range(first, last)])


def group_reduce(partial_rows, group_size):
    current = partial_rows
    section_index = lax.axis_index("section")
    level_count = group_size.bit_length() - 1
    for level in reversed(range(level_count)):
        half = current.shape[0] // 2
        lower = current[:half]
        upper = current[half:]
        high_side = section_index // 2**level % 2 == 1
        kept = jnp.where(high_side, upper, lower)
        sent = jnp.where(high_side, lower, upper)
        received = swapped(sent.astype(jnp.bfloat16), "section", level).astype(sent.dtype)
        current = kept + received
    return current


def spread_kernel(group_size, first, resid_ref, out_ref, sems):
    layer = lax.axis_index("section") // group_size
    rows = out_ref.shape[2]
    copies = [
        pltpu.make_async_copy(
            resid_ref.at[layer, :, pl.ds(first, rows), :], out_ref.at[chip], sems.at[chip]
        )
        for chip in range(out_ref.shape[0])
    ]
    for copy in copies:
        copy.start()
    for copy in copies:
        copy.wait()


def spread(residual, chips, group_size, first, rows):
    width = residual.shape[-1]
    return pl.pallas_call(
        functools.partial(spread_kernel, group_size, first),
        in_specs=[pl.BlockSpec(memory_space=pl.ANY)],
        out_shape=jax.ShapeDtypeStruct((chips, 2, rows, width), residual.dtype),
        scratch_shapes=[pltpu.SemaphoreType.DMA((chips,))],
        compiler_params=pltpu.CompilerParams(vmem_limit_bytes=VMEM_LIMIT),
    )(residual)


def encode_kernel(x_ref, weights_ref, gates_ref, acts_ref):
    count, rows, depth = x_ref.shape
    total = jnp.zeros(acts_ref.shape, jnp.float32)
    for source in range(count):
        total += jnp.dot(
            x_ref[source],
            weights_ref[source * depth:(source + 1) * depth, :],
            preferred_element_type=jnp.float32,
        )
    preact = total + gates_ref[0:1, :]
    acts_ref[...] = jnp.where(preact > gates_ref[1:2, :], preact, 0.0).astype(jnp.bfloat16)


def encode(gathered, weights, gates):
    rows, lat = gathered.shape[1], weights.shape[1]
    return pl.pallas_call(
        encode_kernel,
        out_shape=jax.ShapeDtypeStruct((rows, lat), jnp.bfloat16),
        compiler_params=pltpu.CompilerParams(vmem_limit_bytes=VMEM_LIMIT),
    )(gathered, weights, gates)


def decode_kernel(reach, *refs):
    acts = refs[:reach]
    weights_ref, out_ref = refs[reach:]
    count, _, width = out_ref.shape
    block = math.lcm(width, 128)
    per_block = block // width
    for step in range(count // per_block):
        columns = slice(step * block, (step + 1) * block)
        total = None
        for hop in range(reach):
            part = jnp.dot(acts[hop][...], weights_ref[hop, :, columns], preferred_element_type=jnp.float32)
            total = part if total is None else total + part
        for piece in range(per_block):
            out_ref[step * per_block + piece] = total[:, piece * width:(piece + 1) * width].astype(jnp.bfloat16)


def decode(acts, weights, count):
    reach, _, features = weights.shape
    rows = acts[0].shape[0]
    return pl.pallas_call(
        functools.partial(decode_kernel, reach),
        out_shape=jax.ShapeDtypeStruct((count, rows, features // count), jnp.bfloat16),
        compiler_params=pltpu.CompilerParams(vmem_limit_bytes=VMEM_LIMIT),
    )(*acts, weights)


def shards(residual, encoder, enc_bias, gate_code, decoder):
    group_size = lax.axis_size("section") // LAYERS
    count = lax.axis_size("latent")
    chips = count // 2
    core = lax.axis_index("latent") % 2
    layers, tok, width = residual.shape
    half = tok // 2
    lat = encoder.shape[2]
    reach = decoder.shape[1]
    first_rows = half // 32 * 16
    chunks = [(0, first_rows), (first_rows, half - first_rows)]

    threshold = 10000.0 * (gate_code[0].astype(jnp.float32) - 1.0)
    gates_own = jnp.stack([enc_bias[0], threshold])
    halves = residual.reshape(layers, 2, half, width)
    travelling = []
    for first, rows in chunks:
        outgoing = spread(halves, chips, group_size, first, rows).reshape(count, rows, width)
        travelling.append(lax.all_to_all(outgoing, "latent", 0, 0, tiled=True))

    gates = jnp.concatenate([gates_own, swapped(gates_own, "latent", 0)], axis=1)
    enc_both = jnp.concatenate([encoder[0], swapped(encoder[0], "latent", 0)], axis=1)
    dec_both = jnp.concatenate([decoder[0], swapped(decoder[0], "latent", 0)], axis=1)

    sums, pieces = [], []
    for gathered in travelling:
        gathered, dec_both = lax.optimization_barrier((gathered, dec_both))
        acts = encode(gathered, enc_both, gates)
        sources = [acts]
        for hop in range(1, reach):
            sources.append(passed_along(acts, "section", hop * group_size))
        shares = decode(sources, dec_both, count)
        received = lax.all_to_all(shares, "latent", 0, 0, tiled=True)
        sums.append(jnp.sum(received.reshape(chips, 2, -1, width).astype(jnp.float32), axis=0))
        pieces.append(acts)

    summed = jnp.concatenate(sums, axis=1).reshape(tok, width)
    rebuilt = group_reduce(summed, group_size).astype(jnp.bfloat16)
    acts = jnp.concatenate(pieces, axis=0)
    mine, other = acts[:, :lat], swapped(acts[:, lat:], "latent", 0)
    latent_acts = jnp.where(core == 0, jnp.stack([mine, other]), jnp.stack([other, mine])).reshape(tok, lat)
    return (rebuilt[None], latent_acts[None])


def solution(mesh):
    return jax.shard_map(
        shards,
        mesh=mesh,
        in_specs=(
            P(None, None, "latent"),
            P("section", None, "latent"),
            P("section", "latent"),
            P("section", "latent"),
            P("section", None, "latent", None),
        ),
        out_specs=(P("section", None, "latent"), P("section", None, "latent")),
        check_vma=False,
    )
```

```python
import functools
import math

import jax
import jax.numpy as jnp
from jax import lax
from jax.experimental import pallas as pl
from jax.experimental.pallas import tpu as pltpu
from jax.sharding import PartitionSpec as P

LAYERS = 4
VMEM_LIMIT = 16 * 1024 * 1024


def swapped(shard, axis, stride):
    return lax.ppermute(shard, axis, [(i, i ^ 1 << stride) for i in range(lax.axis_size(axis))])


def passed_along(value, axis, steps):
    count = lax.axis_size(axis)
    first, last = (max(0, -steps), min(count, count - steps))
    return lax.ppermute(value, axis, [(source, source + steps) for source in range(first, last)])


def group_reduce(partial_rows, group_size):
    current = partial_rows
    section_index = lax.axis_index("section")
    level_count = group_size.bit_length() - 1
    for level in reversed(range(level_count)):
        half = current.shape[0] // 2
        lower = current[:half]
        upper = current[half:]
        high_side = section_index // 2**level % 2 == 1
        kept = jnp.where(high_side, upper, lower)
        sent = jnp.where(high_side, lower, upper)
        received = swapped(sent.astype(jnp.bfloat16), "section", level).astype(sent.dtype)
        current = kept + received
    return current


def to_peer(value, offset):
    return lax.ppermute(value, "latent", [(i, i ^ offset) for i in range(lax.axis_size("latent"))])


def call(kernel, out_shape, in_specs=None, scratch=()):
    specs = {} if in_specs is None else {"in_specs": in_specs}
    return pl.pallas_call(
        kernel,
        out_shape=out_shape,
        scratch_shapes=list(scratch),
        compiler_params=pltpu.CompilerParams(vmem_limit_bytes=VMEM_LIMIT),
        **specs,
    )


def halves_kernel(group_size, resid_ref, mine_ref, other_ref, sems):
    layer = lax.axis_index("section") // group_size
    core = lax.axis_index("latent") % 2
    copies = [
        pltpu.make_async_copy(resid_ref.at[layer, core], mine_ref, sems.at[0]),
        pltpu.make_async_copy(resid_ref.at[layer, 1 - core], other_ref, sems.at[1]),
    ]
    for copy in copies:
        copy.start()
    for copy in copies:
        copy.wait()


def token_halves(residual, group_size):
    layers, tok, width = residual.shape
    shape = jax.ShapeDtypeStruct((tok // 2, width), residual.dtype)
    return call(
        functools.partial(halves_kernel, group_size),
        (shape, shape),
        [pl.BlockSpec(memory_space=pltpu.HBM)],
        [pltpu.SemaphoreType.DMA((2,))],
    )(residual.reshape(layers, 2, tok // 2, width))


def encode_kernel(*refs):
    *x_refs, own_ref, sib_ref, bias_ref, thr_ref, acts_ref = refs
    depth = x_refs[0].shape[1]
    place = lax.axis_index("latent")
    total = jnp.zeros(acts_ref.shape, jnp.float32)
    for offset, x_ref in enumerate(x_refs):
        rows = pl.ds(pl.multiple_of((place ^ offset) * depth, 16), depth)
        weights = jnp.concatenate([own_ref[rows, :], sib_ref[rows, :]], axis=1)
        total += jnp.dot(x_ref[...], weights, preferred_element_type=jnp.float32)
    preact = total + bias_ref[...]
    acts_ref[...] = jnp.where(preact > thr_ref[...], preact, 0.0).astype(jnp.bfloat16)


def encode(pieces, own, sib, bias, thr):
    shape = jax.ShapeDtypeStruct((pieces[0].shape[0], 2 * own.shape[1]), jnp.bfloat16)
    return call(encode_kernel, shape)(*pieces, own, sib, bias, thr)


def decoded(acts, own_ref, sib_ref, columns):
    total = None
    for hop, values in enumerate(acts):
        weights = jnp.concatenate([own_ref[hop, :, columns], sib_ref[hop, :, columns]], axis=0)
        part = jnp.dot(values[...], weights, preferred_element_type=jnp.float32)
        total = part if total is None else total + part
    return total


def decode_chip_kernel(chip_offset, *refs):
    *acts, own_ref, sib_ref, same_ref, cross_ref = refs
    width = same_ref.shape[1]
    place = lax.axis_index("latent")
    columns = pl.ds(pl.multiple_of(((place // 2) ^ chip_offset) * (2 * width), 128), 2 * width)
    total = decoded(acts, own_ref, sib_ref, columns).astype(jnp.bfloat16)
    low, high = total[:, :width], total[:, width:]
    first_core = place % 2 == 0
    same_ref[...] = jnp.where(first_core, low, high)
    cross_ref[...] = jnp.where(first_core, high, low)


def decode_chip(chip_offset, acts, own, sib, width):
    shape = jax.ShapeDtypeStruct((acts[0].shape[0], width), jnp.bfloat16)
    return call(functools.partial(decode_chip_kernel, chip_offset), (shape, shape))(*acts, own, sib)


def decode_all_kernel(*refs):
    *acts, own_ref, sib_ref, out_ref = refs
    count, _, width = out_ref.shape
    block = math.lcm(width, 128)
    per_block = block // width
    for step in range(count // per_block):
        total = decoded(acts, own_ref, sib_ref, slice(step * block, (step + 1) * block))
        for piece in range(per_block):
            out_ref[step * per_block + piece] = total[:, piece * width:(piece + 1) * width].astype(jnp.bfloat16)


def sum_two_kernel(a_ref, b_ref, out_ref):
    out_ref[...] = (a_ref[...].astype(jnp.float32) + b_ref[...].astype(jnp.float32)).astype(jnp.bfloat16)


def sum_two(a, b):
    return call(sum_two_kernel, jax.ShapeDtypeStruct(a.shape, jnp.bfloat16))(a, b)


def finish_kernel(*refs):
    *parts, out_ref = refs
    half = len(parts) // 2
    rows = parts[0].shape[0]
    core = lax.axis_index("latent") % 2
    for place, group in ((core, parts[:half]), (1 - core, parts[half:])):
        total = group[0][...].astype(jnp.float32)
        for part in group[1:]:
            total += part[...].astype(jnp.float32)
        out_ref[pl.ds(pl.multiple_of(place * rows, 16), rows), :] = total.astype(out_ref.dtype)


def finish(mine, other, dtype):
    rows, width = mine[0].shape
    return call(finish_kernel, jax.ShapeDtypeStruct((2 * rows, width), dtype))(*mine, *other)


def gather(mine, other):
    count = lax.axis_size("latent")
    if count != 8:
        core = lax.axis_index("latent") % 2
        pair = jnp.where(core == 0, jnp.stack([mine, other]), jnp.stack([other, mine]))
        outgoing = jnp.broadcast_to(pair, (count // 2, *pair.shape)).reshape(count, *mine.shape)
        everyone = lax.all_to_all(outgoing, "latent", 0, 0, tiled=True)
        place = lax.axis_index("latent")
        return [lax.dynamic_index_in_dim(everyone, place ^ i, 0, keepdims=False) for i in range(count)]
    x_same, y_cross = to_peer(mine, 2), to_peer(other, 5)
    x_cross, y_same = to_peer(other, 3), to_peer(mine, 4)
    return [mine, to_peer(other, 1), x_same, x_cross, y_same, y_cross, to_peer(x_same, 4), to_peer(y_cross, 2)]


def decode_and_scatter(acts, own, sib, width, dtype):
    count = lax.axis_size("latent")
    rows = acts[0].shape[0]
    if count != 8:
        shares = call(decode_all_kernel, jax.ShapeDtypeStruct((count, rows, width), jnp.bfloat16))(*acts, own, sib)
        received = lax.all_to_all(shares, "latent", 0, 0, tiled=True)
        return jnp.sum(received.reshape(count // 2, 2 * rows, width).astype(jnp.float32), axis=0).astype(dtype)
    diag_same, diag_cross = decode_chip(3, acts, own, sib, width)
    for_y, for_x = to_peer(diag_same, 2), to_peer(diag_cross, 4)
    x_same, x_cross = decode_chip(1, acts, own, sib, width)
    y_same, y_cross = decode_chip(2, acts, own, sib, width)
    from_x_same, from_y_cross = to_peer(x_same, 2), to_peer(y_cross, 5)
    own_same, own_cross = decode_chip(0, acts, own, sib, width)
    from_sib = to_peer(own_cross, 1)
    from_y_same = to_peer(sum_two(y_same, for_y), 4)
    from_x_cross = to_peer(sum_two(x_cross, for_x), 3)
    return finish((own_same, from_x_same, from_y_same), (from_sib, from_x_cross, from_y_cross), dtype)


def shards(residual, encoder, enc_bias, gate_code, decoder):
    group_size = lax.axis_size("section") // LAYERS
    core = lax.axis_index("latent") % 2
    _, tok, width = residual.shape
    lat = encoder.shape[2]
    reach = decoder.shape[1]

    mine, other = token_halves(residual, group_size)
    pieces = gather(mine, other)

    threshold = 10000.0 * (gate_code[0].astype(jnp.float32) - 1.0)
    gates_own = jnp.stack([enc_bias[0], threshold])
    gates = jnp.concatenate([gates_own, to_peer(gates_own, 1)], axis=1)
    enc_sib = to_peer(encoder[0], 1)
    dec_sib = to_peer(decoder[0], 1)

    acts = encode(pieces, encoder[0], enc_sib, gates[:1], gates[1:])
    sources = [acts]
    for hop in range(1, reach):
        sources.append(passed_along(acts, "section", hop * group_size))
    out_type = jnp.bfloat16 if group_size == 1 else jnp.float32
    summed = decode_and_scatter(sources, decoder[0], dec_sib, width, out_type)
    rebuilt = group_reduce(summed, group_size).astype(jnp.bfloat16)

    kept, passed = acts[:, :lat], to_peer(acts[:, lat:], 1)
    latent_acts = jnp.where(core == 0, jnp.stack([kept, passed]), jnp.stack([passed, kept])).reshape(tok, lat)
    return (rebuilt[None], latent_acts[None])


def solution(mesh):
    return jax.shard_map(
        shards,
        mesh=mesh,
        in_specs=(
            P(None, None, "latent"),
            P("section", None, "latent"),
            P("section", "latent"),
            P("section", "latent"),
            P("section", None, "latent", None),
        ),
        out_specs=(P("section", None, "latent"), P("section", None, "latent")),
        check_vma=False,
    )
```

```python
import functools
import math

import jax
import jax.numpy as jnp
from jax import lax
from jax.experimental import pallas as pl
from jax.experimental.pallas import tpu as pltpu
from jax.sharding import PartitionSpec as P

LAYERS = 4
VMEM_LIMIT = 16 * 1024 * 1024
HALVES_LIMIT = 60 * 1024 * 1024


def swapped(shard, axis, stride):
    return lax.ppermute(shard, axis, [(i, i ^ 1 << stride) for i in range(lax.axis_size(axis))])


def after(value, *others):
    return lax.optimization_barrier((value, *others))[0]


def layer_offsets(reach):
    return sorted({layer ^ (layer - hop) for hop in range(1, reach) for layer in range(hop, LAYERS)})


def other_layers(value, reach, group_size):
    received = []
    for offset in layer_offsets(reach):
        wanted = {layer for layer in range(LAYERS) if 0 < layer - (layer ^ offset) < reach}
        pairs = [(index, index ^ offset * group_size) for index in range(lax.axis_size("section"))]
        pairs = [pair for pair in pairs if wanted & {end // group_size for end in pair}]
        received.append(lax.ppermute(value, "section", pairs))
    return received


def by_hop(acts, reach):
    layer = lax.axis_index("section") // (lax.axis_size("section") // LAYERS)
    own, *received = acts
    yield own[...]
    for hop in range(1, reach):
        source = jnp.zeros(own.shape, own.dtype)
        for offset, arrived in zip(layer_offsets(reach), received):
            for target in range(hop, LAYERS):
                if target ^ offset == target - hop:
                    source = jnp.where(layer == target, arrived[...], source)
        yield source


def group_reduce(partial_rows, group_size):
    current = partial_rows
    section_index = lax.axis_index("section")
    level_count = group_size.bit_length() - 1
    for level in reversed(range(level_count)):
        half = current.shape[0] // 2
        lower = current[:half]
        upper = current[half:]
        high_side = section_index // 2**level % 2 == 1
        kept = jnp.where(high_side, upper, lower)
        sent = jnp.where(high_side, lower, upper)
        received = swapped(sent.astype(jnp.bfloat16), "section", level).astype(sent.dtype)
        current = kept + received
    return current


def to_peer(value, offset):
    return lax.ppermute(value, "latent", [(i, i ^ offset) for i in range(lax.axis_size("latent"))])


def call(kernel, out_shape, in_specs=None, scratch=(), limit=VMEM_LIMIT):
    specs = {} if in_specs is None else {"in_specs": in_specs}
    return pl.pallas_call(
        kernel,
        out_shape=out_shape,
        scratch_shapes=list(scratch),
        compiler_params=pltpu.CompilerParams(vmem_limit_bytes=limit),
        **specs,
    )


def halves_kernel(group_size, resid_ref, mine_ref, other_ref, sems):
    layer = lax.axis_index("section") // group_size
    core = lax.axis_index("latent") % 2
    copies = [
        pltpu.make_async_copy(resid_ref.at[layer, core], mine_ref, sems.at[0]),
        pltpu.make_async_copy(resid_ref.at[layer, 1 - core], other_ref, sems.at[1]),
    ]
    for copy in copies:
        copy.start()
    for copy in copies:
        copy.wait()


def token_halves(residual, group_size):
    layers, tok, width = residual.shape
    shape = jax.ShapeDtypeStruct((tok // 2, width), residual.dtype)
    return call(
        functools.partial(halves_kernel, group_size),
        (shape, shape),
        [pl.BlockSpec(memory_space=pltpu.HBM)],
        [pltpu.SemaphoreType.DMA((2,))],
        HALVES_LIMIT,
    )(residual.reshape(layers, 2, tok // 2, width))


def encode_kernel(*refs):
    *x_refs, own_ref, sib_ref, bias_ref, thr_ref, acts_ref = refs
    depth = x_refs[0].shape[1]
    place = lax.axis_index("latent")
    total = jnp.zeros(acts_ref.shape, jnp.float32)
    for offset, x_ref in enumerate(x_refs):
        rows = pl.ds(pl.multiple_of((place ^ offset) * depth, 16), depth)
        weights = jnp.concatenate([own_ref[rows, :], sib_ref[rows, :]], axis=1)
        total += jnp.dot(x_ref[...], weights, preferred_element_type=jnp.float32)
    preact = total + bias_ref[...]
    acts_ref[...] = jnp.where(preact > thr_ref[...], preact, 0.0).astype(jnp.bfloat16)


def encode(pieces, own, sib, bias, thr):
    shape = jax.ShapeDtypeStruct((pieces[0].shape[0], 2 * own.shape[1]), jnp.bfloat16)
    return call(encode_kernel, shape)(*pieces, own, sib, bias, thr)


def decoded(acts, own_ref, sib_ref, columns):
    total = None
    for hop, values in enumerate(by_hop(acts, own_ref.shape[0])):
        weights = jnp.concatenate([own_ref[hop, :, columns], sib_ref[hop, :, columns]], axis=0)
        part = jnp.dot(values, weights, preferred_element_type=jnp.float32)
        total = part if total is None else total + part
    return total


def decode_chip_kernel(chip_offset, *refs):
    *acts, own_ref, sib_ref, same_ref, cross_ref = refs
    width = same_ref.shape[1]
    place = lax.axis_index("latent")
    columns = pl.ds(pl.multiple_of(((place // 2) ^ chip_offset) * (2 * width), 128), 2 * width)
    total = decoded(acts, own_ref, sib_ref, columns).astype(jnp.bfloat16)
    low, high = total[:, :width], total[:, width:]
    first_core = place % 2 == 0
    same_ref[...] = jnp.where(first_core, low, high)
    cross_ref[...] = jnp.where(first_core, high, low)


def decode_chip(chip_offset, acts, own, sib, width):
    shape = jax.ShapeDtypeStruct((acts[0].shape[0], width), jnp.bfloat16)
    return call(functools.partial(decode_chip_kernel, chip_offset), (shape, shape))(*acts, own, sib)


def decode_all_kernel(*refs):
    *acts, own_ref, sib_ref, out_ref = refs
    count, _, width = out_ref.shape
    block = math.lcm(width, 128)
    per_block = block // width
    for step in range(count // per_block):
        total = decoded(acts, own_ref, sib_ref, slice(step * block, (step + 1) * block))
        for piece in range(per_block):
            out_ref[step * per_block + piece] = total[:, piece * width:(piece + 1) * width].astype(jnp.bfloat16)


def sum_two_kernel(a_ref, b_ref, out_ref):
    out_ref[...] = (a_ref[...].astype(jnp.float32) + b_ref[...].astype(jnp.float32)).astype(jnp.bfloat16)


def sum_two(a, b):
    return call(sum_two_kernel, jax.ShapeDtypeStruct(a.shape, jnp.bfloat16))(a, b)


def finish_kernel(*refs):
    *parts, out_ref = refs
    half = len(parts) // 2
    rows = parts[0].shape[0]
    core = lax.axis_index("latent") % 2
    for place, group in ((core, parts[:half]), (1 - core, parts[half:])):
        total = group[0][...].astype(jnp.float32)
        for part in group[1:]:
            total += part[...].astype(jnp.float32)
        out_ref[pl.ds(pl.multiple_of(place * rows, 16), rows), :] = total.astype(out_ref.dtype)


def finish(mine, other, dtype):
    rows, width = mine[0].shape
    return call(finish_kernel, jax.ShapeDtypeStruct((2 * rows, width), dtype))(*mine, *other)


def gather(mine, other, gates, encoder, decoder):
    count = lax.axis_size("latent")
    if count != 8:
        core = lax.axis_index("latent") % 2
        pair = jnp.where(core == 0, jnp.stack([mine, other]), jnp.stack([other, mine]))
        outgoing = jnp.broadcast_to(pair, (count // 2, *pair.shape)).reshape(count, *mine.shape)
        everyone = lax.all_to_all(outgoing, "latent", 0, 0, tiled=True)
        place = lax.axis_index("latent")
        pieces = [lax.dynamic_index_in_dim(everyone, place ^ i, 0, keepdims=False) for i in range(count)]
        return pieces, *(to_peer(value, 1) for value in (gates, encoder, decoder))
    x_same, y_cross = to_peer(mine, 2), to_peer(other, 5)
    x_cross, y_same = to_peer(other, 3), to_peer(mine, 4)
    enc_sib = to_peer(encoder, 1)
    near = (x_same, y_cross, x_cross, y_same, enc_sib)
    diag_same, diag_cross = to_peer(after(x_same, *near), 4), to_peer(after(y_cross, *near), 2)
    from_sib, gates_sib, dec_sib = (to_peer(after(value, *near), 1) for value in (other, gates, decoder))
    return [mine, from_sib, x_same, x_cross, y_same, y_cross, diag_same, diag_cross], gates_sib, enc_sib, dec_sib


def decode_and_scatter(acts, own, sib, width, dtype):
    count = lax.axis_size("latent")
    rows = acts[0].shape[0]
    if count != 8:
        shares = call(decode_all_kernel, jax.ShapeDtypeStruct((count, rows, width), jnp.bfloat16))(*acts, own, sib)
        received = lax.all_to_all(shares, "latent", 0, 0, tiled=True)
        return jnp.sum(received.reshape(count // 2, 2 * rows, width).astype(jnp.float32), axis=0).astype(dtype)
    diag_same, diag_cross = decode_chip(3, acts, own, sib, width)
    for_y, for_x = to_peer(diag_same, 2), to_peer(diag_cross, 4)
    x_same, x_cross = decode_chip(1, acts, own, sib, width)
    y_same, y_cross = decode_chip(2, acts, own, sib, width)
    from_x_same, from_y_cross = to_peer(x_same, 2), to_peer(y_cross, 5)
    own_same, own_cross = decode_chip(0, acts, own, sib, width)
    from_sib = to_peer(own_cross, 1)
    from_y_same = to_peer(sum_two(y_same, for_y), 4)
    from_x_cross = to_peer(sum_two(x_cross, for_x), 3)
    return finish((own_same, from_x_same, from_y_same), (from_sib, from_x_cross, from_y_cross), dtype)


def shards(residual, encoder, enc_bias, gate_code, decoder):
    group_size = lax.axis_size("section") // LAYERS
    core = lax.axis_index("latent") % 2
    _, tok, width = residual.shape
    lat = encoder.shape[2]
    reach = decoder.shape[1]

    mine, other = token_halves(residual, group_size)
    threshold = 10000.0 * (gate_code[0].astype(jnp.float32) - 1.0)
    gates_own = jnp.stack([enc_bias[0], threshold])
    pieces, gates_sib, enc_sib, dec_sib = gather(mine, other, gates_own, encoder[0], decoder[0])
    gates = jnp.concatenate([gates_own, gates_sib], axis=1)

    acts = encode(pieces, encoder[0], enc_sib, gates[:1], gates[1:])
    sources = [acts, *other_layers(acts, reach, group_size)]
    out_type = jnp.bfloat16 if group_size == 1 else jnp.float32
    summed = decode_and_scatter(sources, decoder[0], dec_sib, width, out_type)
    rebuilt = group_reduce(summed, group_size).astype(jnp.bfloat16)

    kept, passed = acts[:, :lat], to_peer(acts[:, lat:], 1)
    latent_acts = jnp.where(core == 0, jnp.stack([kept, passed]), jnp.stack([passed, kept])).reshape(tok, lat)
    return (rebuilt[None], latent_acts[None])


def solution(mesh):
    return jax.shard_map(
        shards,
        mesh=mesh,
        in_specs=(
            P(None, None, "latent"),
            P("section", None, "latent"),
            P("section", "latent"),
            P("section", "latent"),
            P("section", None, "latent", None),
        ),
        out_specs=(P("section", None, "latent"), P("section", None, "latent")),
        check_vma=False,
    )
```

```python
import functools
import math

import jax
import jax.numpy as jnp
from jax import lax
from jax.experimental import pallas as pl
from jax.experimental.pallas import tpu as pltpu
from jax.sharding import PartitionSpec as P

LAYERS = 4
VMEM_LIMIT = 16 * 1024 * 1024
HALVES_LIMIT = VMEM_LIMIT


def swapped(shard, axis, stride):
    return lax.ppermute(shard, axis, [(i, i ^ 1 << stride) for i in range(lax.axis_size(axis))])


def after(value, *others):
    return lax.optimization_barrier((value, *others))[0]


def layer_offsets(reach):
    return sorted({layer ^ (layer - hop) for hop in range(1, reach) for layer in range(hop, LAYERS)})


def other_layers(value, reach, group_size):
    received = []
    for offset in layer_offsets(reach):
        wanted = {layer for layer in range(LAYERS) if 0 < layer - (layer ^ offset) < reach}
        pairs = [(index, index ^ offset * group_size) for index in range(lax.axis_size("section"))]
        pairs = [pair for pair in pairs if wanted & {end // group_size for end in pair}]
        received.append(lax.ppermute(value, "section", pairs))
    return received


def by_hop(acts, reach):
    layer = lax.axis_index("section") // (lax.axis_size("section") // LAYERS)
    own, *received = acts
    yield own[...]
    for hop in range(1, reach):
        source = jnp.zeros(own.shape, own.dtype)
        for offset, arrived in zip(layer_offsets(reach), received):
            for target in range(hop, LAYERS):
                if target ^ offset == target - hop:
                    source = jnp.where(layer == target, arrived[...], source)
        yield source


def group_reduce(partial_rows, group_size):
    current = partial_rows
    section_index = lax.axis_index("section")
    level_count = group_size.bit_length() - 1
    for level in reversed(range(level_count)):
        half = current.shape[0] // 2
        lower = current[:half]
        upper = current[half:]
        high_side = section_index // 2**level % 2 == 1
        kept = jnp.where(high_side, upper, lower)
        sent = jnp.where(high_side, lower, upper)
        received = swapped(sent.astype(jnp.bfloat16), "section", level).astype(sent.dtype)
        current = kept + received
    return current


def to_peer(value, offset):
    return lax.ppermute(value, "latent", [(i, i ^ offset) for i in range(lax.axis_size("latent"))])


def call(kernel, out_shape, in_specs=None, scratch=(), limit=VMEM_LIMIT, cost=None):
    specs = {} if in_specs is None else {"in_specs": in_specs}
    return pl.pallas_call(
        kernel,
        out_shape=out_shape,
        scratch_shapes=list(scratch),
        cost_estimate=cost,
        compiler_params=pltpu.CompilerParams(vmem_limit_bytes=limit),
        **specs,
    )


def halves_kernel(group_size, resid_ref, mine_ref, other_ref, sems):
    layer = lax.axis_index("section") // group_size
    core = lax.axis_index("latent") % 2
    copies = [
        pltpu.make_async_copy(resid_ref.at[layer, core], mine_ref, sems.at[0]),
        pltpu.make_async_copy(resid_ref.at[layer, 1 - core], other_ref, sems.at[1]),
    ]
    for copy in copies:
        copy.start()
    for copy in copies:
        copy.wait()


def token_halves(residual, group_size):
    layers, tok, width = residual.shape
    shape = jax.ShapeDtypeStruct((tok // 2, width), residual.dtype)
    return call(
        functools.partial(halves_kernel, group_size),
        (shape, shape),
        [pl.BlockSpec(memory_space=pltpu.HBM)],
        [pltpu.SemaphoreType.DMA((2,))],
        HALVES_LIMIT,
    )(residual.reshape(layers, 2, tok // 2, width))


def encoded(total, offsets, x_refs, own_ref, sib_ref):
    depth = x_refs[0].shape[1]
    place = lax.axis_index("latent")
    for offset, x_ref in zip(offsets, x_refs):
        rows = pl.ds(pl.multiple_of((place ^ offset) * depth, 16), depth)
        weights = jnp.concatenate([own_ref[rows, :], sib_ref[rows, :]], axis=1)
        part = jnp.dot(x_ref[...], weights, preferred_element_type=jnp.float32)
        total = part if total is None else total + part
    return total


def encode_near_kernel(offsets, *refs):
    *x_refs, own_ref, sib_ref, gates_ref, gates_sib_ref, out_ref, thr_ref = refs
    bias, thr = (jnp.concatenate([gates_ref[i:i + 1, :], gates_sib_ref[i:i + 1, :]], axis=1) for i in (0, 1))
    out_ref[...] = encoded(None, offsets, x_refs, own_ref, sib_ref) + bias
    thr_ref[...] = thr


def encode_near(pieces, own, sib, gates, gates_sib):
    rows, depth = next(iter(pieces.values())).shape
    shape = jax.ShapeDtypeStruct((rows, 2 * own.shape[1]), jnp.float32)
    cost = pl.CostEstimate(2 * len(pieces) * rows * depth * shape.shape[1], 4 * own.size, 0)
    thr = jax.ShapeDtypeStruct((1, shape.shape[1]), jnp.float32)
    kernel = functools.partial(encode_near_kernel, tuple(pieces))
    return call(kernel, (shape, thr), cost=cost)(*pieces.values(), own, sib, gates, gates_sib)


def encode_kernel(offsets, *refs):
    near_ref, thr_ref, *x_refs, own_ref, sib_ref, acts_ref = refs
    preact = encoded(near_ref[...], offsets, x_refs, own_ref, sib_ref)
    acts_ref[...] = jnp.where(preact > thr_ref[...], preact, 0.0).astype(jnp.bfloat16)


def encode(near, thr, pieces, own, sib):
    shape = jax.ShapeDtypeStruct(near.shape, jnp.bfloat16)
    return call(functools.partial(encode_kernel, tuple(pieces)), shape)(near, thr, *pieces.values(), own, sib)


def decoded(acts, own_ref, sib_ref, columns):
    total = None
    for hop, values in enumerate(by_hop(acts, own_ref.shape[0])):
        weights = jnp.concatenate([own_ref[hop, :, columns], sib_ref[hop, :, columns]], axis=0)
        part = jnp.dot(values, weights, preferred_element_type=jnp.float32)
        total = part if total is None else total + part
    return total


def decode_chip_kernel(chip_offset, *refs):
    *acts, own_ref, sib_ref, same_ref, cross_ref = refs
    width = same_ref.shape[1]
    place = lax.axis_index("latent")
    columns = pl.ds(pl.multiple_of(((place // 2) ^ chip_offset) * (2 * width), 128), 2 * width)
    total = decoded(acts, own_ref, sib_ref, columns).astype(jnp.bfloat16)
    low, high = total[:, :width], total[:, width:]
    first_core = place % 2 == 0
    same_ref[...] = jnp.where(first_core, low, high)
    cross_ref[...] = jnp.where(first_core, high, low)


def decode_chip(chip_offset, acts, own, sib, width):
    shape = jax.ShapeDtypeStruct((acts[0].shape[0], width), jnp.bfloat16)
    return call(functools.partial(decode_chip_kernel, chip_offset), (shape, shape))(*acts, own, sib)


def decode_all_kernel(*refs):
    *acts, own_ref, sib_ref, out_ref = refs
    count, _, width = out_ref.shape
    block = math.lcm(width, 128)
    per_block = block // width
    for step in range(count // per_block):
        total = decoded(acts, own_ref, sib_ref, slice(step * block, (step + 1) * block))
        for piece in range(per_block):
            out_ref[step * per_block + piece] = total[:, piece * width:(piece + 1) * width].astype(jnp.bfloat16)


def sum_two_kernel(a_ref, b_ref, out_ref):
    out_ref[...] = (a_ref[...].astype(jnp.float32) + b_ref[...].astype(jnp.float32)).astype(jnp.bfloat16)


def sum_two(a, b):
    return call(sum_two_kernel, jax.ShapeDtypeStruct(a.shape, jnp.bfloat16))(a, b)


def finish_kernel(*refs):
    *parts, out_ref = refs
    half = len(parts) // 2
    rows = parts[0].shape[0]
    core = lax.axis_index("latent") % 2
    for place, group in ((core, parts[:half]), (1 - core, parts[half:])):
        total = group[0][...].astype(jnp.float32)
        for part in group[1:]:
            total += part[...].astype(jnp.float32)
        out_ref[pl.ds(pl.multiple_of(place * rows, 16), rows), :] = total.astype(out_ref.dtype)


def finish(mine, other, dtype):
    rows, width = mine[0].shape
    return call(finish_kernel, jax.ShapeDtypeStruct((2 * rows, width), dtype))(*mine, *other)


def gather_and_encode(mine, other, gates, encoder, decoder):
    count = lax.axis_size("latent")
    enc_sib, gates_sib = to_peer(encoder, 1), to_peer(gates, 1)
    if count != 8:
        core = lax.axis_index("latent") % 2
        pair = jnp.where(core == 0, jnp.stack([mine, other]), jnp.stack([other, mine]))
        outgoing = jnp.broadcast_to(pair, (count // 2, *pair.shape)).reshape(count, *mine.shape)
        everyone = lax.all_to_all(outgoing, "latent", 0, 0, tiled=True)
        place = lax.axis_index("latent")
        pieces = {i: lax.dynamic_index_in_dim(everyone, place ^ i, 0, keepdims=False) for i in range(count)}
        near, far = {i: pieces[i] for i in range(count // 2)}, {i: pieces[i] for i in range(count // 2, count)}
        dec_sib = to_peer(decoder, 1)
        near_sum, thr = encode_near(near, encoder, enc_sib, gates, gates_sib)
    else:
        near = {0: mine, 1: to_peer(other, 1), 2: to_peer(mine, 2), 5: to_peer(other, 5)}
        far = {6: to_peer(near[2], 4), 7: to_peer(near[5], 2)}
        near |= {3: to_peer(other, 3), 4: to_peer(mine, 4)}
        near_sum, thr = encode_near(near, encoder, enc_sib, gates, gates_sib)
        dec_sib = to_peer(after(decoder, far[6], far[7], near_sum), 1)
    return encode(near_sum, thr, far, encoder, enc_sib), dec_sib


def decode_and_scatter(acts, own, sib, width, dtype):
    count = lax.axis_size("latent")
    rows = acts[0].shape[0]
    if count != 8:
        shares = call(decode_all_kernel, jax.ShapeDtypeStruct((count, rows, width), jnp.bfloat16))(*acts, own, sib)
        received = lax.all_to_all(shares, "latent", 0, 0, tiled=True)
        return jnp.sum(received.reshape(count // 2, 2 * rows, width).astype(jnp.float32), axis=0).astype(dtype)
    diag_same, diag_cross = decode_chip(3, acts, own, sib, width)
    for_y, for_x = to_peer(diag_same, 2), to_peer(diag_cross, 4)
    x_same, x_cross = decode_chip(1, acts, own, sib, width)
    y_same, y_cross = decode_chip(2, acts, own, sib, width)
    from_x_same, from_y_cross = to_peer(x_same, 2), to_peer(y_cross, 5)
    own_same, own_cross = decode_chip(0, acts, own, sib, width)
    from_sib = to_peer(own_cross, 1)
    from_y_same = to_peer(sum_two(y_same, for_y), 4)
    from_x_cross = to_peer(sum_two(x_cross, for_x), 3)
    return finish((own_same, from_x_same, from_y_same), (from_sib, from_x_cross, from_y_cross), dtype)


def shards(residual, encoder, enc_bias, gate_code, decoder):
    group_size = lax.axis_size("section") // LAYERS
    core = lax.axis_index("latent") % 2
    _, tok, width = residual.shape
    lat = encoder.shape[2]
    reach = decoder.shape[1]

    mine, other = token_halves(residual, group_size)
    threshold = 10000.0 * (gate_code[0].astype(jnp.float32) - 1.0)
    gates_own = jnp.stack([enc_bias[0], threshold])
    acts, dec_sib = gather_and_encode(mine, other, gates_own, encoder[0], decoder[0])
    sources = [acts, *other_layers(acts, reach, group_size)]
    out_type = jnp.bfloat16 if group_size == 1 else jnp.float32
    summed = decode_and_scatter(sources, decoder[0], dec_sib, width, out_type)
    rebuilt = group_reduce(summed, group_size).astype(jnp.bfloat16)

    kept, passed = acts[:, :lat], to_peer(acts[:, lat:], 1)
    latent_acts = jnp.where(core == 0, jnp.stack([kept, passed]), jnp.stack([passed, kept])).reshape(tok, lat)
    return (rebuilt[None], latent_acts[None])


def solution(mesh):
    return jax.shard_map(
        shards,
        mesh=mesh,
        in_specs=(
            P(None, None, "latent"),
            P("section", None, "latent"),
            P("section", "latent"),
            P("section", "latent"),
            P("section", None, "latent", None),
        ),
        out_specs=(P("section", None, "latent"), P("section", None, "latent")),
        check_vma=False,
    )
```

```python
import functools
import math

import jax
import jax.numpy as jnp
from jax import lax
from jax.experimental import pallas as pl
from jax.experimental.pallas import tpu as pltpu
from jax.sharding import PartitionSpec as P

LAYERS = 4
VMEM_LIMIT = 16 * 1024 * 1024
HALVES_LIMIT = VMEM_LIMIT


def swapped(shard, axis, stride):
    return lax.ppermute(shard, axis, [(i, i ^ 1 << stride) for i in range(lax.axis_size(axis))])


def after(value, *others):
    return lax.optimization_barrier((value, *others))[0]


def layer_offsets(reach):
    return sorted({layer ^ (layer - hop) for hop in range(1, reach) for layer in range(hop, LAYERS)})


def other_layers(value, reach, group_size):
    received = []
    for offset in layer_offsets(reach):
        wanted = {layer for layer in range(LAYERS) if 0 < layer - (layer ^ offset) < reach}
        pairs = [(index, index ^ offset * group_size) for index in range(lax.axis_size("section"))]
        pairs = [pair for pair in pairs if wanted & {end // group_size for end in pair}]
        received.append(lax.ppermute(value, "section", pairs))
    return received


def by_hop(acts, reach):
    layer = lax.axis_index("section") // (lax.axis_size("section") // LAYERS)
    own, *received = acts
    yield own[...]
    for hop in range(1, reach):
        source = jnp.zeros(own.shape, own.dtype)
        for offset, arrived in zip(layer_offsets(reach), received):
            for target in range(hop, LAYERS):
                if target ^ offset == target - hop:
                    source = jnp.where(layer == target, arrived[...], source)
        yield source


def group_reduce(partial_rows, group_size):
    current = partial_rows
    section_index = lax.axis_index("section")
    level_count = group_size.bit_length() - 1
    for level in reversed(range(level_count)):
        half = current.shape[0] // 2
        lower = current[:half]
        upper = current[half:]
        high_side = section_index // 2**level % 2 == 1
        kept = jnp.where(high_side, upper, lower)
        sent = jnp.where(high_side, lower, upper)
        received = swapped(sent.astype(jnp.bfloat16), "section", level).astype(sent.dtype)
        current = kept + received
    return current


def to_peer(value, offset):
    return lax.ppermute(value, "latent", [(i, i ^ offset) for i in range(lax.axis_size("latent"))])


def call(kernel, out_shape, in_specs=None, scratch=(), limit=VMEM_LIMIT, cost=None):
    specs = {} if in_specs is None else {"in_specs": in_specs}
    return pl.pallas_call(
        kernel,
        out_shape=out_shape,
        scratch_shapes=list(scratch),
        cost_estimate=cost,
        compiler_params=pltpu.CompilerParams(vmem_limit_bytes=limit),
        **specs,
    )


def halves_kernel(group_size, resid_ref, mine_ref, other_ref, sems):
    layer = lax.axis_index("section") // group_size
    core = lax.axis_index("latent") % 2
    copies = [
        pltpu.make_async_copy(resid_ref.at[layer, core], mine_ref, sems.at[0]),
        pltpu.make_async_copy(resid_ref.at[layer, 1 - core], other_ref, sems.at[1]),
    ]
    for copy in copies:
        copy.start()
    for copy in copies:
        copy.wait()


def token_halves(residual, group_size):
    layers, tok, width = residual.shape
    shape = jax.ShapeDtypeStruct((tok // 2, width), residual.dtype)
    return call(
        functools.partial(halves_kernel, group_size),
        (shape, shape),
        [pl.BlockSpec(memory_space=pltpu.HBM)],
        [pltpu.SemaphoreType.DMA((2,))],
        HALVES_LIMIT,
    )(residual.reshape(layers, 2, tok // 2, width))


def encoded(total, offsets, x_refs, own_ref, sib_ref):
    depth = x_refs[0].shape[1]
    place = lax.axis_index("latent")
    for offset, x_ref in zip(offsets, x_refs):
        rows = pl.ds(pl.multiple_of((place ^ offset) * depth, 16), depth)
        weights = jnp.concatenate([own_ref[rows, :], sib_ref[rows, :]], axis=1)
        part = jnp.dot(x_ref[...], weights, preferred_element_type=jnp.float32)
        total = part if total is None else total + part
    return total


def encode_near_kernel(offsets, *refs):
    *x_refs, own_ref, sib_ref, gates_ref, gates_sib_ref, out_ref, thr_ref = refs
    bias, thr = (jnp.concatenate([gates_ref[i:i + 1, :], gates_sib_ref[i:i + 1, :]], axis=1) for i in (0, 1))
    out_ref[...] = encoded(None, offsets, x_refs, own_ref, sib_ref) + bias
    thr_ref[...] = thr


def encode_near(pieces, own, sib, gates, gates_sib):
    rows, depth = next(iter(pieces.values())).shape
    shape = jax.ShapeDtypeStruct((rows, 2 * own.shape[1]), jnp.float32)
    cost = pl.CostEstimate(2 * len(pieces) * rows * depth * shape.shape[1], 4 * own.size, 0)
    thr = jax.ShapeDtypeStruct((1, shape.shape[1]), jnp.float32)
    kernel = functools.partial(encode_near_kernel, tuple(pieces))
    return call(kernel, (shape, thr), cost=cost)(*pieces.values(), own, sib, gates, gates_sib)


def encode_kernel(offsets, *refs):
    near_ref, thr_ref, *x_refs, own_ref, sib_ref, acts_ref = refs
    preact = encoded(near_ref[...], offsets, x_refs, own_ref, sib_ref)
    acts_ref[...] = jnp.where(preact > thr_ref[...], preact, 0.0).astype(jnp.bfloat16)


def encode(near, thr, pieces, own, sib):
    shape = jax.ShapeDtypeStruct(near.shape, jnp.bfloat16)
    return call(functools.partial(encode_kernel, tuple(pieces)), shape)(near, thr, *pieces.values(), own, sib)


def decoded(acts, own_ref, sib_ref, columns):
    total = None
    for hop, values in enumerate(by_hop(acts, own_ref.shape[0])):
        weights = jnp.concatenate([own_ref[hop, :, columns], sib_ref[hop, :, columns]], axis=0)
        part = jnp.dot(values, weights, preferred_element_type=jnp.float32)
        total = part if total is None else total + part
    return total


def decode_chip_kernel(chip_offset, *refs):
    *acts, own_ref, sib_ref, same_ref, cross_ref = refs
    width = same_ref.shape[1]
    place = lax.axis_index("latent")
    columns = pl.ds(pl.multiple_of(((place // 2) ^ chip_offset) * (2 * width), 128), 2 * width)
    total = decoded(acts, own_ref, sib_ref, columns).astype(jnp.bfloat16)
    low, high = total[:, :width], total[:, width:]
    first_core = place % 2 == 0
    same_ref[...] = jnp.where(first_core, low, high)
    cross_ref[...] = jnp.where(first_core, high, low)


def decode_chip(chip_offset, acts, own, sib, width):
    shape = jax.ShapeDtypeStruct((acts[0].shape[0], width), jnp.bfloat16)
    return call(functools.partial(decode_chip_kernel, chip_offset), (shape, shape))(*acts, own, sib)


def decode_all_kernel(*refs):
    *acts, own_ref, sib_ref, out_ref = refs
    count, _, width = out_ref.shape
    block = math.lcm(width, 128)
    per_block = block // width
    for step in range(count // per_block):
        total = decoded(acts, own_ref, sib_ref, slice(step * block, (step + 1) * block))
        for piece in range(per_block):
            out_ref[step * per_block + piece] = total[:, piece * width:(piece + 1) * width].astype(jnp.bfloat16)


def sum_two_kernel(a_ref, b_ref, out_ref):
    out_ref[...] = (a_ref[...].astype(jnp.float32) + b_ref[...].astype(jnp.float32)).astype(jnp.bfloat16)


def sum_two(a, b):
    return call(sum_two_kernel, jax.ShapeDtypeStruct(a.shape, jnp.bfloat16))(a, b)


def finish_kernel(*refs):
    *parts, out_ref = refs
    half = len(parts) // 2
    rows = parts[0].shape[0]
    core = lax.axis_index("latent") % 2
    for place, group in ((core, parts[:half]), (1 - core, parts[half:])):
        total = group[0][...].astype(jnp.float32)
        for part in group[1:]:
            total += part[...].astype(jnp.float32)
        out_ref[pl.ds(pl.multiple_of(place * rows, 16), rows), :] = total.astype(out_ref.dtype)


def finish(mine, other, dtype):
    rows, width = mine[0].shape
    return call(finish_kernel, jax.ShapeDtypeStruct((2 * rows, width), dtype))(*mine, *other)


def gather_and_encode(mine, other, gates, encoder, decoder):
    count = lax.axis_size("latent")
    if count != 8:
        core = lax.axis_index("latent") % 2
        pair = jnp.where(core == 0, jnp.stack([mine, other]), jnp.stack([other, mine]))
        outgoing = jnp.broadcast_to(pair, (count // 2, *pair.shape)).reshape(count, *mine.shape)
        everyone = lax.all_to_all(outgoing, "latent", 0, 0, tiled=True)
        place = lax.axis_index("latent")
        pieces = {i: lax.dynamic_index_in_dim(everyone, place ^ i, 0, keepdims=False) for i in range(count)}
        near, far = {i: pieces[i] for i in range(count // 2)}, {i: pieces[i] for i in range(count // 2, count)}
        enc_sib, gates_sib, dec_sib = (to_peer(value, 1) for value in (encoder, gates, decoder))
        near_sum, thr = encode_near(near, encoder, enc_sib, gates, gates_sib)
    else:
        near = {0: mine, 2: to_peer(mine, 2), 3: to_peer(other, 3), 4: to_peer(mine, 4), 5: to_peer(other, 5)}
        enc_sib = to_peer(encoder, 1)
        far = {6: to_peer(near[2], 4), 7: to_peer(near[5], 2)}
        near[1] = to_peer(after(other, enc_sib), 1)
        gates_sib = to_peer(after(gates, enc_sib), 1)
        near_sum, thr = encode_near(near, encoder, enc_sib, gates, gates_sib)
        dec_sib = to_peer(after(decoder, far[6], far[7], near_sum), 1)
    return encode(near_sum, thr, far, encoder, enc_sib), dec_sib


def decode_and_scatter(acts, own, sib, width, dtype):
    count = lax.axis_size("latent")
    rows = acts[0].shape[0]
    if count != 8:
        shares = call(decode_all_kernel, jax.ShapeDtypeStruct((count, rows, width), jnp.bfloat16))(*acts, own, sib)
        received = lax.all_to_all(shares, "latent", 0, 0, tiled=True)
        return jnp.sum(received.reshape(count // 2, 2 * rows, width).astype(jnp.float32), axis=0).astype(dtype)
    diag_same, diag_cross = decode_chip(3, acts, own, sib, width)
    for_y, for_x = to_peer(diag_same, 2), to_peer(diag_cross, 4)
    x_same, x_cross = decode_chip(1, acts, own, sib, width)
    y_same, y_cross = decode_chip(2, acts, own, sib, width)
    from_x_same, from_y_cross = to_peer(x_same, 2), to_peer(y_cross, 5)
    own_same, own_cross = decode_chip(0, acts, own, sib, width)
    from_sib = to_peer(own_cross, 1)
    from_y_same = to_peer(sum_two(y_same, for_y), 4)
    from_x_cross = to_peer(sum_two(x_cross, for_x), 3)
    return finish((own_same, from_x_same, from_y_same), (from_sib, from_x_cross, from_y_cross), dtype)


def shards(residual, encoder, enc_bias, gate_code, decoder):
    group_size = lax.axis_size("section") // LAYERS
    core = lax.axis_index("latent") % 2
    _, tok, width = residual.shape
    lat = encoder.shape[2]
    reach = decoder.shape[1]

    mine, other = token_halves(residual, group_size)
    threshold = 10000.0 * (gate_code[0].astype(jnp.float32) - 1.0)
    gates_own = jnp.stack([enc_bias[0], threshold])
    acts, dec_sib = gather_and_encode(mine, other, gates_own, encoder[0], decoder[0])
    sources = [acts, *other_layers(acts, reach, group_size)]
    out_type = jnp.bfloat16 if group_size == 1 else jnp.float32
    summed = decode_and_scatter(sources, decoder[0], dec_sib, width, out_type)
    rebuilt = group_reduce(summed, group_size).astype(jnp.bfloat16)

    kept, passed = acts[:, :lat], to_peer(acts[:, lat:], 1)
    latent_acts = jnp.where(core == 0, jnp.stack([kept, passed]), jnp.stack([passed, kept])).reshape(tok, lat)
    return (rebuilt[None], latent_acts[None])


def solution(mesh):
    return jax.shard_map(
        shards,
        mesh=mesh,
        in_specs=(
            P(None, None, "latent"),
            P("section", None, "latent"),
            P("section", "latent"),
            P("section", "latent"),
            P("section", None, "latent", None),
        ),
        out_specs=(P("section", None, "latent"), P("section", None, "latent")),
        check_vma=False,
    )
```

```python
import functools
import math

import jax
import jax.numpy as jnp
from jax import lax
from jax.experimental import pallas as pl
from jax.experimental.pallas import tpu as pltpu
from jax.sharding import PartitionSpec as P

LAYERS = 4
VMEM_LIMIT = 16 * 1024 * 1024
HALVES_LIMIT = 60 * 1024 * 1024


def swapped(shard, axis, stride):
    return lax.ppermute(shard, axis, [(i, i ^ 1 << stride) for i in range(lax.axis_size(axis))])


def after(value, *others):
    return lax.optimization_barrier((value, *others))[0]


def layer_offsets(reach):
    return sorted({layer ^ (layer - hop) for hop in range(1, reach) for layer in range(hop, LAYERS)})


def other_layers(value, reach, group_size):
    received = []
    for offset in layer_offsets(reach):
        wanted = {layer for layer in range(LAYERS) if 0 < layer - (layer ^ offset) < reach}
        pairs = [(index, index ^ offset * group_size) for index in range(lax.axis_size("section"))]
        pairs = [pair for pair in pairs if wanted & {end // group_size for end in pair}]
        received.append(lax.ppermute(value, "section", pairs))
    return received


def by_hop(acts, reach):
    layer = lax.axis_index("section") // (lax.axis_size("section") // LAYERS)
    own, *received = acts
    yield own[...]
    for hop in range(1, reach):
        source = jnp.zeros(own.shape, own.dtype)
        for offset, arrived in zip(layer_offsets(reach), received):
            for target in range(hop, LAYERS):
                if target ^ offset == target - hop:
                    source = jnp.where(layer == target, arrived[...], source)
        yield source


def group_reduce(partial_rows, group_size):
    current = partial_rows
    section_index = lax.axis_index("section")
    level_count = group_size.bit_length() - 1
    for level in reversed(range(level_count)):
        half = current.shape[0] // 2
        lower = current[:half]
        upper = current[half:]
        high_side = section_index // 2**level % 2 == 1
        kept = jnp.where(high_side, upper, lower)
        sent = jnp.where(high_side, lower, upper)
        received = swapped(sent.astype(jnp.bfloat16), "section", level).astype(sent.dtype)
        current = kept + received
    return current


def to_peer(value, offset):
    return lax.ppermute(value, "latent", [(i, i ^ offset) for i in range(lax.axis_size("latent"))])


def call(kernel, out_shape, in_specs=None, out_specs=None, scratch=(), limit=VMEM_LIMIT, cost=None):
    specs = {"in_specs": in_specs, "out_specs": out_specs}
    specs = {name: value for name, value in specs.items() if value is not None}
    return pl.pallas_call(
        kernel,
        out_shape=out_shape,
        scratch_shapes=list(scratch),
        cost_estimate=cost,
        compiler_params=pltpu.CompilerParams(vmem_limit_bytes=limit),
        **specs,
    )


def halves_kernel(group_size, resid_ref, mine_ref, other_ref, sems):
    layer = lax.axis_index("section") // group_size
    core = lax.axis_index("latent") % 2
    copies = [
        pltpu.make_async_copy(resid_ref.at[layer, core], mine_ref, sems.at[0]),
        pltpu.make_async_copy(resid_ref.at[layer, 1 - core], other_ref, sems.at[1]),
    ]
    for copy in copies:
        copy.start()
    for copy in copies:
        copy.wait()


def token_halves(residual, group_size):
    layers, tok, width = residual.shape
    shape = jax.ShapeDtypeStruct((tok // 2, width), residual.dtype)
    return call(
        functools.partial(halves_kernel, group_size),
        (shape, shape),
        [pl.BlockSpec(memory_space=pltpu.HBM)],
        (pl.BlockSpec(memory_space=pltpu.HBM),) * 2,
        [pltpu.SemaphoreType.DMA((2,))],
        HALVES_LIMIT,
    )(residual.reshape(layers, 2, tok // 2, width))


def encoded(total, offsets, x_refs, own_ref, sib_ref):
    depth = x_refs[0].shape[1]
    place = lax.axis_index("latent")
    for offset, x_ref in zip(offsets, x_refs):
        rows = pl.ds(pl.multiple_of((place ^ offset) * depth, 16), depth)
        weights = jnp.concatenate([own_ref[rows, :], sib_ref[rows, :]], axis=1)
        part = jnp.dot(x_ref[...], weights, preferred_element_type=jnp.float32)
        total = part if total is None else total + part
    return total


def encode_near_kernel(offsets, *refs):
    *x_refs, own_ref, sib_ref, gates_ref, gates_sib_ref, out_ref, thr_ref = refs
    bias, thr = (jnp.concatenate([gates_ref[i:i + 1, :], gates_sib_ref[i:i + 1, :]], axis=1) for i in (0, 1))
    out_ref[...] = encoded(None, offsets, x_refs, own_ref, sib_ref) + bias
    thr_ref[...] = thr


def encode_near(pieces, own, sib, gates, gates_sib):
    rows, depth = next(iter(pieces.values())).shape
    shape = jax.ShapeDtypeStruct((rows, 2 * own.shape[1]), jnp.float32)
    cost = pl.CostEstimate(2 * len(pieces) * rows * depth * shape.shape[1], 4 * own.size, 0)
    thr = jax.ShapeDtypeStruct((1, shape.shape[1]), jnp.float32)
    kernel = functools.partial(encode_near_kernel, tuple(pieces))
    return call(kernel, (shape, thr), cost=cost)(*pieces.values(), own, sib, gates, gates_sib)


def encode_kernel(offsets, *refs):
    near_ref, thr_ref, *x_refs, own_ref, sib_ref, acts_ref = refs
    preact = encoded(near_ref[...], offsets, x_refs, own_ref, sib_ref)
    acts_ref[...] = jnp.where(preact > thr_ref[...], preact, 0.0).astype(jnp.bfloat16)


def encode(near, thr, pieces, own, sib):
    shape = jax.ShapeDtypeStruct(near.shape, jnp.bfloat16)
    return call(functools.partial(encode_kernel, tuple(pieces)), shape)(near, thr, *pieces.values(), own, sib)


def decoded(acts, own_ref, sib_ref, columns):
    total = None
    for hop, values in enumerate(by_hop(acts, own_ref.shape[0])):
        weights = jnp.concatenate([own_ref[hop, :, columns], sib_ref[hop, :, columns]], axis=0)
        part = jnp.dot(values, weights, preferred_element_type=jnp.float32)
        total = part if total is None else total + part
    return total


def decode_chip_kernel(chip_offset, *refs):
    *acts, own_ref, sib_ref, same_ref, cross_ref = refs
    width = same_ref.shape[1]
    place = lax.axis_index("latent")
    columns = pl.ds(pl.multiple_of(((place // 2) ^ chip_offset) * (2 * width), 128), 2 * width)
    total = decoded(acts, own_ref, sib_ref, columns).astype(jnp.bfloat16)
    low, high = total[:, :width], total[:, width:]
    first_core = place % 2 == 0
    same_ref[...] = jnp.where(first_core, low, high)
    cross_ref[...] = jnp.where(first_core, high, low)


def decode_chip(chip_offset, acts, own, sib, width):
    shape = jax.ShapeDtypeStruct((acts[0].shape[0], width), jnp.bfloat16)
    return call(functools.partial(decode_chip_kernel, chip_offset), (shape, shape))(*acts, own, sib)


def decode_all_kernel(*refs):
    *acts, own_ref, sib_ref, out_ref = refs
    count, _, width = out_ref.shape
    block = math.lcm(width, 128)
    per_block = block // width
    for step in range(count // per_block):
        total = decoded(acts, own_ref, sib_ref, slice(step * block, (step + 1) * block))
        for piece in range(per_block):
            out_ref[step * per_block + piece] = total[:, piece * width:(piece + 1) * width].astype(jnp.bfloat16)


def sum_two_kernel(a_ref, b_ref, out_ref):
    out_ref[...] = (a_ref[...].astype(jnp.float32) + b_ref[...].astype(jnp.float32)).astype(jnp.bfloat16)


def sum_two(a, b):
    return call(sum_two_kernel, jax.ShapeDtypeStruct(a.shape, jnp.bfloat16))(a, b)


def finish_kernel(*refs):
    *parts, out_ref = refs
    half = len(parts) // 2
    rows = parts[0].shape[0]
    core = lax.axis_index("latent") % 2
    for place, group in ((core, parts[:half]), (1 - core, parts[half:])):
        total = group[0][...].astype(jnp.float32)
        for part in group[1:]:
            total += part[...].astype(jnp.float32)
        out_ref[pl.ds(pl.multiple_of(place * rows, 16), rows), :] = total.astype(out_ref.dtype)


def finish(mine, other, dtype):
    rows, width = mine[0].shape
    return call(finish_kernel, jax.ShapeDtypeStruct((2 * rows, width), dtype))(*mine, *other)


def gather_and_encode(mine, other, gates, encoder, decoder):
    count = lax.axis_size("latent")
    if count != 8:
        core = lax.axis_index("latent") % 2
        pair = jnp.where(core == 0, jnp.stack([mine, other]), jnp.stack([other, mine]))
        outgoing = jnp.broadcast_to(pair, (count // 2, *pair.shape)).reshape(count, *mine.shape)
        everyone = lax.all_to_all(outgoing, "latent", 0, 0, tiled=True)
        place = lax.axis_index("latent")
        pieces = {i: lax.dynamic_index_in_dim(everyone, place ^ i, 0, keepdims=False) for i in range(count)}
        near, far = {i: pieces[i] for i in range(count // 2)}, {i: pieces[i] for i in range(count // 2, count)}
        enc_sib, gates_sib, dec_sib = (to_peer(value, 1) for value in (encoder, gates, decoder))
        near_sum, thr = encode_near(near, encoder, enc_sib, gates, gates_sib)
    else:
        near = {0: mine, 2: to_peer(mine, 2), 3: to_peer(other, 3), 4: to_peer(mine, 4), 5: to_peer(other, 5)}
        enc_sib = to_peer(encoder, 1)
        far = {6: to_peer(near[2], 4), 7: to_peer(near[5], 2)}
        near[1] = to_peer(after(other, enc_sib), 1)
        gates_sib = to_peer(after(gates, enc_sib), 1)
        near_sum, thr = encode_near(near, encoder, enc_sib, gates, gates_sib)
        dec_sib = to_peer(after(decoder, far[6], far[7], near_sum), 1)
    return encode(near_sum, thr, far, encoder, enc_sib), dec_sib


def decode_and_scatter(acts, own, sib, width, dtype):
    count = lax.axis_size("latent")
    rows = acts[0].shape[0]
    if count != 8:
        shares = call(decode_all_kernel, jax.ShapeDtypeStruct((count, rows, width), jnp.bfloat16))(*acts, own, sib)
        received = lax.all_to_all(shares, "latent", 0, 0, tiled=True)
        return jnp.sum(received.reshape(count // 2, 2 * rows, width).astype(jnp.float32), axis=0).astype(dtype)
    diag_same, diag_cross = decode_chip(3, acts, own, sib, width)
    for_y, for_x = to_peer(diag_same, 2), to_peer(diag_cross, 4)
    x_same, x_cross = decode_chip(1, acts, own, sib, width)
    y_same, y_cross = decode_chip(2, acts, own, sib, width)
    from_x_same, from_y_cross = to_peer(x_same, 2), to_peer(y_cross, 5)
    own_same, own_cross = decode_chip(0, acts, own, sib, width)
    y_sum, x_sum = sum_two(y_same, for_y), sum_two(x_cross, for_x)
    from_y_same, from_x_cross = to_peer(y_sum, 4), to_peer(x_sum, 3)
    from_sib = to_peer(own_cross, 1)
    return finish((own_same, from_x_same, from_y_same), (from_sib, from_x_cross, from_y_cross), dtype)


def shards(residual, encoder, enc_bias, gate_code, decoder):
    group_size = lax.axis_size("section") // LAYERS
    core = lax.axis_index("latent") % 2
    _, tok, width = residual.shape
    lat = encoder.shape[2]
    reach = decoder.shape[1]

    mine, other = token_halves(residual, group_size)
    threshold = 10000.0 * (gate_code[0].astype(jnp.float32) - 1.0)
    gates_own = jnp.stack([enc_bias[0], threshold])
    acts, dec_sib = gather_and_encode(mine, other, gates_own, encoder[0], decoder[0])
    kept, passed = acts[:, :lat], to_peer(acts[:, lat:], 1)
    latent_acts = jnp.where(core == 0, jnp.stack([kept, passed]), jnp.stack([passed, kept])).reshape(tok, lat)

    received = other_layers(acts, reach, group_size)
    received[1] = after(received[1], passed)
    out_type = jnp.bfloat16 if group_size == 1 else jnp.float32
    summed = decode_and_scatter([acts, *received], decoder[0], dec_sib, width, out_type)
    rebuilt = group_reduce(summed, group_size).astype(jnp.bfloat16)
    return (rebuilt[None], latent_acts[None])


def solution(mesh):
    return jax.shard_map(
        shards,
        mesh=mesh,
        in_specs=(
            P(None, None, "latent"),
            P("section", None, "latent"),
            P("section", "latent"),
            P("section", "latent"),
            P("section", None, "latent", None),
        ),
        out_specs=(P("section", None, "latent"), P("section", None, "latent")),
        check_vma=False,
    )
```

```python
import functools
import math

import jax
import jax.numpy as jnp
from jax import lax
from jax.experimental import pallas as pl
from jax.experimental.pallas import tpu as pltpu
from jax.sharding import PartitionSpec as P

LAYERS = 4
VMEM_LIMIT = 16 * 1024 * 1024


def swapped(shard, axis, stride):
    return lax.ppermute(shard, axis, [(i, i ^ 1 << stride) for i in range(lax.axis_size(axis))])


def after(value, *others):
    return lax.optimization_barrier((value, *others))[0]


def layer_offsets(reach):
    return sorted({layer ^ (layer - hop) for hop in range(1, reach) for layer in range(hop, LAYERS)})


def other_layers(value, reach, group_size):
    received = []
    for offset in layer_offsets(reach):
        wanted = {layer for layer in range(LAYERS) if 0 < layer - (layer ^ offset) < reach}
        pairs = [(index, index ^ offset * group_size) for index in range(lax.axis_size("section"))]
        pairs = [pair for pair in pairs if wanted & {end // group_size for end in pair}]
        received.append(lax.ppermute(value, "section", pairs))
    return received


def by_hop(acts, reach):
    layer = lax.axis_index("section") // (lax.axis_size("section") // LAYERS)
    own, *received = acts
    yield own[...]
    for hop in range(1, reach):
        source = jnp.zeros(own.shape, own.dtype)
        for offset, arrived in zip(layer_offsets(reach), received):
            for target in range(hop, LAYERS):
                if target ^ offset == target - hop:
                    source = jnp.where(layer == target, arrived[...], source)
        yield source


def group_reduce(partial_rows, group_size):
    current = partial_rows
    section_index = lax.axis_index("section")
    level_count = group_size.bit_length() - 1
    for level in reversed(range(level_count)):
        half = current.shape[0] // 2
        lower = current[:half]
        upper = current[half:]
        high_side = section_index // 2**level % 2 == 1
        kept = jnp.where(high_side, upper, lower)
        sent = jnp.where(high_side, lower, upper)
        received = swapped(sent.astype(jnp.bfloat16), "section", level).astype(sent.dtype)
        current = kept + received
    return current


def to_peer(value, offset):
    return lax.ppermute(value, "latent", [(i, i ^ offset) for i in range(lax.axis_size("latent"))])


def call(kernel, out_shape, cost=None):
    return pl.pallas_call(
        kernel,
        out_shape=out_shape,
        cost_estimate=cost,
        compiler_params=pltpu.CompilerParams(vmem_limit_bytes=VMEM_LIMIT),
    )


def encode_near_kernel(offsets, far_offsets, *refs):
    *x_refs, own_ref, sib_ref, gates_ref, gates_sib_ref, out_ref, thr_ref, far_ref = refs
    depth = x_refs[0].shape[1]
    place = lax.axis_index("latent")

    def weights(offset):
        rows = pl.ds(pl.multiple_of((place ^ offset) * depth, 16), depth)
        return jnp.concatenate([own_ref[rows, :], sib_ref[rows, :]], axis=1)

    bias, thr = (jnp.concatenate([gates_ref[i:i + 1, :], gates_sib_ref[i:i + 1, :]], axis=1) for i in (0, 1))
    total = jnp.broadcast_to(bias, out_ref.shape)
    for offset, x_ref in zip(offsets, x_refs):
        total += jnp.dot(x_ref[...], weights(offset), preferred_element_type=jnp.float32)
    out_ref[...] = total
    thr_ref[...] = thr
    for index, offset in enumerate(far_offsets):
        far_ref[index] = weights(offset)


def encode_near(pieces, far_offsets, own, sib, gates, gates_sib):
    rows, depth = next(iter(pieces.values())).shape
    lat = 2 * own.shape[1]
    shapes = (
        jax.ShapeDtypeStruct((rows, lat), jnp.float32),
        jax.ShapeDtypeStruct((1, lat), jnp.float32),
        jax.ShapeDtypeStruct((len(far_offsets), depth, lat), own.dtype),
    )
    cost = pl.CostEstimate(2 * len(pieces) * rows * depth * lat, 4 * own.size, 0)
    kernel = functools.partial(encode_near_kernel, tuple(pieces), far_offsets)
    return call(kernel, shapes, cost=cost)(*pieces.values(), own, sib, gates, gates_sib)


def encode_kernel(near_ref, thr_ref, weights_ref, *refs):
    *x_refs, acts_ref = refs
    preact = near_ref[...]
    for index, x_ref in enumerate(x_refs):
        preact += jnp.dot(x_ref[...], weights_ref[index], preferred_element_type=jnp.float32)
    acts_ref[...] = jnp.where(preact > thr_ref[...], preact, 0.0).astype(jnp.bfloat16)


def encode(near, thr, weights, pieces):
    return call(encode_kernel, jax.ShapeDtypeStruct(near.shape, jnp.bfloat16))(near, thr, weights, *pieces)


def decoded(acts, own_ref, sib_ref, columns):
    total = None
    for hop, values in enumerate(by_hop(acts, own_ref.shape[0])):
        weights = jnp.concatenate([own_ref[hop, :, columns], sib_ref[hop, :, columns]], axis=0)
        part = jnp.dot(values, weights, preferred_element_type=jnp.float32)
        total = part if total is None else total + part
    return total


def decode_chip_kernel(chip_offset, *refs):
    *acts, own_ref, sib_ref, same_ref, cross_ref = refs
    width = same_ref.shape[1]
    place = lax.axis_index("latent")
    columns = pl.ds(pl.multiple_of(((place // 2) ^ chip_offset) * (2 * width), 128), 2 * width)
    total = decoded(acts, own_ref, sib_ref, columns).astype(jnp.bfloat16)
    low, high = total[:, :width], total[:, width:]
    first_core = place % 2 == 0
    same_ref[...] = jnp.where(first_core, low, high)
    cross_ref[...] = jnp.where(first_core, high, low)


def decode_chip(chip_offset, acts, own, sib, width):
    shape = jax.ShapeDtypeStruct((acts[0].shape[0], width), jnp.bfloat16)
    return call(functools.partial(decode_chip_kernel, chip_offset), (shape, shape))(*acts, own, sib)


def decode_all_kernel(*refs):
    *acts, own_ref, sib_ref, out_ref = refs
    count, _, width = out_ref.shape
    block = math.lcm(width, 128)
    per_block = block // width
    for step in range(count // per_block):
        total = decoded(acts, own_ref, sib_ref, slice(step * block, (step + 1) * block))
        for piece in range(per_block):
            out_ref[step * per_block + piece] = total[:, piece * width:(piece + 1) * width].astype(jnp.bfloat16)


def sum_two_kernel(a_ref, b_ref, out_ref):
    out_ref[...] = (a_ref[...].astype(jnp.float32) + b_ref[...].astype(jnp.float32)).astype(jnp.bfloat16)


def sum_two(a, b):
    return call(sum_two_kernel, jax.ShapeDtypeStruct(a.shape, jnp.bfloat16))(a, b)


def finish_kernel(*refs):
    *parts, out_ref = refs
    half = len(parts) // 2
    rows = parts[0].shape[0]
    core = lax.axis_index("latent") % 2
    for place, group in ((core, parts[:half]), (1 - core, parts[half:])):
        total = group[0][...].astype(jnp.float32)
        for part in group[1:]:
            total += part[...].astype(jnp.float32)
        out_ref[pl.ds(pl.multiple_of(place * rows, 16), rows), :] = total.astype(out_ref.dtype)


def finish(mine, other, dtype):
    rows, width = mine[0].shape
    return call(finish_kernel, jax.ShapeDtypeStruct((2 * rows, width), dtype))(*mine, *other)


def gather_and_encode(mine, other, gates, encoder, decoder):
    count = lax.axis_size("latent")
    if count != 8:
        core = lax.axis_index("latent") % 2
        pair = jnp.where(core == 0, jnp.stack([mine, other]), jnp.stack([other, mine]))
        outgoing = jnp.broadcast_to(pair, (count // 2, *pair.shape)).reshape(count, *mine.shape)
        everyone = lax.all_to_all(outgoing, "latent", 0, 0, tiled=True)
        place = lax.axis_index("latent")
        pieces = {i: lax.dynamic_index_in_dim(everyone, place ^ i, 0, keepdims=False) for i in range(count)}
        near, far = {i: pieces[i] for i in range(count // 2)}, {i: pieces[i] for i in range(count // 2, count)}
        enc_sib, gates_sib, dec_sib = (to_peer(value, 1) for value in (encoder, gates, decoder))
        near_sum, *rest = encode_near(near, tuple(far), encoder, enc_sib, gates, gates_sib)
    else:
        near = {0: mine, 2: to_peer(mine, 2), 3: to_peer(other, 3), 4: to_peer(mine, 4), 5: to_peer(other, 5)}
        enc_sib = to_peer(encoder, 1)
        far = {6: to_peer(near[2], 4), 7: to_peer(near[5], 2)}
        near[1] = to_peer(after(other, enc_sib), 1)
        gates_sib = to_peer(after(gates, enc_sib), 1)
        near_sum, *rest = encode_near(near, tuple(far), encoder, enc_sib, gates, gates_sib)
        dec_sib = to_peer(after(decoder, far[6], far[7], near_sum), 1)
    return encode(near_sum, *rest, far.values()), dec_sib


def decode_and_scatter(acts, own, sib, width, dtype):
    count = lax.axis_size("latent")
    rows = acts[0].shape[0]
    if count != 8:
        shares = call(decode_all_kernel, jax.ShapeDtypeStruct((count, rows, width), jnp.bfloat16))(*acts, own, sib)
        received = lax.all_to_all(shares, "latent", 0, 0, tiled=True)
        return jnp.sum(received.reshape(count // 2, 2 * rows, width).astype(jnp.float32), axis=0).astype(dtype)
    diag_same, diag_cross = decode_chip(3, acts, own, sib, width)
    for_y, for_x = to_peer(diag_same, 2), to_peer(diag_cross, 4)
    x_same, x_cross = decode_chip(1, acts, own, sib, width)
    y_same, y_cross = decode_chip(2, acts, own, sib, width)
    from_x_same, from_y_cross = to_peer(x_same, 2), to_peer(y_cross, 5)
    own_same, own_cross = decode_chip(0, acts, own, sib, width)
    y_sum, x_sum = sum_two(y_same, for_y), sum_two(x_cross, for_x)
    from_y_same, from_x_cross = to_peer(y_sum, 4), to_peer(x_sum, 3)
    from_sib = to_peer(own_cross, 1)
    return finish((own_same, from_x_same, from_y_same), (from_sib, from_x_cross, from_y_cross), dtype)


def shards(residual, encoder, enc_bias, gate_code, decoder):
    group_size = lax.axis_size("section") // LAYERS
    core = lax.axis_index("latent") % 2
    _, tok, width = residual.shape
    lat = encoder.shape[2]
    reach = decoder.shape[1]

    halves = residual.reshape(residual.shape[0] * 2, tok // 2, width)
    place = 2 * (lax.axis_index("section") // group_size)
    mine, other = (lax.dynamic_index_in_dim(halves, place + half, 0, keepdims=False) for half in (core, 1 - core))
    threshold = 10000.0 * (gate_code[0].astype(jnp.float32) - 1.0)
    gates_own = jnp.stack([enc_bias[0], threshold])
    acts, dec_sib = gather_and_encode(mine, other, gates_own, encoder[0], decoder[0])
    kept, passed = acts[:, :lat], to_peer(acts[:, lat:], 1)
    latent_acts = jnp.where(core == 0, jnp.stack([kept, passed]), jnp.stack([passed, kept])).reshape(tok, lat)

    received = other_layers(acts, reach, group_size)
    received[1] = after(received[1], passed)
    out_type = jnp.bfloat16 if group_size == 1 else jnp.float32
    summed = decode_and_scatter([acts, *received], decoder[0], dec_sib, width, out_type)
    rebuilt = group_reduce(summed, group_size).astype(jnp.bfloat16)
    return (rebuilt[None], latent_acts[None])


def solution(mesh):
    return jax.shard_map(
        shards,
        mesh=mesh,
        in_specs=(
            P(None, None, "latent"),
            P("section", None, "latent"),
            P("section", "latent"),
            P("section", "latent"),
            P("section", None, "latent", None),
        ),
        out_specs=(P("section", None, "latent"), P("section", None, "latent")),
        check_vma=False,
    )
```

```python
import functools
import math

import jax
import jax.numpy as jnp
from jax import lax
from jax.experimental import pallas as pl
from jax.experimental.pallas import tpu as pltpu
from jax.sharding import PartitionSpec as P

LAYERS = 4
VMEM_LIMIT = 16 * 1024 * 1024


def swapped(shard, axis, stride):
    return lax.ppermute(shard, axis, [(i, i ^ 1 << stride) for i in range(lax.axis_size(axis))])


def after(value, *others):
    return lax.optimization_barrier((value, *others))[0]


def layer_offsets(reach):
    return sorted({layer ^ (layer - hop) for hop in range(1, reach) for layer in range(hop, LAYERS)})


def other_layers(value, reach, group_size):
    received = []
    for offset in layer_offsets(reach):
        wanted = {layer for layer in range(LAYERS) if 0 < layer - (layer ^ offset) < reach}
        wanted |= {layer ^ offset for layer in wanted}
        pairs = [
            (index, index ^ offset * group_size if index // group_size in wanted else index)
            for index in range(lax.axis_size("section"))
        ]
        received.append(lax.ppermute(value, "section", pairs))
    return received


def by_hop(acts, reach):
    layer = lax.axis_index("section") // (lax.axis_size("section") // LAYERS)
    own, *received = acts
    yield own[...]
    for hop in range(1, reach):
        source = jnp.zeros(own.shape, own.dtype)
        for offset, arrived in zip(layer_offsets(reach), received):
            for target in range(hop, LAYERS):
                if target ^ offset == target - hop:
                    source = jnp.where(layer == target, arrived[...], source)
        yield source


def group_reduce(partial_rows, group_size):
    current = partial_rows
    section_index = lax.axis_index("section")
    level_count = group_size.bit_length() - 1
    for level in reversed(range(level_count)):
        half = current.shape[0] // 2
        lower = current[:half]
        upper = current[half:]
        high_side = section_index // 2**level % 2 == 1
        kept = jnp.where(high_side, upper, lower)
        sent = jnp.where(high_side, lower, upper)
        received = swapped(sent.astype(jnp.bfloat16), "section", level).astype(sent.dtype)
        current = kept + received
    return current


def to_peer(value, offset):
    return lax.ppermute(value, "latent", [(i, i ^ offset) for i in range(lax.axis_size("latent"))])


def call(kernel, out_shape, cost=None):
    return pl.pallas_call(
        kernel,
        out_shape=out_shape,
        cost_estimate=cost,
        compiler_params=pltpu.CompilerParams(vmem_limit_bytes=VMEM_LIMIT),
    )


def encode_near_kernel(offsets, far_offsets, *refs):
    *x_refs, own_ref, sib_ref, gates_ref, gates_sib_ref, out_ref, thr_ref, far_ref = refs
    depth = x_refs[0].shape[1]
    place = lax.axis_index("latent")

    def weights(offset):
        rows = pl.ds(pl.multiple_of((place ^ offset) * depth, 16), depth)
        return jnp.concatenate([own_ref[rows, :], sib_ref[rows, :]], axis=1)

    bias, thr = (jnp.concatenate([gates_ref[i:i + 1, :], gates_sib_ref[i:i + 1, :]], axis=1) for i in (0, 1))
    total = jnp.broadcast_to(bias, out_ref.shape)
    for offset, x_ref in zip(offsets, x_refs):
        total += jnp.dot(x_ref[...], weights(offset), preferred_element_type=jnp.float32)
    out_ref[...] = total
    thr_ref[...] = thr
    for index, offset in enumerate(far_offsets):
        far_ref[index] = weights(offset)


def encode_near(pieces, far_offsets, own, sib, gates, gates_sib):
    rows, depth = next(iter(pieces.values())).shape
    lat = 2 * own.shape[1]
    shapes = (
        jax.ShapeDtypeStruct((rows, lat), jnp.float32),
        jax.ShapeDtypeStruct((1, lat), jnp.float32),
        jax.ShapeDtypeStruct((len(far_offsets), depth, lat), own.dtype),
    )
    cost = pl.CostEstimate(2 * len(pieces) * rows * depth * lat, 4 * own.size, 0)
    kernel = functools.partial(encode_near_kernel, tuple(pieces), far_offsets)
    return call(kernel, shapes, cost=cost)(*pieces.values(), own, sib, gates, gates_sib)


def encode_kernel(near_ref, thr_ref, weights_ref, *refs):
    *x_refs, acts_ref = refs
    preact = near_ref[...]
    for index, x_ref in enumerate(x_refs):
        preact += jnp.dot(x_ref[...], weights_ref[index], preferred_element_type=jnp.float32)
    acts_ref[...] = jnp.where(preact > thr_ref[...], preact, 0.0).astype(jnp.bfloat16)


def encode(near, thr, weights, pieces):
    return call(encode_kernel, jax.ShapeDtypeStruct(near.shape, jnp.bfloat16))(near, thr, weights, *pieces)


def decoded(acts, own_ref, sib_ref, columns):
    total = None
    for hop, values in enumerate(by_hop(acts, own_ref.shape[0])):
        weights = jnp.concatenate([own_ref[hop, :, columns], sib_ref[hop, :, columns]], axis=0)
        part = jnp.dot(values, weights, preferred_element_type=jnp.float32)
        total = part if total is None else total + part
    return total


def decode_chip_kernel(chip_offset, *refs):
    *acts, own_ref, sib_ref, same_ref, cross_ref = refs
    width = same_ref.shape[1]
    place = lax.axis_index("latent")
    columns = pl.ds(pl.multiple_of(((place // 2) ^ chip_offset) * (2 * width), 128), 2 * width)
    total = decoded(acts, own_ref, sib_ref, columns).astype(jnp.bfloat16)
    low, high = total[:, :width], total[:, width:]
    first_core = place % 2 == 0
    same_ref[...] = jnp.where(first_core, low, high)
    cross_ref[...] = jnp.where(first_core, high, low)


def decode_chip(chip_offset, acts, own, sib, width):
    shape = jax.ShapeDtypeStruct((acts[0].shape[0], width), jnp.bfloat16)
    return call(functools.partial(decode_chip_kernel, chip_offset), (shape, shape))(*acts, own, sib)


def decode_all_kernel(*refs):
    *acts, own_ref, sib_ref, out_ref = refs
    count, _, width = out_ref.shape
    block = math.lcm(width, 128)
    per_block = block // width
    for step in range(count // per_block):
        total = decoded(acts, own_ref, sib_ref, slice(step * block, (step + 1) * block))
        for piece in range(per_block):
            out_ref[step * per_block + piece] = total[:, piece * width:(piece + 1) * width].astype(jnp.bfloat16)


def sum_two_kernel(a_ref, b_ref, out_ref):
    out_ref[...] = (a_ref[...].astype(jnp.float32) + b_ref[...].astype(jnp.float32)).astype(jnp.bfloat16)


def sum_two(a, b):
    return call(sum_two_kernel, jax.ShapeDtypeStruct(a.shape, jnp.bfloat16))(a, b)


def finish_kernel(*refs):
    *parts, out_ref = refs
    half = len(parts) // 2
    rows = parts[0].shape[0]
    core = lax.axis_index("latent") % 2
    for place, group in ((core, parts[:half]), (1 - core, parts[half:])):
        total = group[0][...].astype(jnp.float32)
        for part in group[1:]:
            total += part[...].astype(jnp.float32)
        out_ref[pl.ds(pl.multiple_of(place * rows, 16), rows), :] = total.astype(out_ref.dtype)


def finish(mine, other, dtype):
    rows, width = mine[0].shape
    return call(finish_kernel, jax.ShapeDtypeStruct((2 * rows, width), dtype))(*mine, *other)


def gather_and_encode(mine, other, gates, encoder, decoder):
    count = lax.axis_size("latent")
    if count != 8:
        core = lax.axis_index("latent") % 2
        pair = jnp.where(core == 0, jnp.stack([mine, other]), jnp.stack([other, mine]))
        outgoing = jnp.broadcast_to(pair, (count // 2, *pair.shape)).reshape(count, *mine.shape)
        everyone = lax.all_to_all(outgoing, "latent", 0, 0, tiled=True)
        place = lax.axis_index("latent")
        pieces = {i: lax.dynamic_index_in_dim(everyone, place ^ i, 0, keepdims=False) for i in range(count)}
        near, far = {i: pieces[i] for i in range(count // 2)}, {i: pieces[i] for i in range(count // 2, count)}
        enc_sib, gates_sib, dec_sib = (to_peer(value, 1) for value in (encoder, gates, decoder))
        near_sum, *rest = encode_near(near, tuple(far), encoder, enc_sib, gates, gates_sib)
    else:
        near = {0: mine, 2: to_peer(mine, 2), 3: to_peer(other, 3), 4: to_peer(mine, 4), 5: to_peer(other, 5)}
        enc_sib = to_peer(encoder, 1)
        far = {6: to_peer(near[2], 4), 7: to_peer(near[5], 2)}
        near[1] = to_peer(after(other, enc_sib), 1)
        gates_sib = to_peer(after(gates, enc_sib), 1)
        near_sum, *rest = encode_near(near, tuple(far), encoder, enc_sib, gates, gates_sib)
        dec_sib = to_peer(after(decoder, far[6], far[7], near_sum), 1)
    return encode(near_sum, *rest, far.values()), dec_sib


def decode_and_scatter(acts, own, sib, width, dtype):
    count = lax.axis_size("latent")
    rows = acts[0].shape[0]
    if count != 8:
        shares = call(decode_all_kernel, jax.ShapeDtypeStruct((count, rows, width), jnp.bfloat16))(*acts, own, sib)
        received = lax.all_to_all(shares, "latent", 0, 0, tiled=True)
        return jnp.sum(received.reshape(count // 2, 2 * rows, width).astype(jnp.float32), axis=0).astype(dtype)
    diag_same, diag_cross = decode_chip(3, acts, own, sib, width)
    for_y, for_x = to_peer(diag_same, 2), to_peer(diag_cross, 4)
    x_same, x_cross = decode_chip(1, acts, own, sib, width)
    y_same, y_cross = decode_chip(2, acts, own, sib, width)
    from_x_same, from_y_cross = to_peer(x_same, 2), to_peer(y_cross, 5)
    own_same, own_cross = decode_chip(0, acts, own, sib, width)
    y_sum, x_sum = sum_two(y_same, for_y), sum_two(x_cross, for_x)
    from_y_same, from_x_cross = to_peer(y_sum, 4), to_peer(x_sum, 3)
    from_sib = to_peer(own_cross, 1)
    return finish((own_same, from_x_same, from_y_same), (from_sib, from_x_cross, from_y_cross), dtype)


def shards(residual, encoder, enc_bias, gate_code, decoder):
    group_size = lax.axis_size("section") // LAYERS
    core = lax.axis_index("latent") % 2
    _, tok, width = residual.shape
    lat = encoder.shape[2]
    reach = decoder.shape[1]

    halves = residual.reshape(residual.shape[0] * 2, tok // 2, width)
    place = 2 * (lax.axis_index("section") // group_size)
    mine, other = (lax.dynamic_index_in_dim(halves, place + half, 0, keepdims=False) for half in (core, 1 - core))
    threshold = 10000.0 * (gate_code[0].astype(jnp.float32) - 1.0)
    gates_own = jnp.stack([enc_bias[0], threshold])
    acts, dec_sib = gather_and_encode(mine, other, gates_own, encoder[0], decoder[0])
    kept, passed = acts[:, :lat], to_peer(acts[:, lat:], 1)
    latent_acts = jnp.where(core == 0, jnp.stack([kept, passed]), jnp.stack([passed, kept])).reshape(tok, lat)

    received = other_layers(acts, reach, group_size)
    received[1] = after(received[1], passed)
    out_type = jnp.bfloat16 if group_size == 1 else jnp.float32
    summed = decode_and_scatter([acts, *received], decoder[0], dec_sib, width, out_type)
    rebuilt = group_reduce(summed, group_size).astype(jnp.bfloat16)
    return (rebuilt[None], latent_acts[None])


def solution(mesh):
    return jax.shard_map(
        shards,
        mesh=mesh,
        in_specs=(
            P(None, None, "latent"),
            P("section", None, "latent"),
            P("section", "latent"),
            P("section", "latent"),
            P("section", None, "latent", None),
        ),
        out_specs=(P("section", None, "latent"), P("section", None, "latent")),
        check_vma=False,
    )
```

```python
import functools
import math

import jax
import jax.numpy as jnp
from jax import lax
from jax.experimental import pallas as pl
from jax.experimental.pallas import tpu as pltpu
from jax.sharding import PartitionSpec as P

LAYERS = 4
VMEM_LIMIT = 16 * 1024 * 1024


def swapped(shard, axis, stride):
    return lax.ppermute(shard, axis, [(i, i ^ 1 << stride) for i in range(lax.axis_size(axis))])


def after(value, *others):
    return lax.optimization_barrier((value, *others))[0]


def traded(value, parity, group_size):
    def partner(layer):
        other = layer - 1 if layer % 2 == parity else layer + 1
        return other if 0 <= other < LAYERS else layer

    pairs = [(i, partner(i // group_size) * group_size + i % group_size) for i in range(lax.axis_size("section"))]
    return lax.ppermute(value, "section", pairs)


def earlier_layers(value, reach, group_size):
    received, even, odd = [], value, value
    for _ in range(1, reach):
        even, odd = traded(odd, 0, group_size), traded(even, 1, group_size)
        received += [even, odd]
    return received


def by_hop(acts, reach):
    layer = lax.axis_index("section") // (lax.axis_size("section") // LAYERS)
    own, *received = acts
    yield own[...]
    for hop in range(1, reach):
        even, odd = received[2 * hop - 2:2 * hop]
        source = jnp.where(layer % 2 == 0, even[...], odd[...])
        yield jnp.where(layer >= hop, source, jnp.zeros_like(source))


def group_reduce(partial_rows, group_size):
    current = partial_rows
    section_index = lax.axis_index("section")
    level_count = group_size.bit_length() - 1
    for level in reversed(range(level_count)):
        half = current.shape[0] // 2
        lower = current[:half]
        upper = current[half:]
        high_side = section_index // 2**level % 2 == 1
        kept = jnp.where(high_side, upper, lower)
        sent = jnp.where(high_side, lower, upper)
        received = swapped(sent.astype(jnp.bfloat16), "section", level).astype(sent.dtype)
        current = kept + received
    return current


def to_peer(value, offset):
    return lax.ppermute(value, "latent", [(i, i ^ offset) for i in range(lax.axis_size("latent"))])


def call(kernel, out_shape, cost=None):
    return pl.pallas_call(
        kernel,
        out_shape=out_shape,
        cost_estimate=cost,
        compiler_params=pltpu.CompilerParams(vmem_limit_bytes=VMEM_LIMIT),
    )


def encode_near_kernel(offsets, far_offsets, *refs):
    *x_refs, own_ref, sib_ref, gates_ref, gates_sib_ref, out_ref, thr_ref, far_ref = refs
    depth = x_refs[0].shape[1]
    place = lax.axis_index("latent")

    def weights(offset):
        rows = pl.ds(pl.multiple_of((place ^ offset) * depth, 16), depth)
        return jnp.concatenate([own_ref[rows, :], sib_ref[rows, :]], axis=1)

    bias, thr = (jnp.concatenate([gates_ref[i:i + 1, :], gates_sib_ref[i:i + 1, :]], axis=1) for i in (0, 1))
    total = jnp.broadcast_to(bias, out_ref.shape)
    for offset, x_ref in zip(offsets, x_refs):
        total += jnp.dot(x_ref[...], weights(offset), preferred_element_type=jnp.float32)
    out_ref[...] = total
    thr_ref[...] = thr
    for index, offset in enumerate(far_offsets):
        far_ref[index] = weights(offset)


def encode_near(pieces, far_offsets, own, sib, gates, gates_sib):
    rows, depth = next(iter(pieces.values())).shape
    lat = 2 * own.shape[1]
    shapes = (
        jax.ShapeDtypeStruct((rows, lat), jnp.float32),
        jax.ShapeDtypeStruct((1, lat), jnp.float32),
        jax.ShapeDtypeStruct((len(far_offsets), depth, lat), own.dtype),
    )
    cost = pl.CostEstimate(2 * len(pieces) * rows * depth * lat, 4 * own.size, 0)
    kernel = functools.partial(encode_near_kernel, tuple(pieces), far_offsets)
    return call(kernel, shapes, cost=cost)(*pieces.values(), own, sib, gates, gates_sib)


def encode_kernel(near_ref, thr_ref, weights_ref, *refs):
    *x_refs, acts_ref = refs
    preact = near_ref[...]
    for index, x_ref in enumerate(x_refs):
        preact += jnp.dot(x_ref[...], weights_ref[index], preferred_element_type=jnp.float32)
    acts_ref[...] = jnp.where(preact > thr_ref[...], preact, 0.0).astype(jnp.bfloat16)


def encode(near, thr, weights, pieces):
    return call(encode_kernel, jax.ShapeDtypeStruct(near.shape, jnp.bfloat16))(near, thr, weights, *pieces)


def decoded(acts, own_ref, sib_ref, columns):
    total = None
    for hop, values in enumerate(by_hop(acts, own_ref.shape[0])):
        weights = jnp.concatenate([own_ref[hop, :, columns], sib_ref[hop, :, columns]], axis=0)
        part = jnp.dot(values, weights, preferred_element_type=jnp.float32)
        total = part if total is None else total + part
    return total


def decode_chip_kernel(chip_offset, *refs):
    *acts, own_ref, sib_ref, same_ref, cross_ref = refs
    width = same_ref.shape[1]
    place = lax.axis_index("latent")
    columns = pl.ds(pl.multiple_of(((place // 2) ^ chip_offset) * (2 * width), 128), 2 * width)
    total = decoded(acts, own_ref, sib_ref, columns).astype(jnp.bfloat16)
    low, high = total[:, :width], total[:, width:]
    first_core = place % 2 == 0
    same_ref[...] = jnp.where(first_core, low, high)
    cross_ref[...] = jnp.where(first_core, high, low)


def decode_chip(chip_offset, acts, own, sib, width):
    shape = jax.ShapeDtypeStruct((acts[0].shape[0], width), jnp.bfloat16)
    return call(functools.partial(decode_chip_kernel, chip_offset), (shape, shape))(*acts, own, sib)


def decode_all_kernel(*refs):
    *acts, own_ref, sib_ref, out_ref = refs
    count, _, width = out_ref.shape
    block = math.lcm(width, 128)
    per_block = block // width
    for step in range(count // per_block):
        total = decoded(acts, own_ref, sib_ref, slice(step * block, (step + 1) * block))
        for piece in range(per_block):
            out_ref[step * per_block + piece] = total[:, piece * width:(piece + 1) * width].astype(jnp.bfloat16)


def sum_two_kernel(a_ref, b_ref, out_ref):
    out_ref[...] = (a_ref[...].astype(jnp.float32) + b_ref[...].astype(jnp.float32)).astype(jnp.bfloat16)


def sum_two(a, b):
    return call(sum_two_kernel, jax.ShapeDtypeStruct(a.shape, jnp.bfloat16))(a, b)


def finish_kernel(*refs):
    *parts, out_ref = refs
    half = len(parts) // 2
    rows = parts[0].shape[0]
    core = lax.axis_index("latent") % 2
    for place, group in ((core, parts[:half]), (1 - core, parts[half:])):
        total = group[0][...].astype(jnp.float32)
        for part in group[1:]:
            total += part[...].astype(jnp.float32)
        out_ref[pl.ds(pl.multiple_of(place * rows, 16), rows), :] = total.astype(out_ref.dtype)


def finish(mine, other, dtype):
    rows, width = mine[0].shape
    return call(finish_kernel, jax.ShapeDtypeStruct((2 * rows, width), dtype))(*mine, *other)


def gather_and_encode(mine, other, gates, encoder, decoder):
    count = lax.axis_size("latent")
    if count != 8:
        core = lax.axis_index("latent") % 2
        pair = jnp.where(core == 0, jnp.stack([mine, other]), jnp.stack([other, mine]))
        outgoing = jnp.broadcast_to(pair, (count // 2, *pair.shape)).reshape(count, *mine.shape)
        everyone = lax.all_to_all(outgoing, "latent", 0, 0, tiled=True)
        place = lax.axis_index("latent")
        pieces = {i: lax.dynamic_index_in_dim(everyone, place ^ i, 0, keepdims=False) for i in range(count)}
        near, far = {i: pieces[i] for i in range(count // 2)}, {i: pieces[i] for i in range(count // 2, count)}
        enc_sib, gates_sib, dec_sib = (to_peer(value, 1) for value in (encoder, gates, decoder))
        near_sum, *rest = encode_near(near, tuple(far), encoder, enc_sib, gates, gates_sib)
    else:
        near = {0: mine, 2: to_peer(mine, 2), 3: to_peer(other, 3), 4: to_peer(mine, 4), 5: to_peer(other, 5)}
        enc_sib = to_peer(encoder, 1)
        far = {6: to_peer(near[2], 4), 7: to_peer(near[5], 2)}
        near[1] = to_peer(after(other, enc_sib), 1)
        gates_sib = to_peer(after(gates, enc_sib), 1)
        near_sum, *rest = encode_near(near, tuple(far), encoder, enc_sib, gates, gates_sib)
        dec_sib = to_peer(after(decoder, far[6], far[7], near_sum), 1)
    return encode(near_sum, *rest, far.values()), dec_sib


def decode_and_scatter(acts, own, sib, width, dtype):
    count = lax.axis_size("latent")
    rows = acts[0].shape[0]
    if count != 8:
        shares = call(decode_all_kernel, jax.ShapeDtypeStruct((count, rows, width), jnp.bfloat16))(*acts, own, sib)
        received = lax.all_to_all(shares, "latent", 0, 0, tiled=True)
        return jnp.sum(received.reshape(count // 2, 2 * rows, width).astype(jnp.float32), axis=0).astype(dtype)
    diag_same, diag_cross = decode_chip(3, acts, own, sib, width)
    for_y, for_x = to_peer(diag_same, 2), to_peer(diag_cross, 4)
    x_same, x_cross = decode_chip(1, acts, own, sib, width)
    y_same, y_cross = decode_chip(2, acts, own, sib, width)
    from_x_same, from_y_cross = to_peer(x_same, 2), to_peer(y_cross, 5)
    own_same, own_cross = decode_chip(0, acts, own, sib, width)
    y_sum, x_sum = sum_two(y_same, for_y), sum_two(x_cross, for_x)
    from_y_same, from_x_cross = to_peer(y_sum, 4), to_peer(x_sum, 3)
    from_sib = to_peer(own_cross, 1)
    return finish((own_same, from_x_same, from_y_same), (from_sib, from_x_cross, from_y_cross), dtype)


def shards(residual, encoder, enc_bias, gate_code, decoder):
    group_size = lax.axis_size("section") // LAYERS
    core = lax.axis_index("latent") % 2
    _, tok, width = residual.shape
    lat = encoder.shape[2]
    reach = decoder.shape[1]

    halves = residual.reshape(residual.shape[0] * 2, tok // 2, width)
    place = 2 * (lax.axis_index("section") // group_size)
    mine, other = (lax.dynamic_index_in_dim(halves, place + half, 0, keepdims=False) for half in (core, 1 - core))
    threshold = 10000.0 * (gate_code[0].astype(jnp.float32) - 1.0)
    gates_own = jnp.stack([enc_bias[0], threshold])
    acts, dec_sib = gather_and_encode(mine, other, gates_own, encoder[0], decoder[0])
    kept, passed = acts[:, :lat], to_peer(acts[:, lat:], 1)
    latent_acts = jnp.where(core == 0, jnp.stack([kept, passed]), jnp.stack([passed, kept])).reshape(tok, lat)

    received = earlier_layers(acts, reach, group_size)
    received[-1] = after(received[-1], passed)
    out_type = jnp.bfloat16 if group_size == 1 else jnp.float32
    summed = decode_and_scatter([acts, *received], decoder[0], dec_sib, width, out_type)
    rebuilt = group_reduce(summed, group_size).astype(jnp.bfloat16)
    return (rebuilt[None], latent_acts[None])


def solution(mesh):
    return jax.shard_map(
        shards,
        mesh=mesh,
        in_specs=(
            P(None, None, "latent"),
            P("section", None, "latent"),
            P("section", "latent"),
            P("section", "latent"),
            P("section", None, "latent", None),
        ),
        out_specs=(P("section", None, "latent"), P("section", None, "latent")),
        check_vma=False,
    )
```

```python
import functools
import math

import jax
import jax.numpy as jnp
from jax import lax
from jax.experimental import pallas as pl
from jax.experimental.pallas import tpu as pltpu
from jax.sharding import PartitionSpec as P

LAYERS = 4
VMEM_LIMIT = 16 * 1024 * 1024


def swapped(shard, axis, stride):
    return lax.ppermute(shard, axis, [(i, i ^ 1 << stride) for i in range(lax.axis_size(axis))])


def after(value, *others):
    return lax.optimization_barrier((value, *others))[0]


def earlier_layers(value, reach, group_size):
    count = lax.axis_size("section")
    shifts = [hop * group_size for hop in range(1, reach)]
    return [lax.ppermute(value, "section", [(i, (i + shift) % count) for i in range(count)]) for shift in shifts]


def by_hop(acts, reach):
    layer = lax.axis_index("section") // (lax.axis_size("section") // LAYERS)
    for hop, values in enumerate(acts[:reach]):
        yield jnp.where(layer >= hop, values[...], jnp.zeros(values.shape, values.dtype)) if hop else values[...]


def group_reduce(partial_rows, group_size):
    current = partial_rows
    section_index = lax.axis_index("section")
    level_count = group_size.bit_length() - 1
    for level in reversed(range(level_count)):
        half = current.shape[0] // 2
        lower = current[:half]
        upper = current[half:]
        high_side = section_index // 2**level % 2 == 1
        kept = jnp.where(high_side, upper, lower)
        sent = jnp.where(high_side, lower, upper)
        received = swapped(sent.astype(jnp.bfloat16), "section", level).astype(sent.dtype)
        current = kept + received
    return current


def to_peer(value, offset):
    return lax.ppermute(value, "latent", [(i, i ^ offset) for i in range(lax.axis_size("latent"))])


def call(kernel, out_shape, cost=None):
    return pl.pallas_call(
        kernel,
        out_shape=out_shape,
        cost_estimate=cost,
        compiler_params=pltpu.CompilerParams(vmem_limit_bytes=VMEM_LIMIT),
    )


def encode_near_kernel(offsets, far_offsets, *refs):
    *x_refs, own_ref, sib_ref, gates_ref, gates_sib_ref, out_ref, thr_ref, far_ref = refs
    depth = x_refs[0].shape[1]
    place = lax.axis_index("latent")

    def weights(offset):
        rows = pl.ds(pl.multiple_of((place ^ offset) * depth, 16), depth)
        return jnp.concatenate([own_ref[rows, :], sib_ref[rows, :]], axis=1)

    bias, thr = (jnp.concatenate([gates_ref[i:i + 1, :], gates_sib_ref[i:i + 1, :]], axis=1) for i in (0, 1))
    total = jnp.broadcast_to(bias, out_ref.shape)
    for offset, x_ref in zip(offsets, x_refs):
        total += jnp.dot(x_ref[...], weights(offset), preferred_element_type=jnp.float32)
    out_ref[...] = total
    thr_ref[...] = thr
    for index, offset in enumerate(far_offsets):
        far_ref[index] = weights(offset)


def encode_near(pieces, far_offsets, own, sib, gates, gates_sib):
    rows, depth = next(iter(pieces.values())).shape
    lat = 2 * own.shape[1]
    shapes = (
        jax.ShapeDtypeStruct((rows, lat), jnp.float32),
        jax.ShapeDtypeStruct((1, lat), jnp.float32),
        jax.ShapeDtypeStruct((len(far_offsets), depth, lat), own.dtype),
    )
    cost = pl.CostEstimate(2 * len(pieces) * rows * depth * lat, 4 * own.size, 0)
    kernel = functools.partial(encode_near_kernel, tuple(pieces), far_offsets)
    return call(kernel, shapes, cost=cost)(*pieces.values(), own, sib, gates, gates_sib)


def encode_kernel(near_ref, thr_ref, weights_ref, *refs):
    *x_refs, acts_ref = refs
    preact = near_ref[...]
    for index, x_ref in enumerate(x_refs):
        preact += jnp.dot(x_ref[...], weights_ref[index], preferred_element_type=jnp.float32)
    acts_ref[...] = jnp.where(preact > thr_ref[...], preact, 0.0).astype(jnp.bfloat16)


def encode(near, thr, weights, pieces):
    return call(encode_kernel, jax.ShapeDtypeStruct(near.shape, jnp.bfloat16))(near, thr, weights, *pieces)


def decoded(acts, own_ref, sib_ref, columns):
    total = None
    for hop, values in enumerate(by_hop(acts, own_ref.shape[0])):
        weights = jnp.concatenate([own_ref[hop, :, columns], sib_ref[hop, :, columns]], axis=0)
        part = jnp.dot(values, weights, preferred_element_type=jnp.float32)
        total = part if total is None else total + part
    return total


def decode_chip_kernel(chip_offset, *refs):
    *acts, own_ref, sib_ref, same_ref, cross_ref = refs
    width = same_ref.shape[1]
    place = lax.axis_index("latent")
    columns = pl.ds(pl.multiple_of(((place // 2) ^ chip_offset) * (2 * width), 128), 2 * width)
    total = decoded(acts, own_ref, sib_ref, columns).astype(jnp.bfloat16)
    low, high = total[:, :width], total[:, width:]
    first_core = place % 2 == 0
    same_ref[...] = jnp.where(first_core, low, high)
    cross_ref[...] = jnp.where(first_core, high, low)


def decode_chip(chip_offset, acts, own, sib, width):
    shape = jax.ShapeDtypeStruct((acts[0].shape[0], width), jnp.bfloat16)
    return call(functools.partial(decode_chip_kernel, chip_offset), (shape, shape))(*acts, own, sib)


def decode_all_kernel(*refs):
    *acts, own_ref, sib_ref, out_ref = refs
    count, _, width = out_ref.shape
    block = math.lcm(width, 128)
    per_block = block // width
    for step in range(count // per_block):
        total = decoded(acts, own_ref, sib_ref, slice(step * block, (step + 1) * block))
        for piece in range(per_block):
            out_ref[step * per_block + piece] = total[:, piece * width:(piece + 1) * width].astype(jnp.bfloat16)


def sum_two_kernel(a_ref, b_ref, out_ref):
    out_ref[...] = (a_ref[...].astype(jnp.float32) + b_ref[...].astype(jnp.float32)).astype(jnp.bfloat16)


def sum_two(a, b):
    return call(sum_two_kernel, jax.ShapeDtypeStruct(a.shape, jnp.bfloat16))(a, b)


def finish_kernel(*refs):
    *parts, out_ref, sums, sems = refs
    half = len(parts) // 2
    rows = parts[0].shape[0]
    core = lax.axis_index("latent") % 2
    copies = []
    for index, (place, group) in enumerate(((core, parts[:half]), (1 - core, parts[half:]))):
        total = group[0][...].astype(jnp.float32)
        for part in group[1:]:
            total += part[...].astype(jnp.float32)
        sums[index] = total.astype(out_ref.dtype)
        target = out_ref.at[pl.ds(pl.multiple_of(place * rows, 16), rows), :]
        copies.append(pltpu.make_async_copy(sums.at[index], target, sems.at[index]))
        copies[-1].start()
    for copy in copies:
        copy.wait()


def finish(mine, other, dtype):
    rows, width = mine[0].shape
    return pl.pallas_call(
        finish_kernel,
        out_shape=jax.ShapeDtypeStruct((2 * rows, width), dtype),
        out_specs=pl.BlockSpec(memory_space=pl.ANY),
        scratch_shapes=[pltpu.VMEM((2, rows, width), dtype), pltpu.SemaphoreType.DMA((2,))],
        compiler_params=pltpu.CompilerParams(vmem_limit_bytes=VMEM_LIMIT),
    )(*mine, *other)


def gather_and_encode(mine, other, gates, encoder, decoder):
    count = lax.axis_size("latent")
    if count != 8:
        core = lax.axis_index("latent") % 2
        pair = jnp.where(core == 0, jnp.stack([mine, other]), jnp.stack([other, mine]))
        outgoing = jnp.broadcast_to(pair, (count // 2, *pair.shape)).reshape(count, *mine.shape)
        everyone = lax.all_to_all(outgoing, "latent", 0, 0, tiled=True)
        place = lax.axis_index("latent")
        pieces = {i: lax.dynamic_index_in_dim(everyone, place ^ i, 0, keepdims=False) for i in range(count)}
        near, far = {i: pieces[i] for i in range(count // 2)}, {i: pieces[i] for i in range(count // 2, count)}
        enc_sib, gates_sib, dec_sib = (to_peer(value, 1) for value in (encoder, gates, decoder))
        near_sum, *rest = encode_near(near, tuple(far), encoder, enc_sib, gates, gates_sib)
    else:
        near = {0: mine, 2: to_peer(mine, 2), 3: to_peer(other, 3), 4: to_peer(mine, 4), 5: to_peer(other, 5)}
        enc_sib = to_peer(encoder, 1)
        far = {6: to_peer(near[2], 4), 7: to_peer(near[5], 2)}
        near[1] = to_peer(after(other, enc_sib), 1)
        gates_sib = to_peer(after(gates, enc_sib), 1)
        near_sum, *rest = encode_near(near, tuple(far), encoder, enc_sib, gates, gates_sib)
        dec_sib = to_peer(after(decoder, far[6], far[7], near_sum), 1)
    return encode(near_sum, *rest, far.values()), dec_sib


def decode_and_scatter(acts, own, sib, width, dtype):
    count = lax.axis_size("latent")
    rows = acts[0].shape[0]
    if count != 8:
        shares = call(decode_all_kernel, jax.ShapeDtypeStruct((count, rows, width), jnp.bfloat16))(*acts, own, sib)
        received = lax.all_to_all(shares, "latent", 0, 0, tiled=True)
        return jnp.sum(received.reshape(count // 2, 2 * rows, width).astype(jnp.float32), axis=0).astype(dtype)
    diag_same, diag_cross = decode_chip(3, acts, own, sib, width)
    for_y, for_x = to_peer(diag_same, 2), to_peer(diag_cross, 4)
    x_same, x_cross = decode_chip(1, acts, own, sib, width)
    y_same, y_cross = decode_chip(2, acts, own, sib, width)
    from_x_same, from_y_cross = to_peer(x_same, 2), to_peer(y_cross, 5)
    own_same, own_cross = decode_chip(0, acts, own, sib, width)
    y_sum, x_sum = sum_two(y_same, for_y), sum_two(x_cross, for_x)
    from_y_same, from_x_cross = to_peer(y_sum, 4), to_peer(x_sum, 3)
    from_sib = to_peer(own_cross, 1)
    return finish((own_same, from_x_same, from_y_same), (from_sib, from_x_cross, from_y_cross), dtype)


def shards(residual, encoder, enc_bias, gate_code, decoder):
    group_size = lax.axis_size("section") // LAYERS
    core = lax.axis_index("latent") % 2
    _, tok, width = residual.shape
    lat = encoder.shape[2]
    reach = decoder.shape[1]

    halves = residual.reshape(residual.shape[0] * 2, tok // 2, width)
    place = 2 * (lax.axis_index("section") // group_size)
    mine, other = (lax.dynamic_index_in_dim(halves, place + half, 0, keepdims=False) for half in (core, 1 - core))
    threshold = 10000.0 * (gate_code[0].astype(jnp.float32) - 1.0)
    gates_own = jnp.stack([enc_bias[0], threshold])
    acts, dec_sib = gather_and_encode(mine, other, gates_own, encoder[0], decoder[0])
    kept, passed = acts[:, :lat], to_peer(acts[:, lat:], 1)
    latent_acts = jnp.where(core == 0, jnp.stack([kept, passed]), jnp.stack([passed, kept])).reshape(tok, lat)

    received = earlier_layers(acts, reach, group_size)
    received[-1] = after(received[-1], passed)
    out_type = jnp.bfloat16 if group_size == 1 else jnp.float32
    summed = decode_and_scatter([acts, *received], decoder[0], dec_sib, width, out_type)
    rebuilt = group_reduce(summed, group_size).astype(jnp.bfloat16)
    return (rebuilt[None], latent_acts[None])


def solution(mesh):
    return jax.shard_map(
        shards,
        mesh=mesh,
        in_specs=(
            P(None, None, "latent"),
            P("section", None, "latent"),
            P("section", "latent"),
            P("section", "latent"),
            P("section", None, "latent", None),
        ),
        out_specs=(P("section", None, "latent"), P("section", None, "latent")),
        check_vma=False,
    )
```

```python
import functools
import math

import jax
import jax.numpy as jnp
from jax import lax
from jax.experimental import pallas as pl
from jax.experimental.pallas import tpu as pltpu
from jax.sharding import PartitionSpec as P

LAYERS = 4
CHUNKS = (96, 64)
VMEM_LIMIT = 16 * 1024 * 1024


def swapped(shard, axis, stride):
    return lax.ppermute(shard, axis, [(i, i ^ 1 << stride) for i in range(lax.axis_size(axis))])


def after(value, *others):
    return lax.optimization_barrier((value, *others))[0]


def earlier_layers(value, reach, group_size):
    count = lax.axis_size("section")
    shifts = [hop * group_size for hop in range(1, reach)]
    return [lax.ppermute(value, "section", [(i, (i + shift) % count) for i in range(count)]) for shift in shifts]


def by_hop(acts, reach):
    layer = lax.axis_index("section") // (lax.axis_size("section") // LAYERS)
    for hop, values in enumerate(acts[:reach]):
        yield jnp.where(layer >= hop, values[...], jnp.zeros(values.shape, values.dtype)) if hop else values[...]


def group_reduce(partial_rows, group_size):
    current = partial_rows
    section_index = lax.axis_index("section")
    level_count = group_size.bit_length() - 1
    for level in reversed(range(level_count)):
        half = current.shape[0] // 2
        lower = current[:half]
        upper = current[half:]
        high_side = section_index // 2**level % 2 == 1
        kept = jnp.where(high_side, upper, lower)
        sent = jnp.where(high_side, lower, upper)
        received = swapped(sent.astype(jnp.bfloat16), "section", level).astype(sent.dtype)
        current = kept + received
    return current


def to_peer(value, offset):
    return lax.ppermute(value, "latent", [(i, i ^ offset) for i in range(lax.axis_size("latent"))])


def call(kernel, out_shape, cost=None):
    return pl.pallas_call(
        kernel,
        out_shape=out_shape,
        cost_estimate=cost,
        compiler_params=pltpu.CompilerParams(vmem_limit_bytes=VMEM_LIMIT),
    )


def encode_near_kernel(offsets, far_offsets, *refs):
    x_refs = refs[:len(offsets)]
    own_ref, sib_ref, gates_ref, gates_sib_ref, *out_refs, thr_ref, far_ref = refs[len(offsets):]
    depth = x_refs[0].shape[1]
    place = lax.axis_index("latent")

    def weights(offset):
        rows = pl.ds(pl.multiple_of((place ^ offset) * depth, 16), depth)
        return jnp.concatenate([own_ref[rows, :], sib_ref[rows, :]], axis=1)

    bias, thr = (jnp.concatenate([gates_ref[i:i + 1, :], gates_sib_ref[i:i + 1, :]], axis=1) for i in (0, 1))
    total = bias
    for offset, x_ref in zip(offsets, x_refs):
        total = total + jnp.dot(x_ref[...], weights(offset), preferred_element_type=jnp.float32)
    first = 0
    for out_ref in out_refs:
        out_ref[...] = total[first:first + out_ref.shape[0]]
        first += out_ref.shape[0]
    thr_ref[...] = thr
    for index, offset in enumerate(far_offsets):
        far_ref[index] = weights(offset)


def encode_near(pieces, far_offsets, chunks, own, sib, gates, gates_sib):
    rows, depth = next(iter(pieces.values())).shape
    lat = 2 * own.shape[1]
    shapes = [jax.ShapeDtypeStruct((chunk, lat), jnp.float32) for chunk in chunks] + [
        jax.ShapeDtypeStruct((1, lat), jnp.float32),
        jax.ShapeDtypeStruct((len(far_offsets), depth, lat), own.dtype),
    ]
    cost = pl.CostEstimate(2 * len(pieces) * rows * depth * lat, 4 * own.size, 0)
    kernel = functools.partial(encode_near_kernel, tuple(pieces), far_offsets)
    *sums, thr, weights = call(kernel, shapes, cost=cost)(*pieces.values(), own, sib, gates, gates_sib)
    return sums, thr, weights


def encode_kernel(near_ref, thr_ref, weights_ref, *refs):
    *x_refs, acts_ref = refs
    preact = near_ref[...]
    for index, x_ref in enumerate(x_refs):
        preact += jnp.dot(x_ref[...], weights_ref[index], preferred_element_type=jnp.float32)
    acts_ref[...] = jnp.where(preact > thr_ref[...], preact, 0.0).astype(jnp.bfloat16)


def encode(near, thr, weights, pieces):
    cost = pl.CostEstimate(2 * near.shape[0] * weights.size, 2 * weights.size, 0)
    return call(encode_kernel, jax.ShapeDtypeStruct(near.shape, jnp.bfloat16), cost)(near, thr, weights, *pieces)


def split_kernel(whole_ref, *out_refs):
    first = 0
    for out_ref in out_refs:
        out_ref[...] = whole_ref[first:first + out_ref.shape[0], :]
        first += out_ref.shape[0]


def split(whole, chunks):
    if len(chunks) == 1:
        return [whole]
    return call(split_kernel, [jax.ShapeDtypeStruct((rows, whole.shape[1]), whole.dtype) for rows in chunks])(whole)


def decoded(acts, own_ref, sib_ref, columns):
    total = None
    reach = own_ref.shape[0]
    chunks = [by_hop(acts[first:first + reach], reach) for first in range(0, len(acts), reach)]
    for hop, values in enumerate(zip(*chunks)):
        weights = jnp.concatenate([own_ref[hop, :, columns], sib_ref[hop, :, columns]], axis=0)
        part = jnp.dot(jnp.concatenate(values, axis=0), weights, preferred_element_type=jnp.float32)
        total = part if total is None else total + part
    return total


def decode_chip_kernel(chip_offset, *refs):
    *acts, own_ref, sib_ref, same_ref, cross_ref = refs
    width = same_ref.shape[1]
    place = lax.axis_index("latent")
    columns = pl.ds(pl.multiple_of(((place // 2) ^ chip_offset) * (2 * width), 128), 2 * width)
    total = decoded(acts, own_ref, sib_ref, columns).astype(jnp.bfloat16)
    low, high = total[:, :width], total[:, width:]
    first_core = place % 2 == 0
    same_ref[...] = jnp.where(first_core, low, high)
    cross_ref[...] = jnp.where(first_core, high, low)


def decode_chip(chip_offset, acts, own, sib, width):
    rows = sum(chunk.shape[0] for chunk in acts[::own.shape[0]])
    shape = jax.ShapeDtypeStruct((rows, width), jnp.bfloat16)
    return call(functools.partial(decode_chip_kernel, chip_offset), (shape, shape))(*acts, own, sib)


def decode_all_kernel(*refs):
    *acts, own_ref, sib_ref, out_ref = refs
    count, _, width = out_ref.shape
    block = math.lcm(width, 128)
    per_block = block // width
    for step in range(count // per_block):
        total = decoded(acts, own_ref, sib_ref, slice(step * block, (step + 1) * block))
        for piece in range(per_block):
            out_ref[step * per_block + piece] = total[:, piece * width:(piece + 1) * width].astype(jnp.bfloat16)


def sum_two_kernel(a_ref, b_ref, out_ref):
    out_ref[...] = (a_ref[...].astype(jnp.float32) + b_ref[...].astype(jnp.float32)).astype(jnp.bfloat16)


def sum_two(a, b):
    return call(sum_two_kernel, jax.ShapeDtypeStruct(a.shape, jnp.bfloat16))(a, b)


def finish_kernel(*refs):
    *parts, out_ref, sums, sems = refs
    half = len(parts) // 2
    rows = parts[0].shape[0]
    core = lax.axis_index("latent") % 2
    copies = []
    for index, (place, group) in enumerate(((core, parts[:half]), (1 - core, parts[half:]))):
        total = group[0][...].astype(jnp.float32)
        for part in group[1:]:
            total += part[...].astype(jnp.float32)
        sums[index] = total.astype(out_ref.dtype)
        target = out_ref.at[pl.ds(pl.multiple_of(place * rows, 16), rows), :]
        copies.append(pltpu.make_async_copy(sums.at[index], target, sems.at[index]))
        copies[-1].start()
    for copy in copies:
        copy.wait()


def finish(mine, other, dtype):
    rows, width = mine[0].shape
    return pl.pallas_call(
        finish_kernel,
        out_shape=jax.ShapeDtypeStruct((2 * rows, width), dtype),
        out_specs=pl.BlockSpec(memory_space=pl.ANY),
        scratch_shapes=[pltpu.VMEM((2, rows, width), dtype), pltpu.SemaphoreType.DMA((2,))],
        compiler_params=pltpu.CompilerParams(vmem_limit_bytes=VMEM_LIMIT),
    )(*mine, *other)


def gather_and_encode(mine, other, gates, encoder, decoder):
    rows = mine.shape[0]
    count = lax.axis_size("latent")
    if count != 8:
        core = lax.axis_index("latent") % 2
        pair = jnp.where(core == 0, jnp.stack([mine, other]), jnp.stack([other, mine]))
        outgoing = jnp.broadcast_to(pair, (count // 2, *pair.shape)).reshape(count, *mine.shape)
        everyone = lax.all_to_all(outgoing, "latent", 0, 0, tiled=True)
        place = lax.axis_index("latent")
        pieces = {i: lax.dynamic_index_in_dim(everyone, place ^ i, 0, keepdims=False) for i in range(count)}
        chunks = (rows,)
        near, far = {i: pieces[i] for i in range(count // 2)}, {i: [pieces[i]] for i in range(count // 2, count)}
        enc_sib, gates_sib, dec_sib = (to_peer(value, 1) for value in (encoder, gates, decoder))
    else:
        chunks = CHUNKS
        near = {0: mine, 1: to_peer(other, 1), 2: to_peer(mine, 2), 5: to_peer(other, 5)}
        enc_sib, dec_sib = to_peer(encoder, 1), to_peer(decoder, 1)
        near[3], near[4] = to_peer(after(other, near[1]), 3), to_peer(after(mine, enc_sib), 4)
        far = {}
        for place, value, offset in ((6, near[2], 4), (7, near[5], 2)):
            first, *later = split(value, chunks)
            later = [after(part, near[3], near[4]) for part in later]
            far[place] = [to_peer(part, offset) for part in (first, *later)]
        gates_sib = after(to_peer(after(gates, near[2]), 1), dec_sib)
    sums, thr, weights = encode_near(near, tuple(far), chunks, encoder, enc_sib, gates, gates_sib)
    return [encode(part, thr, weights, far_parts) for part, *far_parts in zip(sums, *far.values())], dec_sib


def decode_and_scatter(acts, own, sib, width, dtype):
    count = lax.axis_size("latent")
    rows = acts[0].shape[0]
    if count != 8:
        shares = call(decode_all_kernel, jax.ShapeDtypeStruct((count, rows, width), jnp.bfloat16))(*acts, own, sib)
        received = lax.all_to_all(shares, "latent", 0, 0, tiled=True)
        return jnp.sum(received.reshape(count // 2, 2 * rows, width).astype(jnp.float32), axis=0).astype(dtype)
    diag_same, diag_cross = decode_chip(3, acts, own, sib, width)
    for_y, for_x = to_peer(diag_same, 2), to_peer(diag_cross, 4)
    x_same, x_cross = decode_chip(1, acts, own, sib, width)
    y_same, y_cross = decode_chip(2, acts, own, sib, width)
    from_x_same, from_y_cross = to_peer(x_same, 2), to_peer(y_cross, 5)
    own_same, own_cross = decode_chip(0, acts, own, sib, width)
    y_sum, x_sum = sum_two(y_same, for_y), sum_two(x_cross, for_x)
    from_y_same, from_x_cross = to_peer(y_sum, 4), to_peer(x_sum, 3)
    from_sib = to_peer(own_cross, 1)
    return finish((own_same, from_x_same, from_y_same), (from_sib, from_x_cross, from_y_cross), dtype)


def shards(residual, encoder, enc_bias, gate_code, decoder):
    group_size = lax.axis_size("section") // LAYERS
    core = lax.axis_index("latent") % 2
    _, tok, width = residual.shape
    lat = encoder.shape[2]
    reach = decoder.shape[1]

    halves = residual.reshape(residual.shape[0] * 2, tok // 2, width)
    place = 2 * (lax.axis_index("section") // group_size)
    mine, other = (lax.dynamic_index_in_dim(halves, place + half, 0, keepdims=False) for half in (core, 1 - core))
    threshold = 10000.0 * (gate_code[0].astype(jnp.float32) - 1.0)
    gates_own = jnp.stack([enc_bias[0], threshold])
    acts, dec_sib = gather_and_encode(mine, other, gates_own, encoder[0], decoder[0])
    whole = jnp.concatenate(acts, axis=0)
    kept, passed = whole[:, :lat], to_peer(whole[:, lat:], 1)
    latent_acts = jnp.where(core == 0, jnp.stack([kept, passed]), jnp.stack([passed, kept])).reshape(tok, lat)

    sources = [value for chunk in acts for value in (chunk, *earlier_layers(chunk, reach, group_size))]
    sources[-1] = after(sources[-1], passed)
    out_type = jnp.bfloat16 if group_size == 1 else jnp.float32
    summed = decode_and_scatter(sources, decoder[0], dec_sib, width, out_type)
    rebuilt = group_reduce(summed, group_size).astype(jnp.bfloat16)
    return (rebuilt[None], latent_acts[None])


def solution(mesh):
    return jax.shard_map(
        shards,
        mesh=mesh,
        in_specs=(
            P(None, None, "latent"),
            P("section", None, "latent"),
            P("section", "latent"),
            P("section", "latent"),
            P("section", None, "latent", None),
        ),
        out_specs=(P("section", None, "latent"), P("section", None, "latent")),
        check_vma=False,
    )
```

```python
import functools
import math

import jax
import jax.numpy as jnp
from jax import lax
from jax.experimental import pallas as pl
from jax.experimental.pallas import tpu as pltpu
from jax.sharding import PartitionSpec as P

LAYERS = 4
VMEM_LIMIT = 16 * 1024 * 1024


def swapped(shard, axis, stride):
    return lax.ppermute(shard, axis, [(i, i ^ 1 << stride) for i in range(lax.axis_size(axis))])


def after(value, *others):
    return lax.optimization_barrier((value, *others))[0]


def earlier_layers(value, reach, group_size):
    count = lax.axis_size("section")
    shifts = [hop * group_size for hop in range(1, reach)]
    return [lax.ppermute(value, "section", [(i, (i + shift) % count) for i in range(count)]) for shift in shifts]


def by_hop(acts, reach):
    layer = lax.axis_index("section") // (lax.axis_size("section") // LAYERS)
    for hop, values in enumerate(acts[:reach]):
        yield jnp.where(layer >= hop, values[...], jnp.zeros(values.shape, values.dtype)) if hop else values[...]


def group_reduce(partial_rows, group_size):
    current = partial_rows
    section_index = lax.axis_index("section")
    level_count = group_size.bit_length() - 1
    for level in reversed(range(level_count)):
        half = current.shape[0] // 2
        lower = current[:half]
        upper = current[half:]
        high_side = section_index // 2**level % 2 == 1
        kept = jnp.where(high_side, upper, lower)
        sent = jnp.where(high_side, lower, upper)
        received = swapped(sent.astype(jnp.bfloat16), "section", level).astype(sent.dtype)
        current = kept + received
    return current


def to_peer(value, offset):
    return lax.ppermute(value, "latent", [(i, i ^ offset) for i in range(lax.axis_size("latent"))])


def call(kernel, out_shape, cost=None):
    return pl.pallas_call(
        kernel,
        out_shape=out_shape,
        cost_estimate=cost,
        compiler_params=pltpu.CompilerParams(vmem_limit_bytes=VMEM_LIMIT),
    )


def encode_near_kernel(offsets, far_offsets, *refs):
    *x_refs, own_ref, sib_ref, gates_ref, gates_sib_ref, out_ref, thr_ref, far_ref = refs
    depth = x_refs[0].shape[1]
    place = lax.axis_index("latent")

    def weights(offset):
        rows = pl.ds(pl.multiple_of((place ^ offset) * depth, 16), depth)
        return jnp.concatenate([own_ref[rows, :], sib_ref[rows, :]], axis=1)

    bias, thr = (jnp.concatenate([gates_ref[i:i + 1, :], gates_sib_ref[i:i + 1, :]], axis=1) for i in (0, 1))
    total = jnp.broadcast_to(bias, out_ref.shape)
    for offset, x_ref in zip(offsets, x_refs):
        total += jnp.dot(x_ref[...], weights(offset), preferred_element_type=jnp.float32)
    out_ref[...] = total
    thr_ref[...] = thr
    for index, offset in enumerate(far_offsets):
        far_ref[index] = weights(offset)


def encode_near(pieces, far_offsets, own, sib, gates, gates_sib):
    rows, depth = next(iter(pieces.values())).shape
    lat = 2 * own.shape[1]
    shapes = (
        jax.ShapeDtypeStruct((rows, lat), jnp.float32),
        jax.ShapeDtypeStruct((1, lat), jnp.float32),
        jax.ShapeDtypeStruct((len(far_offsets), depth, lat), own.dtype),
    )
    cost = pl.CostEstimate(2 * len(pieces) * rows * depth * lat, 4 * own.size, 0)
    kernel = functools.partial(encode_near_kernel, tuple(pieces), far_offsets)
    return call(kernel, shapes, cost=cost)(*pieces.values(), own, sib, gates, gates_sib)


def encode_kernel(near_ref, thr_ref, weights_ref, *refs):
    *x_refs, acts_ref = refs
    preact = near_ref[...]
    for index, x_ref in enumerate(x_refs):
        preact += jnp.dot(x_ref[...], weights_ref[index], preferred_element_type=jnp.float32)
    acts_ref[...] = jnp.where(preact > thr_ref[...], preact, 0.0).astype(jnp.bfloat16)


def encode(near, thr, weights, pieces):
    return call(encode_kernel, jax.ShapeDtypeStruct(near.shape, jnp.bfloat16))(near, thr, weights, *pieces)


def decoded(acts, own_ref, sib_ref, columns):
    total = None
    for hop, values in enumerate(by_hop(acts, own_ref.shape[0])):
        weights = jnp.concatenate([own_ref[hop, :, columns], sib_ref[hop, :, columns]], axis=0)
        part = jnp.dot(values, weights, preferred_element_type=jnp.float32)
        total = part if total is None else total + part
    return total


def decode_chip_kernel(chip_offset, *refs):
    *acts, own_ref, sib_ref, same_ref, cross_ref = refs
    width = same_ref.shape[1]
    place = lax.axis_index("latent")
    columns = pl.ds(pl.multiple_of(((place // 2) ^ chip_offset) * (2 * width), 128), 2 * width)
    total = decoded(acts, own_ref, sib_ref, columns).astype(jnp.bfloat16)
    low, high = total[:, :width], total[:, width:]
    first_core = place % 2 == 0
    same_ref[...] = jnp.where(first_core, low, high)
    cross_ref[...] = jnp.where(first_core, high, low)


def decode_chip(chip_offset, acts, own, sib, width):
    shape = jax.ShapeDtypeStruct((acts[0].shape[0], width), jnp.bfloat16)
    return call(functools.partial(decode_chip_kernel, chip_offset), (shape, shape))(*acts, own, sib)


def decode_all_kernel(*refs):
    *acts, own_ref, sib_ref, out_ref = refs
    count, _, width = out_ref.shape
    block = math.lcm(width, 128)
    per_block = block // width
    for step in range(count // per_block):
        total = decoded(acts, own_ref, sib_ref, slice(step * block, (step + 1) * block))
        for piece in range(per_block):
            out_ref[step * per_block + piece] = total[:, piece * width:(piece + 1) * width].astype(jnp.bfloat16)


def sum_two_kernel(a_ref, b_ref, out_ref):
    out_ref[...] = (a_ref[...].astype(jnp.float32) + b_ref[...].astype(jnp.float32)).astype(jnp.bfloat16)


def sum_two(a, b):
    return call(sum_two_kernel, jax.ShapeDtypeStruct(a.shape, jnp.bfloat16))(a, b)


def finish_kernel(*refs):
    *parts, out_ref, sums, sems = refs
    half = len(parts) // 2
    rows = parts[0].shape[0]
    core = lax.axis_index("latent") % 2
    copies = []
    for index, (place, group) in enumerate(((core, parts[:half]), (1 - core, parts[half:]))):
        total = group[0][...].astype(jnp.float32)
        for part in group[1:]:
            total += part[...].astype(jnp.float32)
        sums[index] = total.astype(out_ref.dtype)
        target = out_ref.at[pl.ds(pl.multiple_of(place * rows, 16), rows), :]
        copies.append(pltpu.make_async_copy(sums.at[index], target, sems.at[index]))
        copies[-1].start()
    for copy in copies:
        copy.wait()


def finish(mine, other, dtype):
    rows, width = mine[0].shape
    return pl.pallas_call(
        finish_kernel,
        out_shape=jax.ShapeDtypeStruct((2 * rows, width), dtype),
        out_specs=pl.BlockSpec(memory_space=pl.ANY),
        scratch_shapes=[pltpu.VMEM((2, rows, width), dtype), pltpu.SemaphoreType.DMA((2,))],
        compiler_params=pltpu.CompilerParams(vmem_limit_bytes=VMEM_LIMIT),
    )(*mine, *other)


def gather_and_encode(mine, other, gates, encoder, decoder):
    count = lax.axis_size("latent")
    if count != 8:
        core = lax.axis_index("latent") % 2
        pair = jnp.where(core == 0, jnp.stack([mine, other]), jnp.stack([other, mine]))
        outgoing = jnp.broadcast_to(pair, (count // 2, *pair.shape)).reshape(count, *mine.shape)
        everyone = lax.all_to_all(outgoing, "latent", 0, 0, tiled=True)
        place = lax.axis_index("latent")
        pieces = {i: lax.dynamic_index_in_dim(everyone, place ^ i, 0, keepdims=False) for i in range(count)}
        near, far = {i: pieces[i] for i in range(count // 2)}, {i: pieces[i] for i in range(count // 2, count)}
        enc_sib, gates_sib, dec_sib = (to_peer(value, 1) for value in (encoder, gates, decoder))
        near_sum, *rest = encode_near(near, tuple(far), encoder, enc_sib, gates, gates_sib)
    else:
        near = {0: mine, 2: to_peer(mine, 2), 3: to_peer(other, 3), 4: to_peer(mine, 4), 5: to_peer(other, 5)}
        enc_sib = to_peer(encoder, 1)
        far = {6: to_peer(near[2], 4), 7: to_peer(near[5], 2)}
        near[1] = to_peer(after(other, enc_sib), 1)
        gates_sib = to_peer(after(gates, enc_sib), 1)
        near_sum, *rest = encode_near(near, tuple(far), encoder, enc_sib, gates, gates_sib)
        dec_sib = to_peer(after(decoder, far[6], far[7], near_sum), 1)
    return encode(near_sum, *rest, far.values()), dec_sib


def decode_and_scatter(acts, own, sib, width, dtype):
    count = lax.axis_size("latent")
    rows = acts[0].shape[0]
    if count != 8:
        shares = call(decode_all_kernel, jax.ShapeDtypeStruct((count, rows, width), jnp.bfloat16))(*acts, own, sib)
        received = lax.all_to_all(shares, "latent", 0, 0, tiled=True)
        return jnp.sum(received.reshape(count // 2, 2 * rows, width).astype(jnp.float32), axis=0).astype(dtype)
    diag_same, diag_cross = decode_chip(3, acts, own, sib, width)
    for_y, for_x = to_peer(diag_same, 2), to_peer(diag_cross, 4)
    x_same, x_cross = decode_chip(1, acts, own, sib, width)
    y_same, y_cross = decode_chip(2, acts, own, sib, width)
    from_x_same, from_y_cross = to_peer(x_same, 2), to_peer(y_cross, 5)
    own_same, own_cross = decode_chip(0, acts, own, sib, width)
    y_sum, x_sum = sum_two(y_same, for_y), sum_two(x_cross, for_x)
    from_y_same, from_x_cross = to_peer(y_sum, 4), to_peer(x_sum, 3)
    from_sib = to_peer(own_cross, 1)
    return finish((own_same, from_x_same, from_y_same), (from_sib, from_x_cross, from_y_cross), dtype)


def shards(residual, encoder, enc_bias, gate_code, decoder):
    group_size = lax.axis_size("section") // LAYERS
    core = lax.axis_index("latent") % 2
    _, tok, width = residual.shape
    lat = encoder.shape[2]
    reach = decoder.shape[1]

    halves = residual.reshape(residual.shape[0] * 2, tok // 2, width)
    place = 2 * (lax.axis_index("section") // group_size)
    mine, other = (lax.dynamic_index_in_dim(halves, place + half, 0, keepdims=False) for half in (core, 1 - core))
    threshold = 10000.0 * (gate_code[0].astype(jnp.float32) - 1.0)
    gates_own = jnp.stack([enc_bias[0], threshold])
    acts, dec_sib = gather_and_encode(mine, other, gates_own, encoder[0], decoder[0])
    kept, passed = acts[:, :lat], to_peer(acts[:, lat:], 1)
    latent_acts = jnp.where(core == 0, jnp.stack([kept, passed]), jnp.stack([passed, kept])).reshape(tok, lat)

    received = earlier_layers(acts, reach, group_size)
    received[0] = after(received[0], passed)
    out_type = jnp.bfloat16 if group_size == 1 else jnp.float32
    summed = decode_and_scatter([acts, *received], decoder[0], dec_sib, width, out_type)
    rebuilt = group_reduce(summed, group_size).astype(jnp.bfloat16)
    return (rebuilt[None], latent_acts[None])


def solution(mesh):
    return jax.shard_map(
        shards,
        mesh=mesh,
        in_specs=(
            P(None, None, "latent"),
            P("section", None, "latent"),
            P("section", "latent"),
            P("section", "latent"),
            P("section", None, "latent", None),
        ),
        out_specs=(P("section", None, "latent"), P("section", None, "latent")),
        check_vma=False,
    )
```

```python
import functools
import math

import jax
import jax.numpy as jnp
from jax import lax
from jax.experimental import pallas as pl
from jax.experimental.pallas import tpu as pltpu
from jax.sharding import PartitionSpec as P

LAYERS = 4
VMEM_LIMIT = 16 * 1024 * 1024


def swapped(shard, axis, stride):
    return lax.ppermute(shard, axis, [(i, i ^ 1 << stride) for i in range(lax.axis_size(axis))])


def after(value, *others):
    return lax.optimization_barrier((value, *others))[0]


def layer_offsets(reach):
    offsets = {layer ^ (layer - hop) for hop in range(1, reach) for layer in range(hop, LAYERS)}
    return sorted(offsets, key=lambda offset: (offset % 2, offset))


def other_layers(value, reach, group_size):
    received = []
    for offset in layer_offsets(reach):
        wanted = {layer for layer in range(LAYERS) if 0 < layer - (layer ^ offset) < reach}
        wanted |= {layer ^ offset for layer in wanted}
        pairs = [
            (index, index ^ offset * group_size if index // group_size in wanted else index)
            for index in range(lax.axis_size("section"))
        ]
        received.append(lax.ppermute(value, "section", pairs))
    return received


def by_hop(acts, reach):
    layer = lax.axis_index("section") // (lax.axis_size("section") // LAYERS)
    own, *received = acts
    yield own[...]
    for hop in range(1, reach):
        source = jnp.zeros(own.shape, own.dtype)
        for offset, arrived in zip(layer_offsets(reach), received):
            for target in range(hop, LAYERS):
                if target ^ offset == target - hop:
                    source = jnp.where(layer == target, arrived[...], source)
        yield source


def group_reduce(partial_rows, group_size):
    current = partial_rows
    section_index = lax.axis_index("section")
    level_count = group_size.bit_length() - 1
    for level in reversed(range(level_count)):
        half = current.shape[0] // 2
        lower = current[:half]
        upper = current[half:]
        high_side = section_index // 2**level % 2 == 1
        kept = jnp.where(high_side, upper, lower)
        sent = jnp.where(high_side, lower, upper)
        received = swapped(sent.astype(jnp.bfloat16), "section", level).astype(sent.dtype)
        current = kept + received
    return current


def to_peer(value, offset):
    return lax.ppermute(value, "latent", [(i, i ^ offset) for i in range(lax.axis_size("latent"))])


def call(kernel, out_shape, cost=None):
    return pl.pallas_call(
        kernel,
        out_shape=out_shape,
        cost_estimate=cost,
        compiler_params=pltpu.CompilerParams(vmem_limit_bytes=VMEM_LIMIT),
    )


def encode_near_kernel(offsets, far_offsets, *refs):
    *x_refs, own_ref, sib_ref, gates_ref, gates_sib_ref, out_ref, thr_ref, far_ref = refs
    depth = x_refs[0].shape[1]
    place = lax.axis_index("latent")

    def weights(offset):
        rows = pl.ds(pl.multiple_of((place ^ offset) * depth, 16), depth)
        return jnp.concatenate([own_ref[rows, :], sib_ref[rows, :]], axis=1)

    bias, thr = (jnp.concatenate([gates_ref[i:i + 1, :], gates_sib_ref[i:i + 1, :]], axis=1) for i in (0, 1))
    total = jnp.broadcast_to(bias, out_ref.shape)
    for offset, x_ref in zip(offsets, x_refs):
        total += jnp.dot(x_ref[...], weights(offset), preferred_element_type=jnp.float32)
    out_ref[...] = total
    thr_ref[...] = thr
    for index, offset in enumerate(far_offsets):
        far_ref[index] = weights(offset)


def encode_near(pieces, far_offsets, own, sib, gates, gates_sib):
    rows, depth = next(iter(pieces.values())).shape
    lat = 2 * own.shape[1]
    shapes = (
        jax.ShapeDtypeStruct((rows, lat), jnp.float32),
        jax.ShapeDtypeStruct((1, lat), jnp.float32),
        jax.ShapeDtypeStruct((len(far_offsets), depth, lat), own.dtype),
    )
    cost = pl.CostEstimate(2 * len(pieces) * rows * depth * lat, 4 * own.size, 0)
    kernel = functools.partial(encode_near_kernel, tuple(pieces), far_offsets)
    return call(kernel, shapes, cost=cost)(*pieces.values(), own, sib, gates, gates_sib)


def encode_kernel(near_ref, thr_ref, weights_ref, *refs):
    *x_refs, acts_ref = refs
    preact = near_ref[...]
    for index, x_ref in enumerate(x_refs):
        preact += jnp.dot(x_ref[...], weights_ref[index], preferred_element_type=jnp.float32)
    acts_ref[...] = jnp.where(preact > thr_ref[...], preact, 0.0).astype(jnp.bfloat16)


def encode(near, thr, weights, pieces):
    return call(encode_kernel, jax.ShapeDtypeStruct(near.shape, jnp.bfloat16))(near, thr, weights, *pieces)


def decoded(acts, own_ref, sib_ref, columns):
    total = None
    for hop, values in enumerate(by_hop(acts, own_ref.shape[0])):
        weights = jnp.concatenate([own_ref[hop, :, columns], sib_ref[hop, :, columns]], axis=0)
        part = jnp.dot(values, weights, preferred_element_type=jnp.float32)
        total = part if total is None else total + part
    return total


def decode_chip_kernel(chip_offset, *refs):
    *acts, own_ref, sib_ref, same_ref, cross_ref = refs
    width = same_ref.shape[1]
    place = lax.axis_index("latent")
    columns = pl.ds(pl.multiple_of(((place // 2) ^ chip_offset) * (2 * width), 128), 2 * width)
    total = decoded(acts, own_ref, sib_ref, columns).astype(jnp.bfloat16)
    low, high = total[:, :width], total[:, width:]
    first_core = place % 2 == 0
    same_ref[...] = jnp.where(first_core, low, high)
    cross_ref[...] = jnp.where(first_core, high, low)


def decode_chip(chip_offset, acts, own, sib, width):
    shape = jax.ShapeDtypeStruct((acts[0].shape[0], width), jnp.bfloat16)
    return call(functools.partial(decode_chip_kernel, chip_offset), (shape, shape))(*acts, own, sib)


def decode_all_kernel(*refs):
    *acts, own_ref, sib_ref, out_ref = refs
    count, _, width = out_ref.shape
    block = math.lcm(width, 128)
    per_block = block // width
    for step in range(count // per_block):
        total = decoded(acts, own_ref, sib_ref, slice(step * block, (step + 1) * block))
        for piece in range(per_block):
            out_ref[step * per_block + piece] = total[:, piece * width:(piece + 1) * width].astype(jnp.bfloat16)


def sum_two_kernel(a_ref, b_ref, out_ref):
    out_ref[...] = (a_ref[...].astype(jnp.float32) + b_ref[...].astype(jnp.float32)).astype(jnp.bfloat16)


def sum_two(a, b):
    return call(sum_two_kernel, jax.ShapeDtypeStruct(a.shape, jnp.bfloat16))(a, b)


def finish_kernel(*refs):
    *parts, out_ref, sums, sems = refs
    half = len(parts) // 2
    rows = parts[0].shape[0]
    core = lax.axis_index("latent") % 2
    copies = []
    for index, (place, group) in enumerate(((core, parts[:half]), (1 - core, parts[half:]))):
        total = group[0][...].astype(jnp.float32)
        for part in group[1:]:
            total += part[...].astype(jnp.float32)
        sums[index] = total.astype(out_ref.dtype)
        target = out_ref.at[pl.ds(pl.multiple_of(place * rows, 16), rows), :]
        copies.append(pltpu.make_async_copy(sums.at[index], target, sems.at[index]))
        copies[-1].start()
    for copy in copies:
        copy.wait()


def finish(mine, other, dtype):
    rows, width = mine[0].shape
    return pl.pallas_call(
        finish_kernel,
        out_shape=jax.ShapeDtypeStruct((2 * rows, width), dtype),
        out_specs=pl.BlockSpec(memory_space=pl.ANY),
        scratch_shapes=[pltpu.VMEM((2, rows, width), dtype), pltpu.SemaphoreType.DMA((2,))],
        compiler_params=pltpu.CompilerParams(vmem_limit_bytes=VMEM_LIMIT),
    )(*mine, *other)


def gather_and_encode(mine, other, gates, encoder, decoder):
    count = lax.axis_size("latent")
    if count != 8:
        core = lax.axis_index("latent") % 2
        pair = jnp.where(core == 0, jnp.stack([mine, other]), jnp.stack([other, mine]))
        outgoing = jnp.broadcast_to(pair, (count // 2, *pair.shape)).reshape(count, *mine.shape)
        everyone = lax.all_to_all(outgoing, "latent", 0, 0, tiled=True)
        place = lax.axis_index("latent")
        pieces = {i: lax.dynamic_index_in_dim(everyone, place ^ i, 0, keepdims=False) for i in range(count)}
        near, far = {i: pieces[i] for i in range(count // 2)}, {i: pieces[i] for i in range(count // 2, count)}
        enc_sib, gates_sib, dec_sib = (to_peer(value, 1) for value in (encoder, gates, decoder))
        near_sum, *rest = encode_near(near, tuple(far), encoder, enc_sib, gates, gates_sib)
    else:
        near = {0: mine, 2: to_peer(mine, 2), 3: to_peer(other, 3), 4: to_peer(mine, 4), 5: to_peer(other, 5)}
        enc_sib = to_peer(encoder, 1)
        far = {6: to_peer(near[2], 4), 7: to_peer(near[5], 2)}
        near[1] = to_peer(after(other, enc_sib), 1)
        gates_sib = to_peer(after(gates, enc_sib), 1)
        near_sum, *rest = encode_near(near, tuple(far), encoder, enc_sib, gates, gates_sib)
        dec_sib = to_peer(after(decoder, far[6], far[7], near_sum), 1)
    return encode(near_sum, *rest, far.values()), dec_sib


def decode_and_scatter(acts, own, sib, width, dtype):
    count = lax.axis_size("latent")
    rows = acts[0].shape[0]
    if count != 8:
        shares = call(decode_all_kernel, jax.ShapeDtypeStruct((count, rows, width), jnp.bfloat16))(*acts, own, sib)
        received = lax.all_to_all(shares, "latent", 0, 0, tiled=True)
        return jnp.sum(received.reshape(count // 2, 2 * rows, width).astype(jnp.float32), axis=0).astype(dtype)
    diag_same, diag_cross = decode_chip(3, acts, own, sib, width)
    for_y, for_x = to_peer(diag_same, 2), to_peer(diag_cross, 4)
    x_same, x_cross = decode_chip(1, acts, own, sib, width)
    y_same, y_cross = decode_chip(2, acts, own, sib, width)
    from_x_same, from_y_cross = to_peer(x_same, 2), to_peer(y_cross, 5)
    own_same, own_cross = decode_chip(0, acts, own, sib, width)
    y_sum, x_sum = sum_two(y_same, for_y), sum_two(x_cross, for_x)
    from_y_same, from_x_cross = to_peer(y_sum, 4), to_peer(x_sum, 3)
    from_sib = to_peer(own_cross, 1)
    return finish((own_same, from_x_same, from_y_same), (from_sib, from_x_cross, from_y_cross), dtype)


def shards(residual, encoder, enc_bias, gate_code, decoder):
    group_size = lax.axis_size("section") // LAYERS
    core = lax.axis_index("latent") % 2
    _, tok, width = residual.shape
    lat = encoder.shape[2]
    reach = decoder.shape[1]

    halves = residual.reshape(residual.shape[0] * 2, tok // 2, width)
    place = 2 * (lax.axis_index("section") // group_size)
    mine, other = (lax.dynamic_index_in_dim(halves, place + half, 0, keepdims=False) for half in (core, 1 - core))
    threshold = 10000.0 * (gate_code[0].astype(jnp.float32) - 1.0)
    gates_own = jnp.stack([enc_bias[0], threshold])
    acts, dec_sib = gather_and_encode(mine, other, gates_own, encoder[0], decoder[0])
    kept, passed = acts[:, :lat], to_peer(acts[:, lat:], 1)
    latent_acts = jnp.where(core == 0, jnp.stack([kept, passed]), jnp.stack([passed, kept])).reshape(tok, lat)

    received = other_layers(acts, reach, group_size)
    received[2] = after(received[2], passed)
    out_type = jnp.bfloat16 if group_size == 1 else jnp.float32
    summed = decode_and_scatter([acts, *received], decoder[0], dec_sib, width, out_type)
    rebuilt = group_reduce(summed, group_size).astype(jnp.bfloat16)
    return (rebuilt[None], latent_acts[None])


def solution(mesh):
    return jax.shard_map(
        shards,
        mesh=mesh,
        in_specs=(
            P(None, None, "latent"),
            P("section", None, "latent"),
            P("section", "latent"),
            P("section", "latent"),
            P("section", None, "latent", None),
        ),
        out_specs=(P("section", None, "latent"), P("section", None, "latent")),
        check_vma=False,
    )
```

```python
import functools
import math

import jax
import jax.numpy as jnp
from jax import lax
from jax.experimental import pallas as pl
from jax.experimental.pallas import tpu as pltpu
from jax.sharding import PartitionSpec as P

LAYERS = 4
TAIL_PARTS = 2
VMEM_LIMIT = 16 * 1024 * 1024


def swapped(shard, axis, stride):
    return lax.ppermute(shard, axis, [(i, i ^ 1 << stride) for i in range(lax.axis_size(axis))])


def after(value, *others):
    return lax.optimization_barrier((value, *others))[0]


def earlier_layers(value, reach, group_size):
    count = lax.axis_size("section")
    shifts = [hop * group_size for hop in range(1, reach)]
    return [lax.ppermute(value, "section", [(i, (i + shift) % count) for i in range(count)]) for shift in shifts]


def by_hop(acts, reach):
    layer = lax.axis_index("section") // (lax.axis_size("section") // LAYERS)
    for hop, values in enumerate(acts[:reach]):
        yield jnp.where(layer >= hop, values[...], jnp.zeros(values.shape, values.dtype)) if hop else values[...]


def group_reduce(partial_rows, group_size):
    current = partial_rows
    section_index = lax.axis_index("section")
    level_count = group_size.bit_length() - 1
    for level in reversed(range(level_count)):
        half = current.shape[0] // 2
        lower = current[:half]
        upper = current[half:]
        high_side = section_index // 2**level % 2 == 1
        kept = jnp.where(high_side, upper, lower)
        sent = jnp.where(high_side, lower, upper)
        received = swapped(sent.astype(jnp.bfloat16), "section", level).astype(sent.dtype)
        current = kept + received
    return current


def to_peer(value, offset):
    return lax.ppermute(value, "latent", [(i, i ^ offset) for i in range(lax.axis_size("latent"))])


def call(kernel, out_shape, cost=None):
    return pl.pallas_call(
        kernel,
        out_shape=out_shape,
        cost_estimate=cost,
        compiler_params=pltpu.CompilerParams(vmem_limit_bytes=VMEM_LIMIT),
    )


def encode_near_kernel(offsets, far_offsets, *refs):
    *x_refs, own_ref, sib_ref, gates_ref, gates_sib_ref, out_ref, thr_ref, far_ref = refs
    depth = x_refs[0].shape[1]
    place = lax.axis_index("latent")

    def weights(offset):
        rows = pl.ds(pl.multiple_of((place ^ offset) * depth, 16), depth)
        return jnp.concatenate([own_ref[rows, :], sib_ref[rows, :]], axis=1)

    bias, thr = (jnp.concatenate([gates_ref[i:i + 1, :], gates_sib_ref[i:i + 1, :]], axis=1) for i in (0, 1))
    total = jnp.broadcast_to(bias, out_ref.shape)
    for offset, x_ref in zip(offsets, x_refs):
        total += jnp.dot(x_ref[...], weights(offset), preferred_element_type=jnp.float32)
    out_ref[...] = total
    thr_ref[...] = thr
    for index, offset in enumerate(far_offsets):
        far_ref[index] = weights(offset)


def encode_near(pieces, far_offsets, own, sib, gates, gates_sib):
    rows, depth = next(iter(pieces.values())).shape
    lat = 2 * own.shape[1]
    shapes = (
        jax.ShapeDtypeStruct((rows, lat), jnp.float32),
        jax.ShapeDtypeStruct((1, lat), jnp.float32),
        jax.ShapeDtypeStruct((len(far_offsets), depth, lat), own.dtype),
    )
    cost = pl.CostEstimate(2 * len(pieces) * rows * depth * lat, 4 * own.size, 0)
    kernel = functools.partial(encode_near_kernel, tuple(pieces), far_offsets)
    return call(kernel, shapes, cost=cost)(*pieces.values(), own, sib, gates, gates_sib)


def encode_kernel(near_ref, thr_ref, weights_ref, *refs):
    *x_refs, acts_ref = refs
    preact = near_ref[...]
    for index, x_ref in enumerate(x_refs):
        preact += jnp.dot(x_ref[...], weights_ref[index], preferred_element_type=jnp.float32)
    acts_ref[...] = jnp.where(preact > thr_ref[...], preact, 0.0).astype(jnp.bfloat16)


def encode(near, thr, weights, pieces):
    return call(encode_kernel, jax.ShapeDtypeStruct(near.shape, jnp.bfloat16))(near, thr, weights, *pieces)


def decoded(acts, own_ref, sib_ref, columns):
    total = None
    for hop, values in enumerate(by_hop(acts, own_ref.shape[0])):
        weights = jnp.concatenate([own_ref[hop, :, columns], sib_ref[hop, :, columns]], axis=0)
        part = jnp.dot(values, weights, preferred_element_type=jnp.float32)
        total = part if total is None else total + part
    return total


def decode_chip_kernel(chip_offset, *refs):
    *acts, own_ref, sib_ref, same_ref, cross_ref = refs
    width = same_ref.shape[1]
    place = lax.axis_index("latent")
    columns = pl.ds(pl.multiple_of(((place // 2) ^ chip_offset) * (2 * width), 128), 2 * width)
    total = decoded(acts, own_ref, sib_ref, columns).astype(jnp.bfloat16)
    low, high = total[:, :width], total[:, width:]
    first_core = place % 2 == 0
    same_ref[...] = jnp.where(first_core, low, high)
    cross_ref[...] = jnp.where(first_core, high, low)


def decode_chip(chip_offset, acts, own, sib, width):
    shape = jax.ShapeDtypeStruct((acts[0].shape[0], width), jnp.bfloat16)
    return call(functools.partial(decode_chip_kernel, chip_offset), (shape, shape))(*acts, own, sib)


def decode_all_kernel(*refs):
    *acts, own_ref, sib_ref, out_ref = refs
    count, _, width = out_ref.shape
    block = math.lcm(width, 128)
    per_block = block // width
    for step in range(count // per_block):
        total = decoded(acts, own_ref, sib_ref, slice(step * block, (step + 1) * block))
        for piece in range(per_block):
            out_ref[step * per_block + piece] = total[:, piece * width:(piece + 1) * width].astype(jnp.bfloat16)


def sum_two_kernel(a_ref, b_ref, *out_refs):
    first = 0
    for out_ref in out_refs:
        rows = slice(first, first + out_ref.shape[0])
        out_ref[...] = (a_ref[rows, :].astype(jnp.float32) + b_ref[rows, :].astype(jnp.float32)).astype(jnp.bfloat16)
        first = rows.stop


def sum_two(a, b, parts):
    rows, width = a.shape
    edges = [rows * part // parts // 16 * 16 for part in range(parts)] + [rows]
    shapes = [jax.ShapeDtypeStruct((end - start, width), jnp.bfloat16) for start, end in zip(edges, edges[1:])]
    return call(sum_two_kernel, shapes)(a, b)


def finish_kernel(half, *refs):
    *parts, out_ref, sums, sems = refs
    rows = sums.shape[1]
    core = lax.axis_index("latent") % 2
    copies = []
    for index, (place, group) in enumerate(((core, parts[:half]), (1 - core, parts[half:]))):
        first = 0
        for last in group[2:]:
            some = slice(first, first + last.shape[0])
            total = sum(part[some, :].astype(jnp.float32) for part in group[:2]) + last[...].astype(jnp.float32)
            sums[index, some, :] = total.astype(out_ref.dtype)
            first = some.stop
        target = out_ref.at[pl.ds(pl.multiple_of(place * rows, 16), rows), :]
        copies.append(pltpu.make_async_copy(sums.at[index], target, sems.at[index]))
        copies[-1].start()
    for copy in copies:
        copy.wait()


def finish(mine, other, dtype):
    rows, width = mine[0].shape
    return pl.pallas_call(
        functools.partial(finish_kernel, len(mine)),
        out_shape=jax.ShapeDtypeStruct((2 * rows, width), dtype),
        out_specs=pl.BlockSpec(memory_space=pl.ANY),
        scratch_shapes=[pltpu.VMEM((2, rows, width), dtype), pltpu.SemaphoreType.DMA((2,))],
        compiler_params=pltpu.CompilerParams(vmem_limit_bytes=VMEM_LIMIT),
    )(*mine, *other)


def gather_and_encode(mine, other, gates, encoder, decoder):
    count = lax.axis_size("latent")
    if count != 8:
        core = lax.axis_index("latent") % 2
        pair = jnp.where(core == 0, jnp.stack([mine, other]), jnp.stack([other, mine]))
        outgoing = jnp.broadcast_to(pair, (count // 2, *pair.shape)).reshape(count, *mine.shape)
        everyone = lax.all_to_all(outgoing, "latent", 0, 0, tiled=True)
        place = lax.axis_index("latent")
        pieces = {i: lax.dynamic_index_in_dim(everyone, place ^ i, 0, keepdims=False) for i in range(count)}
        near, far = {i: pieces[i] for i in range(count // 2)}, {i: pieces[i] for i in range(count // 2, count)}
        enc_sib, gates_sib, dec_sib = (to_peer(value, 1) for value in (encoder, gates, decoder))
        near_sum, *rest = encode_near(near, tuple(far), encoder, enc_sib, gates, gates_sib)
    else:
        near = {0: mine, 2: to_peer(mine, 2), 3: to_peer(other, 3), 4: to_peer(mine, 4), 5: to_peer(other, 5)}
        enc_sib = to_peer(encoder, 1)
        far = {6: to_peer(near[2], 4), 7: to_peer(near[5], 2)}
        near[1] = to_peer(after(other, enc_sib), 1)
        gates_sib = to_peer(after(gates, enc_sib), 1)
        near_sum, *rest = encode_near(near, tuple(far), encoder, enc_sib, gates, gates_sib)
        dec_sib = to_peer(after(decoder, far[6], far[7], near_sum), 1)
    return encode(near_sum, *rest, far.values()), dec_sib


def decode_and_scatter(acts, own, sib, width, dtype):
    count = lax.axis_size("latent")
    rows = acts[0].shape[0]
    if count != 8:
        shares = call(decode_all_kernel, jax.ShapeDtypeStruct((count, rows, width), jnp.bfloat16))(*acts, own, sib)
        received = lax.all_to_all(shares, "latent", 0, 0, tiled=True)
        return jnp.sum(received.reshape(count // 2, 2 * rows, width).astype(jnp.float32), axis=0).astype(dtype)
    diag_same, diag_cross = decode_chip(3, acts, own, sib, width)
    for_y, for_x = to_peer(diag_same, 2), to_peer(diag_cross, 4)
    x_same, x_cross = decode_chip(1, acts, own, sib, width)
    y_same, y_cross = decode_chip(2, acts, own, sib, width)
    from_x_same, from_y_cross = to_peer(x_same, 2), to_peer(y_cross, 5)
    own_same, own_cross = decode_chip(0, acts, own, sib, width)
    from_sib = to_peer(own_cross, 1)
    y_sums = [after(part, from_sib) for part in sum_two(y_same, for_y, TAIL_PARTS)]
    from_y_same = [to_peer(part, 4) for part in y_sums]
    from_x_cross = [to_peer(part, 3) for part in sum_two(x_cross, for_x, 1)]
    return finish((own_same, from_x_same, *from_y_same), (from_sib, from_y_cross, *from_x_cross), dtype)


def shards(residual, encoder, enc_bias, gate_code, decoder):
    group_size = lax.axis_size("section") // LAYERS
    core = lax.axis_index("latent") % 2
    _, tok, width = residual.shape
    lat = encoder.shape[2]
    reach = decoder.shape[1]

    halves = residual.reshape(residual.shape[0] * 2, tok // 2, width)
    place = 2 * (lax.axis_index("section") // group_size)
    mine, other = (lax.dynamic_index_in_dim(halves, place + half, 0, keepdims=False) for half in (core, 1 - core))
    threshold = 10000.0 * (gate_code[0].astype(jnp.float32) - 1.0)
    gates_own = jnp.stack([enc_bias[0], threshold])
    acts, dec_sib = gather_and_encode(mine, other, gates_own, encoder[0], decoder[0])
    kept, passed = acts[:, :lat], to_peer(acts[:, lat:], 1)
    latent_acts = jnp.where(core == 0, jnp.stack([kept, passed]), jnp.stack([passed, kept])).reshape(tok, lat)

    received = earlier_layers(acts, reach, group_size)
    received[-1] = after(received[-1], passed)
    out_type = jnp.bfloat16 if group_size == 1 else jnp.float32
    summed = decode_and_scatter([acts, *received], decoder[0], dec_sib, width, out_type)
    rebuilt = group_reduce(summed, group_size).astype(jnp.bfloat16)
    return (rebuilt[None], latent_acts[None])


def solution(mesh):
    return jax.shard_map(
        shards,
        mesh=mesh,
        in_specs=(
            P(None, None, "latent"),
            P("section", None, "latent"),
            P("section", "latent"),
            P("section", "latent"),
            P("section", None, "latent", None),
        ),
        out_specs=(P("section", None, "latent"), P("section", None, "latent")),
        check_vma=False,
    )
```

```python
import functools
import math

import jax
import jax.numpy as jnp
from jax import lax
from jax.experimental import pallas as pl
from jax.experimental.pallas import tpu as pltpu
from jax.sharding import PartitionSpec as P

LAYERS = 4
VMEM_LIMIT = 16 * 1024 * 1024


def swapped(shard, axis, stride):
    return lax.ppermute(shard, axis, [(i, i ^ 1 << stride) for i in range(lax.axis_size(axis))])


def after(value, *others):
    return lax.optimization_barrier((value, *others))[0]


def earlier_layers(value, reach, group_size):
    count = lax.axis_size("section")
    shifts = [hop * group_size for hop in range(1, reach)]
    return [lax.ppermute(value, "section", [(i, (i + shift) % count) for i in range(count)]) for shift in shifts]


def by_hop(acts, reach):
    layer = lax.axis_index("section") // (lax.axis_size("section") // LAYERS)
    for hop, values in enumerate(acts[:reach]):
        yield jnp.where(layer >= hop, values[...], jnp.zeros(values.shape, values.dtype)) if hop else values[...]


def group_reduce(partial_rows, group_size):
    current = partial_rows
    section_index = lax.axis_index("section")
    level_count = group_size.bit_length() - 1
    for level in reversed(range(level_count)):
        half = current.shape[0] // 2
        lower = current[:half]
        upper = current[half:]
        high_side = section_index // 2**level % 2 == 1
        kept = jnp.where(high_side, upper, lower)
        sent = jnp.where(high_side, lower, upper)
        received = swapped(sent.astype(jnp.bfloat16), "section", level).astype(sent.dtype)
        current = kept + received
    return current


def to_peer(value, offset):
    return lax.ppermute(value, "latent", [(i, i ^ offset) for i in range(lax.axis_size("latent"))])


def call(kernel, out_shape, cost=None):
    return pl.pallas_call(
        kernel,
        out_shape=out_shape,
        cost_estimate=cost,
        compiler_params=pltpu.CompilerParams(vmem_limit_bytes=VMEM_LIMIT),
    )


def encode_near_kernel(offsets, far_offsets, *refs):
    *x_refs, own_ref, sib_ref, gates_ref, gates_sib_ref, out_ref, thr_ref, far_ref = refs
    depth = x_refs[0].shape[1]
    place = lax.axis_index("latent")

    def weights(offset):
        rows = pl.ds(pl.multiple_of((place ^ offset) * depth, 16), depth)
        return jnp.concatenate([own_ref[rows, :], sib_ref[rows, :]], axis=1)

    bias, thr = (jnp.concatenate([gates_ref[i:i + 1, :], gates_sib_ref[i:i + 1, :]], axis=1) for i in (0, 1))
    total = jnp.broadcast_to(bias, out_ref.shape)
    for offset, x_ref in zip(offsets, x_refs):
        total += jnp.dot(x_ref[...], weights(offset), preferred_element_type=jnp.float32)
    out_ref[...] = total
    thr_ref[...] = thr
    for index, offset in enumerate(far_offsets):
        far_ref[index] = weights(offset)


def encode_near(pieces, far_offsets, own, sib, gates, gates_sib):
    rows, depth = next(iter(pieces.values())).shape
    lat = 2 * own.shape[1]
    shapes = (
        jax.ShapeDtypeStruct((rows, lat), jnp.float32),
        jax.ShapeDtypeStruct((1, lat), jnp.float32),
        jax.ShapeDtypeStruct((len(far_offsets), depth, lat), own.dtype),
    )
    cost = pl.CostEstimate(2 * len(pieces) * rows * depth * lat, 4 * own.size, 0)
    kernel = functools.partial(encode_near_kernel, tuple(pieces), far_offsets)
    return call(kernel, shapes, cost=cost)(*pieces.values(), own, sib, gates, gates_sib)


def encode_kernel(near_ref, thr_ref, weights_ref, *refs):
    *x_refs, acts_ref = refs
    preact = near_ref[...]
    for index, x_ref in enumerate(x_refs):
        preact += jnp.dot(x_ref[...], weights_ref[index], preferred_element_type=jnp.float32)
    acts_ref[...] = jnp.where(preact > thr_ref[...], preact, 0.0).astype(jnp.bfloat16)


def encode(near, thr, weights, pieces):
    return call(encode_kernel, jax.ShapeDtypeStruct(near.shape, jnp.bfloat16))(near, thr, weights, *pieces)


def decoded(acts, own_ref, sib_ref, columns):
    total = None
    for hop, values in enumerate(by_hop(acts, own_ref.shape[0])):
        weights = jnp.concatenate([own_ref[hop, :, columns], sib_ref[hop, :, columns]], axis=0)
        part = jnp.dot(values, weights, preferred_element_type=jnp.float32)
        total = part if total is None else total + part
    return total


def decode_chip_kernel(chip_offset, *refs):
    *acts, own_ref, sib_ref, same_ref, cross_ref = refs
    width = same_ref.shape[1]
    place = lax.axis_index("latent")
    columns = pl.ds(pl.multiple_of(((place // 2) ^ chip_offset) * (2 * width), 128), 2 * width)
    total = decoded(acts, own_ref, sib_ref, columns).astype(jnp.bfloat16)
    low, high = total[:, :width], total[:, width:]
    first_core = place % 2 == 0
    same_ref[...] = jnp.where(first_core, low, high)
    cross_ref[...] = jnp.where(first_core, high, low)


def decode_chip(chip_offset, acts, own, sib, width):
    shape = jax.ShapeDtypeStruct((acts[0].shape[0], width), jnp.bfloat16)
    return call(functools.partial(decode_chip_kernel, chip_offset), (shape, shape))(*acts, own, sib)


def decode_core_kernel(offset, *refs):
    *acts, own_ref, sib_ref, out_ref = refs
    width = out_ref.shape[1]
    dest = lax.axis_index("latent") ^ offset
    odd = dest % 2
    spare = width % 128
    first = pl.multiple_of(dest * width - odd * spare, 128)
    total = decoded(acts, own_ref, sib_ref, pl.ds(first, width + spare)).astype(jnp.bfloat16)
    out_ref[...] = jnp.where(odd == 0, total[:, :width], total[:, spare:])


def decode_core(offset, acts, own, sib, width):
    rows = acts[0].shape[0]
    shape = jax.ShapeDtypeStruct((rows, width), jnp.bfloat16)
    cost = pl.CostEstimate(4 * rows * width * own.shape[0] * own.shape[1], 4 * own.shape[0] * own.shape[1] * width, 0)
    return call(functools.partial(decode_core_kernel, offset), shape, cost)(*acts, own, sib)


def decode_all_kernel(*refs):
    *acts, own_ref, sib_ref, out_ref = refs
    count, _, width = out_ref.shape
    block = math.lcm(width, 128)
    per_block = block // width
    for step in range(count // per_block):
        total = decoded(acts, own_ref, sib_ref, slice(step * block, (step + 1) * block))
        for piece in range(per_block):
            out_ref[step * per_block + piece] = total[:, piece * width:(piece + 1) * width].astype(jnp.bfloat16)


def sum_two_kernel(a_ref, b_ref, out_ref):
    out_ref[...] = (a_ref[...].astype(jnp.float32) + b_ref[...].astype(jnp.float32)).astype(jnp.bfloat16)


def sum_two(a, b):
    return call(sum_two_kernel, jax.ShapeDtypeStruct(a.shape, jnp.bfloat16))(a, b)


def finish_kernel(*refs):
    *parts, out_ref, sums, sems = refs
    half = len(parts) // 2
    rows = parts[0].shape[0]
    core = lax.axis_index("latent") % 2
    copies = []
    for index, (place, group) in enumerate(((core, parts[:half]), (1 - core, parts[half:]))):
        total = group[0][...].astype(jnp.float32)
        for part in group[1:]:
            total += part[...].astype(jnp.float32)
        sums[index] = total.astype(out_ref.dtype)
        target = out_ref.at[pl.ds(pl.multiple_of(place * rows, 16), rows), :]
        copies.append(pltpu.make_async_copy(sums.at[index], target, sems.at[index]))
        copies[-1].start()
    for copy in copies:
        copy.wait()


def finish(mine, other, dtype):
    rows, width = mine[0].shape
    return pl.pallas_call(
        finish_kernel,
        out_shape=jax.ShapeDtypeStruct((2 * rows, width), dtype),
        out_specs=pl.BlockSpec(memory_space=pl.ANY),
        scratch_shapes=[pltpu.VMEM((2, rows, width), dtype), pltpu.SemaphoreType.DMA((2,))],
        compiler_params=pltpu.CompilerParams(vmem_limit_bytes=VMEM_LIMIT),
    )(*mine, *other)


def gather_and_encode(mine, other, gates, encoder, decoder):
    count = lax.axis_size("latent")
    if count != 8:
        core = lax.axis_index("latent") % 2
        pair = jnp.where(core == 0, jnp.stack([mine, other]), jnp.stack([other, mine]))
        outgoing = jnp.broadcast_to(pair, (count // 2, *pair.shape)).reshape(count, *mine.shape)
        everyone = lax.all_to_all(outgoing, "latent", 0, 0, tiled=True)
        place = lax.axis_index("latent")
        pieces = {i: lax.dynamic_index_in_dim(everyone, place ^ i, 0, keepdims=False) for i in range(count)}
        near, far = {i: pieces[i] for i in range(count // 2)}, {i: pieces[i] for i in range(count // 2, count)}
        enc_sib, gates_sib, dec_sib = (to_peer(value, 1) for value in (encoder, gates, decoder))
        near_sum, *rest = encode_near(near, tuple(far), encoder, enc_sib, gates, gates_sib)
    else:
        near = {0: mine, 2: to_peer(mine, 2), 3: to_peer(other, 3), 4: to_peer(mine, 4), 5: to_peer(other, 5)}
        enc_sib = to_peer(encoder, 1)
        far = {6: to_peer(near[2], 4), 7: to_peer(near[5], 2)}
        near[1] = to_peer(after(other, enc_sib), 1)
        gates_sib = to_peer(after(gates, enc_sib), 1)
        near_sum, *rest = encode_near(near, tuple(far), encoder, enc_sib, gates, gates_sib)
        dec_sib = to_peer(after(decoder, far[6], far[7], near_sum), 1)
    return encode(near_sum, *rest, far.values()), dec_sib


def decode_and_scatter(acts, own, sib, width, dtype):
    count = lax.axis_size("latent")
    rows = acts[0].shape[0]
    if count != 8:
        shares = call(decode_all_kernel, jax.ShapeDtypeStruct((count, rows, width), jnp.bfloat16))(*acts, own, sib)
        received = lax.all_to_all(shares, "latent", 0, 0, tiled=True)
        return jnp.sum(received.reshape(count // 2, 2 * rows, width).astype(jnp.float32), axis=0).astype(dtype)
    for_x = to_peer(decode_core(7, acts, own, sib, width), 4)
    for_y = to_peer(decode_core(6, acts, own, sib, width), 2)
    x_same, x_cross = decode_chip(1, acts, own, sib, width)
    y_same, y_cross = decode_chip(2, acts, own, sib, width)
    from_x_same, from_y_cross = to_peer(x_same, 2), to_peer(y_cross, 5)
    own_same, own_cross = decode_chip(0, acts, own, sib, width)
    y_sum, x_sum = sum_two(y_same, for_y), sum_two(x_cross, for_x)
    from_y_same, from_x_cross = to_peer(y_sum, 4), to_peer(x_sum, 3)
    from_sib = to_peer(own_cross, 1)
    return finish((own_same, from_x_same, from_y_same), (from_sib, from_x_cross, from_y_cross), dtype)


def shards(residual, encoder, enc_bias, gate_code, decoder):
    group_size = lax.axis_size("section") // LAYERS
    core = lax.axis_index("latent") % 2
    _, tok, width = residual.shape
    lat = encoder.shape[2]
    reach = decoder.shape[1]

    halves = residual.reshape(residual.shape[0] * 2, tok // 2, width)
    place = 2 * (lax.axis_index("section") // group_size)
    mine, other = (lax.dynamic_index_in_dim(halves, place + half, 0, keepdims=False) for half in (core, 1 - core))
    threshold = 10000.0 * (gate_code[0].astype(jnp.float32) - 1.0)
    gates_own = jnp.stack([enc_bias[0], threshold])
    acts, dec_sib = gather_and_encode(mine, other, gates_own, encoder[0], decoder[0])
    kept, passed = acts[:, :lat], to_peer(acts[:, lat:], 1)
    latent_acts = jnp.where(core == 0, jnp.stack([kept, passed]), jnp.stack([passed, kept])).reshape(tok, lat)

    received = earlier_layers(acts, reach, group_size)
    received[-1] = after(received[-1], passed)
    out_type = jnp.bfloat16 if group_size == 1 else jnp.float32
    summed = decode_and_scatter([acts, *received], decoder[0], dec_sib, width, out_type)
    rebuilt = group_reduce(summed, group_size).astype(jnp.bfloat16)
    return (rebuilt[None], latent_acts[None])


def solution(mesh):
    return jax.shard_map(
        shards,
        mesh=mesh,
        in_specs=(
            P(None, None, "latent"),
            P("section", None, "latent"),
            P("section", "latent"),
            P("section", "latent"),
            P("section", None, "latent", None),
        ),
        out_specs=(P("section", None, "latent"), P("section", None, "latent")),
        check_vma=False,
    )
```

```python
import functools
import math

import jax
import jax.numpy as jnp
from jax import lax
from jax.experimental import pallas as pl
from jax.experimental.pallas import tpu as pltpu
from jax.sharding import PartitionSpec as P

LAYERS = 4
VMEM_LIMIT = 16 * 1024 * 1024


def swapped(shard, axis, stride):
    return lax.ppermute(shard, axis, [(i, i ^ 1 << stride) for i in range(lax.axis_size(axis))])


def after(value, *others):
    return lax.optimization_barrier((value, *others))[0]


def earlier_layers(value, reach, group_size):
    count = lax.axis_size("section")
    shifts = [hop * group_size for hop in range(1, reach)]
    return [lax.ppermute(value, "section", [(i, (i + shift) % count) for i in range(count)]) for shift in shifts]


def by_hop(acts, reach):
    layer = lax.axis_index("section") // (lax.axis_size("section") // LAYERS)
    for hop, values in enumerate(acts[:reach]):
        yield jnp.where(layer >= hop, values[...], jnp.zeros(values.shape, values.dtype)) if hop else values[...]


def group_reduce(partial_rows, group_size):
    current = partial_rows
    section_index = lax.axis_index("section")
    level_count = group_size.bit_length() - 1
    for level in reversed(range(level_count)):
        half = current.shape[0] // 2
        lower = current[:half]
        upper = current[half:]
        high_side = section_index // 2**level % 2 == 1
        kept = jnp.where(high_side, upper, lower)
        sent = jnp.where(high_side, lower, upper)
        received = swapped(sent.astype(jnp.bfloat16), "section", level).astype(sent.dtype)
        current = kept + received
    return current


def to_peer(value, offset):
    return lax.ppermute(value, "latent", [(i, i ^ offset) for i in range(lax.axis_size("latent"))])


def call(kernel, out_shape, cost=None):
    return pl.pallas_call(
        kernel,
        out_shape=out_shape,
        cost_estimate=cost,
        compiler_params=pltpu.CompilerParams(vmem_limit_bytes=VMEM_LIMIT),
    )


def encode_near_kernel(offsets, far_offsets, *refs):
    *x_refs, own_ref, sib_ref, gates_ref, gates_sib_ref, out_ref, thr_ref, far_ref = refs
    depth = x_refs[0].shape[1]
    place = lax.axis_index("latent")

    def weights(offset):
        rows = pl.ds(pl.multiple_of((place ^ offset) * depth, 16), depth)
        return jnp.concatenate([own_ref[rows, :], sib_ref[rows, :]], axis=1)

    bias, thr = (jnp.concatenate([gates_ref[i:i + 1, :], gates_sib_ref[i:i + 1, :]], axis=1) for i in (0, 1))
    total = jnp.broadcast_to(bias, out_ref.shape)
    for offset, x_ref in zip(offsets, x_refs):
        total += jnp.dot(x_ref[...], weights(offset), preferred_element_type=jnp.float32)
    out_ref[...] = total
    thr_ref[...] = thr
    for index, offset in enumerate(far_offsets):
        far_ref[index] = weights(offset)


def encode_near(pieces, far_offsets, own, sib, gates, gates_sib):
    rows, depth = next(iter(pieces.values())).shape
    lat = 2 * own.shape[1]
    shapes = (
        jax.ShapeDtypeStruct((rows, lat), jnp.float32),
        jax.ShapeDtypeStruct((1, lat), jnp.float32),
        jax.ShapeDtypeStruct((len(far_offsets), depth, lat), own.dtype),
    )
    cost = pl.CostEstimate(2 * len(pieces) * rows * depth * lat, 4 * own.size, 0)
    kernel = functools.partial(encode_near_kernel, tuple(pieces), far_offsets)
    return call(kernel, shapes, cost=cost)(*pieces.values(), own, sib, gates, gates_sib)


def encode_kernel(near_ref, thr_ref, weights_ref, *refs):
    *x_refs, acts_ref = refs
    preact = near_ref[...]
    for index, x_ref in enumerate(x_refs):
        preact += jnp.dot(x_ref[...], weights_ref[index], preferred_element_type=jnp.float32)
    acts_ref[...] = jnp.where(preact > thr_ref[...], preact, 0.0).astype(jnp.bfloat16)


def encode(near, thr, weights, pieces):
    return call(encode_kernel, jax.ShapeDtypeStruct(near.shape, jnp.bfloat16))(near, thr, weights, *pieces)


def decoded(acts, own_ref, sib_ref, columns):
    total = None
    for hop, values in enumerate(by_hop(acts, own_ref.shape[0])):
        weights = jnp.concatenate([own_ref[hop, :, columns], sib_ref[hop, :, columns]], axis=0)
        part = jnp.dot(values, weights, preferred_element_type=jnp.float32)
        total = part if total is None else total + part
    return total


def decode_chip_kernel(chip_offset, *refs):
    *acts, own_ref, sib_ref, same_ref, cross_ref = refs
    width = same_ref.shape[1]
    place = lax.axis_index("latent")
    columns = pl.ds(pl.multiple_of(((place // 2) ^ chip_offset) * (2 * width), 128), 2 * width)
    total = decoded(acts, own_ref, sib_ref, columns).astype(jnp.bfloat16)
    low, high = total[:, :width], total[:, width:]
    first_core = place % 2 == 0
    same_ref[...] = jnp.where(first_core, low, high)
    cross_ref[...] = jnp.where(first_core, high, low)


def decode_chip(chip_offset, acts, own, sib, width):
    shape = jax.ShapeDtypeStruct((acts[0].shape[0], width), jnp.bfloat16)
    return call(functools.partial(decode_chip_kernel, chip_offset), (shape, shape))(*acts, own, sib)


def decode_all_kernel(*refs):
    *acts, own_ref, sib_ref, out_ref = refs
    count, _, width = out_ref.shape
    block = math.lcm(width, 128)
    per_block = block // width
    for step in range(count // per_block):
        total = decoded(acts, own_ref, sib_ref, slice(step * block, (step + 1) * block))
        for piece in range(per_block):
            out_ref[step * per_block + piece] = total[:, piece * width:(piece + 1) * width].astype(jnp.bfloat16)


def sum_two_kernel(a_ref, b_ref, out_ref):
    out_ref[...] = (a_ref[...].astype(jnp.float32) + b_ref[...].astype(jnp.float32)).astype(jnp.bfloat16)


def sum_two(a, b):
    return call(sum_two_kernel, jax.ShapeDtypeStruct(a.shape, jnp.bfloat16))(a, b)


def finish_kernel(*refs):
    *parts, out_ref, sums, sems = refs
    half = len(parts) // 2
    rows = parts[0].shape[0]
    core = lax.axis_index("latent") % 2
    copies = []
    for index, (place, group) in enumerate(((core, parts[:half]), (1 - core, parts[half:]))):
        total = group[0][...].astype(jnp.float32)
        for part in group[1:]:
            total += part[...].astype(jnp.float32)
        sums[index] = total.astype(out_ref.dtype)
        target = out_ref.at[pl.ds(pl.multiple_of(place * rows, 16), rows), :]
        copies.append(pltpu.make_async_copy(sums.at[index], target, sems.at[index]))
        copies[-1].start()
    for copy in copies:
        copy.wait()


def finish(mine, other, dtype):
    rows, width = mine[0].shape
    return pl.pallas_call(
        finish_kernel,
        out_shape=jax.ShapeDtypeStruct((2 * rows, width), dtype),
        out_specs=pl.BlockSpec(memory_space=pl.ANY),
        scratch_shapes=[pltpu.VMEM((2, rows, width), dtype), pltpu.SemaphoreType.DMA((2,))],
        compiler_params=pltpu.CompilerParams(vmem_limit_bytes=VMEM_LIMIT),
    )(*mine, *other)


def gather_and_encode(mine, other, gates, encoder, decoder):
    count = lax.axis_size("latent")
    if count != 8:
        core = lax.axis_index("latent") % 2
        pair = jnp.where(core == 0, jnp.stack([mine, other]), jnp.stack([other, mine]))
        outgoing = jnp.broadcast_to(pair, (count // 2, *pair.shape)).reshape(count, *mine.shape)
        everyone = lax.all_to_all(outgoing, "latent", 0, 0, tiled=True)
        place = lax.axis_index("latent")
        pieces = {i: lax.dynamic_index_in_dim(everyone, place ^ i, 0, keepdims=False) for i in range(count)}
        near, far = {i: pieces[i] for i in range(count // 2)}, {i: pieces[i] for i in range(count // 2, count)}
        enc_sib, gates_sib, dec_sib = (to_peer(value, 1) for value in (encoder, gates, decoder))
        near_sum, *rest = encode_near(near, tuple(far), encoder, enc_sib, gates, gates_sib)
    else:
        near = {0: mine, 5: to_peer(other, 5), 4: to_peer(mine, 4), 3: to_peer(other, 3), 2: to_peer(mine, 2)}
        enc_sib = to_peer(encoder, 1)
        far = {7: to_peer(near[5], 2), 6: to_peer(near[2], 4)}
        near[1] = to_peer(after(other, enc_sib), 1)
        gates_sib = to_peer(after(gates, enc_sib), 1)
        near_sum, *rest = encode_near(near, tuple(far), encoder, enc_sib, gates, gates_sib)
        dec_sib = to_peer(after(decoder, far[6], far[7], near_sum), 1)
    return encode(near_sum, *rest, far.values()), dec_sib


def decode_and_scatter(acts, own, sib, width, dtype):
    count = lax.axis_size("latent")
    rows = acts[0].shape[0]
    if count != 8:
        shares = call(decode_all_kernel, jax.ShapeDtypeStruct((count, rows, width), jnp.bfloat16))(*acts, own, sib)
        received = lax.all_to_all(shares, "latent", 0, 0, tiled=True)
        return jnp.sum(received.reshape(count // 2, 2 * rows, width).astype(jnp.float32), axis=0).astype(dtype)
    diag_same, diag_cross = decode_chip(3, acts, own, sib, width)
    for_y, for_x = to_peer(diag_same, 2), to_peer(diag_cross, 4)
    x_same, x_cross = decode_chip(1, acts, own, sib, width)
    y_same, y_cross = decode_chip(2, acts, own, sib, width)
    from_x_same, from_y_cross = to_peer(x_same, 2), to_peer(y_cross, 5)
    own_same, own_cross = decode_chip(0, acts, own, sib, width)
    y_sum, x_sum = sum_two(y_same, for_y), sum_two(x_cross, for_x)
    from_y_same, from_x_cross = to_peer(y_sum, 4), to_peer(x_sum, 3)
    from_sib = to_peer(own_cross, 1)
    return finish((own_same, from_x_same, from_y_same), (from_sib, from_x_cross, from_y_cross), dtype)


def shards(residual, encoder, enc_bias, gate_code, decoder):
    group_size = lax.axis_size("section") // LAYERS
    core = lax.axis_index("latent") % 2
    _, tok, width = residual.shape
    lat = encoder.shape[2]
    reach = decoder.shape[1]

    halves = residual.reshape(residual.shape[0] * 2, tok // 2, width)
    place = 2 * (lax.axis_index("section") // group_size)
    mine, other = (lax.dynamic_index_in_dim(halves, place + half, 0, keepdims=False) for half in (core, 1 - core))
    threshold = 10000.0 * (gate_code[0].astype(jnp.float32) - 1.0)
    gates_own = jnp.stack([enc_bias[0], threshold])
    acts, dec_sib = gather_and_encode(mine, other, gates_own, encoder[0], decoder[0])
    kept, passed = acts[:, :lat], to_peer(acts[:, lat:], 1)
    latent_acts = jnp.where(core == 0, jnp.stack([kept, passed]), jnp.stack([passed, kept])).reshape(tok, lat)

    received = earlier_layers(acts, reach, group_size)
    received[-1] = after(received[-1], passed)
    out_type = jnp.bfloat16 if group_size == 1 else jnp.float32
    summed = decode_and_scatter([acts, *received], decoder[0], dec_sib, width, out_type)
    rebuilt = group_reduce(summed, group_size).astype(jnp.bfloat16)
    return (rebuilt[None], latent_acts[None])


def solution(mesh):
    return jax.shard_map(
        shards,
        mesh=mesh,
        in_specs=(
            P(None, None, "latent"),
            P("section", None, "latent"),
            P("section", "latent"),
            P("section", "latent"),
            P("section", None, "latent", None),
        ),
        out_specs=(P("section", None, "latent"), P("section", None, "latent")),
        check_vma=False,
    )
```

```python
import functools
import math

import jax
import jax.numpy as jnp
from jax import lax
from jax.experimental import pallas as pl
from jax.experimental.pallas import tpu as pltpu
from jax.sharding import PartitionSpec as P

LAYERS = 4
VMEM_LIMIT = 16 * 1024 * 1024


def swapped(shard, axis, stride):
    return lax.ppermute(shard, axis, [(i, i ^ 1 << stride) for i in range(lax.axis_size(axis))])


def after(value, *others):
    return lax.optimization_barrier((value, *others))[0]


def earlier_layers(value, reach, group_size):
    count = lax.axis_size("section")
    shifts = [hop * group_size for hop in range(1, reach)]
    return [lax.ppermute(value, "section", [(i, (i + shift) % count) for i in range(count)]) for shift in shifts]


def by_hop(acts, reach):
    layer = lax.axis_index("section") // (lax.axis_size("section") // LAYERS)
    for hop, values in enumerate(acts[:reach]):
        yield jnp.where(layer >= hop, values[...], jnp.zeros(values.shape, values.dtype)) if hop else values[...]


def group_reduce(partial_rows, group_size):
    current = partial_rows
    section_index = lax.axis_index("section")
    level_count = group_size.bit_length() - 1
    for level in reversed(range(level_count)):
        half = current.shape[0] // 2
        lower = current[:half]
        upper = current[half:]
        high_side = section_index // 2**level % 2 == 1
        kept = jnp.where(high_side, upper, lower)
        sent = jnp.where(high_side, lower, upper)
        received = swapped(sent.astype(jnp.bfloat16), "section", level).astype(sent.dtype)
        current = kept + received
    return current


def to_peer(value, offset):
    return lax.ppermute(value, "latent", [(i, i ^ offset) for i in range(lax.axis_size("latent"))])


def call(kernel, out_shape, cost=None):
    return pl.pallas_call(
        kernel,
        out_shape=out_shape,
        cost_estimate=cost,
        compiler_params=pltpu.CompilerParams(vmem_limit_bytes=VMEM_LIMIT),
    )


def encode_near_kernel(offsets, far_offsets, *refs):
    *x_refs, own_ref, sib_ref, gates_ref, gates_sib_ref, out_ref, thr_ref, far_ref = refs
    depth = x_refs[0].shape[1]
    place = lax.axis_index("latent")

    def weights(offset):
        rows = pl.ds(pl.multiple_of((place ^ offset) * depth, 16), depth)
        return jnp.concatenate([own_ref[rows, :], sib_ref[rows, :]], axis=1)

    bias, thr = (jnp.concatenate([gates_ref[i:i + 1, :], gates_sib_ref[i:i + 1, :]], axis=1) for i in (0, 1))
    total = jnp.broadcast_to(bias, out_ref.shape)
    for offset, x_ref in zip(offsets, x_refs):
        total += jnp.dot(x_ref[...], weights(offset), preferred_element_type=jnp.float32)
    out_ref[...] = total
    thr_ref[...] = thr
    for index, offset in enumerate(far_offsets):
        far_ref[index] = weights(offset)


def encode_near(pieces, far_offsets, own, sib, gates, gates_sib):
    rows, depth = next(iter(pieces.values())).shape
    lat = 2 * own.shape[1]
    shapes = (
        jax.ShapeDtypeStruct((rows, lat), jnp.float32),
        jax.ShapeDtypeStruct((1, lat), jnp.float32),
        jax.ShapeDtypeStruct((len(far_offsets), depth, lat), own.dtype),
    )
    cost = pl.CostEstimate(2 * len(pieces) * rows * depth * lat, 4 * own.size, 0)
    kernel = functools.partial(encode_near_kernel, tuple(pieces), far_offsets)
    return call(kernel, shapes, cost=cost)(*pieces.values(), own, sib, gates, gates_sib)


def encode_kernel(near_ref, thr_ref, weights_ref, *refs):
    *x_refs, acts_ref = refs
    preact = near_ref[...]
    for index, x_ref in enumerate(x_refs):
        preact += jnp.dot(x_ref[...], weights_ref[index], preferred_element_type=jnp.float32)
    acts_ref[...] = jnp.where(preact > thr_ref[...], preact, 0.0).astype(jnp.bfloat16)


def encode(near, thr, weights, pieces):
    return call(encode_kernel, jax.ShapeDtypeStruct(near.shape, jnp.bfloat16))(near, thr, weights, *pieces)


def decoded(acts, own_ref, sib_ref, columns):
    total = None
    for hop, values in enumerate(by_hop(acts, own_ref.shape[0])):
        weights = jnp.concatenate([own_ref[hop, :, columns], sib_ref[hop, :, columns]], axis=0)
        part = jnp.dot(values, weights, preferred_element_type=jnp.float32)
        total = part if total is None else total + part
    return total


def decode_chip_kernel(chip_offset, *refs):
    *acts, own_ref, sib_ref, same_ref, cross_ref = refs
    width = same_ref.shape[1]
    place = lax.axis_index("latent")
    columns = pl.ds(pl.multiple_of(((place // 2) ^ chip_offset) * (2 * width), 128), 2 * width)
    total = decoded(acts, own_ref, sib_ref, columns).astype(jnp.bfloat16)
    low, high = total[:, :width], total[:, width:]
    first_core = place % 2 == 0
    same_ref[...] = jnp.where(first_core, low, high)
    cross_ref[...] = jnp.where(first_core, high, low)


def decode_chip(chip_offset, acts, own, sib, width):
    shape = jax.ShapeDtypeStruct((acts[0].shape[0], width), jnp.bfloat16)
    return call(functools.partial(decode_chip_kernel, chip_offset), (shape, shape))(*acts, own, sib)


def decode_all_kernel(*refs):
    *acts, own_ref, sib_ref, out_ref = refs
    count, _, width = out_ref.shape
    block = math.lcm(width, 128)
    per_block = block // width
    for step in range(count // per_block):
        total = decoded(acts, own_ref, sib_ref, slice(step * block, (step + 1) * block))
        for piece in range(per_block):
            out_ref[step * per_block + piece] = total[:, piece * width:(piece + 1) * width].astype(jnp.bfloat16)


def sum_two_kernel(a_ref, b_ref, out_ref):
    out_ref[...] = (a_ref[...].astype(jnp.float32) + b_ref[...].astype(jnp.float32)).astype(jnp.bfloat16)


def sum_two(a, b):
    return call(sum_two_kernel, jax.ShapeDtypeStruct(a.shape, jnp.bfloat16))(a, b)


def finish_kernel(*refs):
    *parts, out_ref, sums, sems = refs
    half = len(parts) // 2
    rows = parts[0].shape[0]
    core = lax.axis_index("latent") % 2
    copies = []
    for index, (place, group) in enumerate(((core, parts[:half]), (1 - core, parts[half:]))):
        total = group[0][...].astype(jnp.float32)
        for part in group[1:]:
            total += part[...].astype(jnp.float32)
        sums[index] = total.astype(out_ref.dtype)
        target = out_ref.at[pl.ds(pl.multiple_of(place * rows, 16), rows), :]
        copies.append(pltpu.make_async_copy(sums.at[index], target, sems.at[index]))
        copies[-1].start()
    for copy in copies:
        copy.wait()


def finish(mine, other, dtype):
    rows, width = mine[0].shape
    return pl.pallas_call(
        finish_kernel,
        out_shape=jax.ShapeDtypeStruct((2 * rows, width), dtype),
        out_specs=pl.BlockSpec(memory_space=pl.ANY),
        scratch_shapes=[pltpu.VMEM((2, rows, width), dtype), pltpu.SemaphoreType.DMA((2,))],
        compiler_params=pltpu.CompilerParams(vmem_limit_bytes=VMEM_LIMIT),
    )(*mine, *other)


def gather_and_encode(mine, other, gates, encoder, decoder):
    count = lax.axis_size("latent")
    if count != 8:
        core = lax.axis_index("latent") % 2
        pair = jnp.where(core == 0, jnp.stack([mine, other]), jnp.stack([other, mine]))
        outgoing = jnp.broadcast_to(pair, (count // 2, *pair.shape)).reshape(count, *mine.shape)
        everyone = lax.all_to_all(outgoing, "latent", 0, 0, tiled=True)
        place = lax.axis_index("latent")
        pieces = {i: lax.dynamic_index_in_dim(everyone, place ^ i, 0, keepdims=False) for i in range(count)}
        near, far = {i: pieces[i] for i in range(count // 2)}, {i: pieces[i] for i in range(count // 2, count)}
        enc_sib, gates_sib, dec_sib = (to_peer(value, 1) for value in (encoder, gates, decoder))
        near_sum, *rest = encode_near(near, tuple(far), encoder, enc_sib, gates, gates_sib)
    else:
        near = {0: mine, 5: to_peer(other, 5), 4: to_peer(mine, 4), 3: to_peer(other, 3), 2: to_peer(mine, 2)}
        enc_sib = to_peer(encoder, 1)
        far = {7: to_peer(near[5], 2), 6: to_peer(near[2], 4)}
        near[1] = to_peer(after(other, enc_sib), 1)
        gates_sib = to_peer(after(gates, enc_sib), 1)
        near_sum, *rest = encode_near(near, tuple(far), encoder, enc_sib, gates, gates_sib)
        dec_sib = to_peer(after(decoder, far[6], far[7], near_sum), 1)
    return encode(near_sum, *rest, far.values()), dec_sib


def decode_and_scatter(acts, own, sib, width, dtype):
    count = lax.axis_size("latent")
    rows = acts[0].shape[0]
    if count != 8:
        shares = call(decode_all_kernel, jax.ShapeDtypeStruct((count, rows, width), jnp.bfloat16))(*acts, own, sib)
        received = lax.all_to_all(shares, "latent", 0, 0, tiled=True)
        return jnp.sum(received.reshape(count // 2, 2 * rows, width).astype(jnp.float32), axis=0).astype(dtype)
    diag_same, diag_cross = decode_chip(3, acts, own, sib, width)
    for_y, for_x = to_peer(diag_same, 2), to_peer(diag_cross, 4)
    x_same, x_cross = decode_chip(1, acts, own, sib, width)
    y_same, y_cross = decode_chip(2, acts, own, sib, width)
    from_x_same, from_y_cross = to_peer(x_same, 2), to_peer(y_cross, 5)
    own_same, own_cross = decode_chip(0, acts, own, sib, width)
    y_sum, x_sum = sum_two(y_same, for_y), sum_two(x_cross, for_x)
    from_y_same, from_x_cross = to_peer(y_sum, 4), to_peer(x_sum, 3)
    from_sib = to_peer(after(own_cross, for_x), 1)
    return finish((own_same, from_x_same, from_y_same), (from_sib, from_x_cross, from_y_cross), dtype)


def shards(residual, encoder, enc_bias, gate_code, decoder):
    group_size = lax.axis_size("section") // LAYERS
    core = lax.axis_index("latent") % 2
    _, tok, width = residual.shape
    lat = encoder.shape[2]
    reach = decoder.shape[1]

    halves = residual.reshape(residual.shape[0] * 2, tok // 2, width)
    place = 2 * (lax.axis_index("section") // group_size)
    mine, other = (lax.dynamic_index_in_dim(halves, place + half, 0, keepdims=False) for half in (core, 1 - core))
    threshold = 10000.0 * (gate_code[0].astype(jnp.float32) - 1.0)
    gates_own = jnp.stack([enc_bias[0], threshold])
    acts, dec_sib = gather_and_encode(mine, other, gates_own, encoder[0], decoder[0])
    kept, passed = acts[:, :lat], to_peer(acts[:, lat:], 1)
    latent_acts = jnp.where(core == 0, jnp.stack([kept, passed]), jnp.stack([passed, kept])).reshape(tok, lat)

    received = earlier_layers(acts, reach, group_size)
    received[-1] = after(received[-1], passed)
    out_type = jnp.bfloat16 if group_size == 1 else jnp.float32
    summed = decode_and_scatter([acts, *received], decoder[0], dec_sib, width, out_type)
    rebuilt = group_reduce(summed, group_size).astype(jnp.bfloat16)
    return (rebuilt[None], latent_acts[None])


def solution(mesh):
    return jax.shard_map(
        shards,
        mesh=mesh,
        in_specs=(
            P(None, None, "latent"),
            P("section", None, "latent"),
            P("section", "latent"),
            P("section", "latent"),
            P("section", None, "latent", None),
        ),
        out_specs=(P("section", None, "latent"), P("section", None, "latent")),
        check_vma=False,
    )
```

```python
import functools
import math

import jax
import jax.numpy as jnp
from jax import lax
from jax.experimental import pallas as pl
from jax.experimental.pallas import tpu as pltpu
from jax.sharding import PartitionSpec as P

LAYERS = 4
VMEM_LIMIT = 16 * 1024 * 1024


def swapped(shard, axis, stride):
    return lax.ppermute(shard, axis, [(i, i ^ 1 << stride) for i in range(lax.axis_size(axis))])


def after(value, *others):
    return lax.optimization_barrier((value, *others))[0]


def earlier_layers(value, reach, group_size):
    count = lax.axis_size("section")
    shifts = [hop * group_size for hop in range(1, reach)]
    return [lax.ppermute(value, "section", [(i, (i + shift) % count) for i in range(count)]) for shift in shifts]


def by_hop(acts, reach):
    layer = lax.axis_index("section") // (lax.axis_size("section") // LAYERS)
    for hop, values in enumerate(acts[:reach]):
        yield jnp.where(layer >= hop, values[...], jnp.zeros(values.shape, values.dtype)) if hop else values[...]


def group_reduce(partial_rows, group_size):
    current = partial_rows
    section_index = lax.axis_index("section")
    level_count = group_size.bit_length() - 1
    for level in reversed(range(level_count)):
        half = current.shape[0] // 2
        lower = current[:half]
        upper = current[half:]
        high_side = section_index // 2**level % 2 == 1
        kept = jnp.where(high_side, upper, lower)
        sent = jnp.where(high_side, lower, upper)
        received = swapped(sent.astype(jnp.bfloat16), "section", level).astype(sent.dtype)
        current = kept + received
    return current


def to_peer(value, offset):
    return lax.ppermute(value, "latent", [(i, i ^ offset) for i in range(lax.axis_size("latent"))])


def call(kernel, out_shape, cost=None):
    return pl.pallas_call(
        kernel,
        out_shape=out_shape,
        cost_estimate=cost,
        compiler_params=pltpu.CompilerParams(vmem_limit_bytes=VMEM_LIMIT),
    )


def encode_near_kernel(offsets, far_offsets, *refs):
    *x_refs, own_ref, sib_ref, gates_ref, gates_sib_ref, out_ref, thr_ref, far_ref = refs
    depth = x_refs[0].shape[1]
    place = lax.axis_index("latent")

    def weights(offset):
        rows = pl.ds(pl.multiple_of((place ^ offset) * depth, 16), depth)
        return jnp.concatenate([own_ref[rows, :], sib_ref[rows, :]], axis=1)

    bias, thr = (jnp.concatenate([gates_ref[i:i + 1, :], gates_sib_ref[i:i + 1, :]], axis=1) for i in (0, 1))
    total = jnp.broadcast_to(bias, out_ref.shape)
    for offset, x_ref in zip(offsets, x_refs):
        total += jnp.dot(x_ref[...], weights(offset), preferred_element_type=jnp.float32)
    out_ref[...] = total
    thr_ref[...] = thr
    for index, offset in enumerate(far_offsets):
        far_ref[index] = weights(offset)


def encode_near(pieces, far_offsets, own, sib, gates, gates_sib):
    rows, depth = next(iter(pieces.values())).shape
    lat = 2 * own.shape[1]
    shapes = (
        jax.ShapeDtypeStruct((rows, lat), jnp.float32),
        jax.ShapeDtypeStruct((1, lat), jnp.float32),
        jax.ShapeDtypeStruct((len(far_offsets), depth, lat), own.dtype),
    )
    cost = pl.CostEstimate(2 * len(pieces) * rows * depth * lat, 4 * own.size, 0)
    kernel = functools.partial(encode_near_kernel, tuple(pieces), far_offsets)
    return call(kernel, shapes, cost=cost)(*pieces.values(), own, sib, gates, gates_sib)


def encode_kernel(near_ref, thr_ref, weights_ref, *refs):
    *x_refs, acts_ref = refs
    preact = near_ref[...]
    for index, x_ref in enumerate(x_refs):
        preact += jnp.dot(x_ref[...], weights_ref[index], preferred_element_type=jnp.float32)
    acts_ref[...] = jnp.where(preact > thr_ref[...], preact, 0.0).astype(jnp.bfloat16)


def encode(near, thr, weights, pieces):
    return call(encode_kernel, jax.ShapeDtypeStruct(near.shape, jnp.bfloat16))(near, thr, weights, *pieces)


def decoded(acts, own_ref, sib_ref, columns):
    total = None
    for hop, values in enumerate(by_hop(acts, own_ref.shape[0])):
        weights = jnp.concatenate([own_ref[hop, :, columns], sib_ref[hop, :, columns]], axis=0)
        part = jnp.dot(values, weights, preferred_element_type=jnp.float32)
        total = part if total is None else total + part
    return total


def decode_chip_kernel(chip_offset, *refs):
    *acts, own_ref, sib_ref, same_ref, cross_ref = refs
    width = same_ref.shape[1]
    place = lax.axis_index("latent")
    columns = pl.ds(pl.multiple_of(((place // 2) ^ chip_offset) * (2 * width), 128), 2 * width)
    total = decoded(acts, own_ref, sib_ref, columns).astype(jnp.bfloat16)
    low, high = total[:, :width], total[:, width:]

    @pl.when(place % 2 == 0)
    def _():
        same_ref[...] = low
        cross_ref[...] = high

    @pl.when(place % 2 == 1)
    def _():
        same_ref[...] = high
        cross_ref[...] = low


def decode_chip(chip_offset, acts, own, sib, width):
    shape = jax.ShapeDtypeStruct((acts[0].shape[0], width), jnp.bfloat16)
    return call(functools.partial(decode_chip_kernel, chip_offset), (shape, shape))(*acts, own, sib)


def decode_all_kernel(*refs):
    *acts, own_ref, sib_ref, out_ref = refs
    count, _, width = out_ref.shape
    block = math.lcm(width, 128)
    per_block = block // width
    for step in range(count // per_block):
        total = decoded(acts, own_ref, sib_ref, slice(step * block, (step + 1) * block))
        for piece in range(per_block):
            out_ref[step * per_block + piece] = total[:, piece * width:(piece + 1) * width].astype(jnp.bfloat16)


def sum_two_kernel(a_ref, b_ref, out_ref):
    out_ref[...] = (a_ref[...].astype(jnp.float32) + b_ref[...].astype(jnp.float32)).astype(jnp.bfloat16)


def sum_two(a, b):
    return call(sum_two_kernel, jax.ShapeDtypeStruct(a.shape, jnp.bfloat16))(a, b)


def finish_kernel(*refs):
    *parts, out_ref, sums, sems = refs
    half = len(parts) // 2
    rows = parts[0].shape[0]
    core = lax.axis_index("latent") % 2
    copies = []
    for index, (place, group) in enumerate(((core, parts[:half]), (1 - core, parts[half:]))):
        total = group[0][...].astype(jnp.float32)
        for part in group[1:]:
            total += part[...].astype(jnp.float32)
        sums[index] = total.astype(out_ref.dtype)
        target = out_ref.at[pl.ds(pl.multiple_of(place * rows, 16), rows), :]
        copies.append(pltpu.make_async_copy(sums.at[index], target, sems.at[index]))
        copies[-1].start()
    for copy in copies:
        copy.wait()


def finish(mine, other, dtype):
    rows, width = mine[0].shape
    return pl.pallas_call(
        finish_kernel,
        out_shape=jax.ShapeDtypeStruct((2 * rows, width), dtype),
        out_specs=pl.BlockSpec(memory_space=pl.ANY),
        scratch_shapes=[pltpu.VMEM((2, rows, width), dtype), pltpu.SemaphoreType.DMA((2,))],
        compiler_params=pltpu.CompilerParams(vmem_limit_bytes=VMEM_LIMIT),
    )(*mine, *other)


def gather_and_encode(mine, other, gates, encoder, decoder):
    count = lax.axis_size("latent")
    if count != 8:
        core = lax.axis_index("latent") % 2
        pair = jnp.where(core == 0, jnp.stack([mine, other]), jnp.stack([other, mine]))
        outgoing = jnp.broadcast_to(pair, (count // 2, *pair.shape)).reshape(count, *mine.shape)
        everyone = lax.all_to_all(outgoing, "latent", 0, 0, tiled=True)
        place = lax.axis_index("latent")
        pieces = {i: lax.dynamic_index_in_dim(everyone, place ^ i, 0, keepdims=False) for i in range(count)}
        near, far = {i: pieces[i] for i in range(count // 2)}, {i: pieces[i] for i in range(count // 2, count)}
        enc_sib, gates_sib, dec_sib = (to_peer(value, 1) for value in (encoder, gates, decoder))
        near_sum, *rest = encode_near(near, tuple(far), encoder, enc_sib, gates, gates_sib)
    else:
        near = {0: mine, 5: to_peer(other, 5), 4: to_peer(mine, 4), 3: to_peer(other, 3), 2: to_peer(mine, 2)}
        enc_sib = to_peer(encoder, 1)
        far = {7: to_peer(near[5], 2), 6: to_peer(near[2], 4)}
        near[1] = to_peer(after(other, enc_sib), 1)
        gates_sib = to_peer(after(gates, enc_sib), 1)
        near_sum, *rest = encode_near(near, tuple(far), encoder, enc_sib, gates, gates_sib)
        dec_sib = to_peer(after(decoder, far[6], far[7], near_sum), 1)
    return encode(near_sum, *rest, far.values()), dec_sib


def decode_and_scatter(acts, own, sib, width, dtype):
    count = lax.axis_size("latent")
    rows = acts[0].shape[0]
    if count != 8:
        shares = call(decode_all_kernel, jax.ShapeDtypeStruct((count, rows, width), jnp.bfloat16))(*acts, own, sib)
        received = lax.all_to_all(shares, "latent", 0, 0, tiled=True)
        return jnp.sum(received.reshape(count // 2, 2 * rows, width).astype(jnp.float32), axis=0).astype(dtype)
    diag_same, diag_cross = decode_chip(3, acts, own, sib, width)
    for_y, for_x = to_peer(diag_same, 2), to_peer(diag_cross, 4)
    x_same, x_cross = decode_chip(1, acts, own, sib, width)
    y_same, y_cross = decode_chip(2, acts, own, sib, width)
    from_x_same, from_y_cross = to_peer(x_same, 2), to_peer(y_cross, 5)
    own_same, own_cross = decode_chip(0, acts, own, sib, width)
    y_sum, x_sum = sum_two(y_same, for_y), sum_two(x_cross, for_x)
    from_y_same, from_x_cross = to_peer(y_sum, 4), to_peer(x_sum, 3)
    from_sib = to_peer(own_cross, 1)
    return finish((own_same, from_x_same, from_y_same), (from_sib, from_x_cross, from_y_cross), dtype)


def shards(residual, encoder, enc_bias, gate_code, decoder):
    group_size = lax.axis_size("section") // LAYERS
    core = lax.axis_index("latent") % 2
    _, tok, width = residual.shape
    lat = encoder.shape[2]
    reach = decoder.shape[1]

    halves = residual.reshape(residual.shape[0] * 2, tok // 2, width)
    place = 2 * (lax.axis_index("section") // group_size)
    mine, other = (lax.dynamic_index_in_dim(halves, place + half, 0, keepdims=False) for half in (core, 1 - core))
    threshold = 10000.0 * (gate_code[0].astype(jnp.float32) - 1.0)
    gates_own = jnp.stack([enc_bias[0], threshold])
    acts, dec_sib = gather_and_encode(mine, other, gates_own, encoder[0], decoder[0])
    kept, passed = acts[:, :lat], to_peer(acts[:, lat:], 1)
    latent_acts = jnp.where(core == 0, jnp.stack([kept, passed]), jnp.stack([passed, kept])).reshape(tok, lat)

    received = earlier_layers(acts, reach, group_size)
    received[-1] = after(received[-1], passed)
    out_type = jnp.bfloat16 if group_size == 1 else jnp.float32
    summed = decode_and_scatter([acts, *received], decoder[0], dec_sib, width, out_type)
    rebuilt = group_reduce(summed, group_size).astype(jnp.bfloat16)
    return (rebuilt[None], latent_acts[None])


def solution(mesh):
    return jax.shard_map(
        shards,
        mesh=mesh,
        in_specs=(
            P(None, None, "latent"),
            P("section", None, "latent"),
            P("section", "latent"),
            P("section", "latent"),
            P("section", None, "latent", None),
        ),
        out_specs=(P("section", None, "latent"), P("section", None, "latent")),
        check_vma=False,
    )
```
